256 devices in a mesh: dp: 8 (over x, core), owner: 32 (over z, y).
Axes of the slice: x: 4, y: 4, z: 8, core: 2. Of those that a mesh axis runs over, the one named last changes fastest.
Arguments:
- grads: bfloat16 [8, 224, 512, 512], P('dp', 'owner'), may hold values from -1.5 to 1.5
- plan: int32 [224], replicated, may hold values from 0 to 31, as said below
- left_stat: float32 [32, 13, 512, 512], P('owner', None, 'dp'), as said below
- right_stat: float32 [32, 13, 512, 512], P('owner', None, 'dp'), as said below
- left_root: bfloat16 [32, 13, 512, 512], P('owner', None, 'dp'), as said below
- right_root: bfloat16 [32, 13, 512, 512], P('owner', None, 'dp'), as said below
Outputs:
- left_new: float32 [32, 13, 512, 512], P('owner', None, 'dp')
- right_new: float32 [32, 13, 512, 512], P('owner', None, 'dp')
- update: float32 [224, 512, 512], P('owner', 'dp')
The draws below stay inside these ranges and needn't reach their ends.
Inputs may be any that keep to these rules, and one draw needn't show every extreme that they name: `plan`: the 7 blocks i * 7 to i * 7 + 6 go to 7 different owners. Every owner receives between 1 and 13 blocks, and some owner receives exactly 13. `left_stat`: each slot's matrix is symmetric. `right_stat`: each slot's matrix is symmetric. `left_root`: each slot's matrix is symmetric. `right_root`: each slot's matrix is symmetric.
All inputs are finite; a program needn't handle non-finite values.
Results may differ from the reference program's by a relative error of at most 0.0003.
Values may be sent and summed in bfloat16 or wider, within the bound.
A program may use at most 128 MiB of HBM per device.

```python
import math
import jax
import jax.numpy as jnp
from jax import lax

B = 512
BPO = 7
NBLK = 224
OWN_CAP = 13
N_DP = 8
N_OWNER = 32


def symmetric_field(key, noise_draw, lowest, highest, spread):
    field_shape = noise_draw.shape
    row_index = lax.broadcasted_iota(jnp.int32, field_shape, 2)
    col_index = lax.broadcasted_iota(jnp.int32, field_shape, 3)
    diagonal = jax.random.uniform(key, field_shape[:3], jnp.float32, lowest, highest)
    symmetric = (noise_draw + jnp.swapaxes(noise_draw, 2, 3)) * (spread / math.sqrt(2.0))
    return jnp.where(row_index == col_index, diagonal[..., None], symmetric)


def draw_plan(key, part):
    key = jax.random.fold_in(key, 7)
    pair_key, extra_key, sender_key, place_key = jax.random.split(key, 4)
    shuffled = jax.random.permutation(pair_key, N_OWNER).astype(jnp.int32)
    margin = OWN_CAP - BPO
    extra = jax.random.randint(extra_key, (N_OWNER // 2,), 0, margin + 1).astype(jnp.int32)
    extra = extra.at[0].set(margin)
    loads = jnp.zeros((N_OWNER,), jnp.int32)
    loads = loads.at[shuffled[0::2]].set(BPO + extra).at[shuffled[1::2]].set(BPO - extra)
    bounds = jnp.cumsum(loads).astype(jnp.int32)
    token = jnp.arange(NBLK, dtype=jnp.int32)
    owner_of = jnp.sum((bounds[None, :] <= token[:, None]).astype(jnp.int32), axis=1).astype(jnp.int32)
    relabel = jax.random.permutation(sender_key, N_OWNER).astype(jnp.int32)
    sender = relabel[token % N_OWNER]
    position = token // N_OWNER
    scores = jax.random.randint(place_key, (N_OWNER, BPO), 0, 1 << 20).astype(jnp.int32) * BPO + jnp.arange(BPO, dtype=jnp.int32)[None, :]
    shuffle_rows = jnp.argsort(scores, axis=1).astype(jnp.int32)
    slot_in = shuffle_rows[sender, position]
    return jnp.zeros((NBLK,), jnp.int32).at[sender * BPO + slot_in].set(owner_of)


def stat_noise(key):
    field_shape = (N_OWNER, OWN_CAP, B, B)
    return jax.random.normal(key, field_shape, jnp.float32)


def draw_left_stat(key, part):
    key = jax.random.fold_in(key, 11)
    noise_key, diag_key = jax.random.split(key)
    return symmetric_field(diag_key, stat_noise(noise_key), 1.0, 3.0, 0.2)


def draw_right_stat(key, part):
    key = jax.random.fold_in(key, 13)
    noise_key, diag_key = jax.random.split(key)
    return symmetric_field(diag_key, stat_noise(noise_key), 1.0, 3.0, 0.2)


def draw_left_root(key, part):
    key = jax.random.fold_in(key, 17)
    noise_key, diag_key = jax.random.split(key)
    field = symmetric_field(diag_key, stat_noise(noise_key), 1.0, 2.0, 0.25 / math.sqrt(B))
    return field.astype(jnp.bfloat16)


def draw_right_root(key, part):
    key = jax.random.fold_in(key, 19)
    noise_key, diag_key = jax.random.split(key)
    field = symmetric_field(diag_key, stat_noise(noise_key), 1.0, 2.0, 0.25 / math.sqrt(B))
    return field.astype(jnp.bfloat16)


def shard_levels(rng, dims, cuts, smallest, top_value):
    factor_of = 1.0
    for dim, blocks in cuts:
        heights = jax.random.uniform(jax.random.fold_in(jax.random.fold_in(rng, 6), dim), (blocks,), jnp.float32, smallest / len(cuts), top_value / len(cuts))
        factor_of = factor_of * jnp.repeat(jnp.exp(heights), dims[dim] // blocks).reshape((-1,) + (1,) * (len(dims) - 1 - dim))
    return factor_of


def noise(stream_key, extent, width, bound, pieces=(), held_as=jnp.bfloat16):
    drawn = width * jax.random.normal(stream_key, extent, jnp.float32)
    if pieces:
        drawn = drawn * shard_levels(stream_key, extent, pieces, -0.22, 0.18)
    return jnp.clip(drawn, -bound, bound).astype(held_as)


def setup_inputs(seed: int = 0) -> dict:
    streams_of = jax.random.split(jax.random.key(seed), 7)
    return {
        "grads": noise(streams_of[0], (N_DP, NBLK, B, B), 0.1, 1.5, ((0, 8), (1, 32))),
        "plan": draw_plan(jax.random.fold_in(streams_of[6], 71), 0),
        "left_stat": draw_left_stat(jax.random.fold_in(streams_of[6], 71), 0),
        "right_stat": draw_right_stat(jax.random.fold_in(streams_of[6], 71), 0),
        "left_root": draw_left_root(jax.random.fold_in(streams_of[6], 71), 0),
        "right_root": draw_right_root(jax.random.fold_in(streams_of[6], 71), 0),
    }


def reference(grads, plan, left_stat, right_stat, left_root, right_root):
    highest = lax.Precision.HIGHEST
    summed = grads[0].astype(jnp.float32)
    for replica in range(1, N_DP):
        summed = summed + grads[replica].astype(jnp.float32)
    block_ids = jnp.arange(NBLK, dtype=jnp.int32)
    earlier = (plan[None, :] == plan[:, None]) & (block_ids[None, :] < block_ids[:, None])
    slot_rank = jnp.sum(earlier.astype(jnp.int32), axis=1).astype(jnp.int32)

    def per_block(block_id):
        gradient = summed[block_id]
        owner_now = plan[block_id]
        slot_now = slot_rank[block_id]
        left_factor = left_root[owner_now, slot_now].astype(jnp.float32)
        right_factor = right_root[owner_now, slot_now].astype(jnp.float32)
        left_term = jnp.dot(gradient, gradient.T, precision=highest)
        right_term = jnp.dot(gradient.T, gradient, precision=highest)
        projected = jnp.dot(left_factor, gradient, precision=highest)
        update = jnp.dot(projected, right_factor, precision=highest)
        return left_term, right_term, update

    left_term, right_term, update = lax.map(per_block, block_ids)
    left_new = (0.95 * left_stat).at[plan, slot_rank].add(0.05 * left_term)
    right_new = (0.95 * right_stat).at[plan, slot_rank].add(0.05 * right_term)
    return left_new, right_new, update
```

```python
import functools

import jax
import jax.numpy as jnp
from jax import lax
from jax.experimental import pallas as pl
from jax.experimental.pallas import tpu as pltpu
from jax.sharding import PartitionSpec as P

MESH = pl.DeviceIdType.MESH
f32 = jnp.float32
bf16 = jnp.bfloat16
i16 = jnp.int16
i32 = jnp.int32

stat_decay = 0.95
fresh_share = 0.05

NB = 7
NO = 32
NS = 13
ND = 8
SR = 64
BO = 512
CH = 128
SLOT = 272
UNIT = 912
CUT = 7
LIMIT = 60 * 1024 * 1024


def encode(x):
    m = jnp.maximum(jnp.max(jnp.abs(x), axis=0, keepdims=True), 2.0 ** -100)
    e = jnp.floor(jnp.log2(m) * 256.0) + 1.0
    q = jnp.round(x * (32700.0 * jnp.exp2(e * (-1.0 / 256.0))))
    return q.astype(i32).astype(i16), e


def scale_of(e16):
    return jnp.exp2(e16.astype(i32).astype(f32) * (1.0 / 256.0)) * (1.0 / 32700.0)


def widen(q):
    return q.astype(i32).astype(f32)


def remote(src, dst, send, recv, where):
    return pltpu.make_async_remote_copy(
        src_ref=src, dst_ref=dst, send_sem=send, recv_sem=recv,
        device_id=where, device_id_type=MESH)


def ring_places():
    dp = lax.axis_index("dp")
    x, c = dp // 2, dp % 2
    partner = x * 2 + 1 - c
    right = ((x + 1) % 4) * 2 + c
    left = ((x + 3) % 4) * 2 + c
    across = ((x + 2) % 4) * 2 + c
    return dp, x, c, partner, right, left, across


def greet(barrier, places):
    for place in places:
        pl.semaphore_signal(barrier, inc=1, device_id={"dp": place}, device_id_type=MESH)


def greet_owners(barrier, me):
    def one(k, _):
        pl.semaphore_signal(
            barrier, inc=1, device_id={"owner": (me + k) % NO}, device_id_type=MESH)
        return 0

    lax.fori_loop(1, NO, one, 0)


def sum_kernel(grads, g7, own, par, snd, rcv, psend, precv, lsem, usend, urecv):
    dp, x, c, partner, right, left, across = ring_places()
    barrier = pltpu.get_barrier_semaphore()
    greet(barrier, (partner, right, left))
    pl.semaphore_wait(barrier, 3)
    pair, mine = [], []
    for n, off in enumerate((2, 1, 3, 0)):
        xd = (x + off) % 4
        there = pl.ds(pl.multiple_of((xd * 2 + 1 - c) * SR, SR), SR)
        here = pl.ds(pl.multiple_of((xd * 2 + c) * SR, SR), SR)
        cp = remote(grads.at[:, there, :], par.at[n], psend.at[n], precv.at[n], {"dp": partner})
        cp.start()
        pair.append(cp)
        lc = pltpu.make_async_copy(grads.at[:, here, :], own.at[n], lsem.at[n])
        lc.start()
        mine.append(lc)

    row_id = lax.broadcasted_iota(i32, (16, CH), 0)

    def pair_sum(n, j, k):
        cols = slice(k * CH, k * CH + CH)
        return own[n, j, :, cols].astype(f32) + par[n, j, :, cols].astype(f32)

    def unit_rows(j, kk):
        return pl.ds(pl.multiple_of(j * 128 + kk * SR, SR), SR)

    def received(u, j, kk):
        scales = scale_of(rcv[u, 896:912, :])
        row = jnp.sum(jnp.where(row_id == j * 2 + kk, scales, 0.0), axis=0, keepdims=True)
        return widen(rcv[u, unit_rows(j, kk), :]) * row

    def fill(u, value):
        def block(j, sc):
            for kk in range(2):
                q, e = encode(value(j, kk))
                snd[u, unit_rows(j, kk), :] = q
                sc = jnp.where(row_id == j * 2 + kk, e, sc)
            return sc

        sc = lax.fori_loop(0, NB, block, jnp.zeros((16, CH), f32))
        snd[u, 896:912, :] = sc.astype(i32).astype(i16)

    def ship(u, place):
        cp = remote(snd.at[u], rcv.at[u], usend.at[u], urecv.at[u], {"dp": place})
        cp.start()
        return cp

    def ready(n):
        mine[n].wait()
        pair[n].wait_recv()

    ready(0)
    fill(0, lambda j, kk: pair_sum(0, j, kk))
    c0 = ship(0, right)
    fill(1, lambda j, kk: pair_sum(0, j, 2 + kk))
    c1 = ship(1, left)
    ready(1)
    fill(2, lambda j, kk: pair_sum(1, j, 2 + kk))
    c2 = ship(2, right)
    ready(2)
    fill(3, lambda j, kk: pair_sum(2, j, kk))
    c3 = ship(3, left)
    c0.wait_recv()
    fill(4, lambda j, kk: pair_sum(1, j, kk) + received(0, j, kk))
    c4 = ship(4, right)
    c1.wait_recv()
    fill(5, lambda j, kk: pair_sum(2, j, 2 + kk) + received(1, j, kk))
    c5 = ship(5, left)
    ready(3)
    c2.wait_recv()
    c3.wait_recv()
    c4.wait_recv()
    c5.wait_recv()

    def total(j, _):
        sc = jnp.zeros((16, CH), f32)
        for k in range(4):
            kk = k % 2
            one, two = ((4, 3), (2, 5))[k // 2]
            v = pair_sum(3, j, k) + received(one, j, kk) + received(two, j, kk)
            q, e = encode(v)
            g7[j, k * SR:k * SR + SR, :] = q
            sc = jnp.where(row_id == k, e, sc)
        g7[j, 256:272, :] = sc.astype(i32).astype(i16)
        return 0

    lax.fori_loop(0, NB, total, 0)
    for cp in (c0, c1, c2, c3, c4, c5):
        cp.wait_send()
    for cp in pair:
        cp.wait_send()


def sum_over_dp(grads):
    return pl.pallas_call(
        sum_kernel,
        out_shape=jax.ShapeDtypeStruct((NB, SLOT, CH), i16),
        in_specs=[pl.BlockSpec(memory_space=pl.ANY)],
        out_specs=pl.BlockSpec(memory_space=pltpu.VMEM),
        scratch_shapes=[
            pltpu.VMEM((4, NB, SR, BO), bf16),
            pltpu.VMEM((4, NB, SR, BO), bf16),
            pltpu.VMEM((6, UNIT, CH), i16),
            pltpu.VMEM((6, UNIT, CH), i16),
            pltpu.SemaphoreType.DMA((4,)),
            pltpu.SemaphoreType.DMA((4,)),
            pltpu.SemaphoreType.DMA((4,)),
            pltpu.SemaphoreType.DMA((6,)),
            pltpu.SemaphoreType.DMA((6,)),
        ],
        compiler_params=pltpu.CompilerParams(
            collective_id=0, has_side_effects=True, vmem_limit_bytes=LIMIT),
        name="sum_over_dp",
    )(grads)


class Gather:
    def __init__(self, src, full, send, recv):
        self.src, self.full, self.send, self.recv = src, full, send, recv
        self.sent = []

    def _go(self, n, src, dst, place):
        cp = remote(src, dst, self.send.at[n], self.recv.at[n], {"dp": place})
        cp.start()
        self.sent.append(cp)
        return cp

    def begin(self):
        dp, x, c, partner, right, left, across = ring_places()
        a, b = slice(0, CUT), slice(CUT, NS)
        full, src = self.full, self.src
        self.ra = self._go(0, src.at[a], full.at[dp, a], right)
        self.lb = self._go(1, src.at[b], full.at[dp, b], left)
        self.rb = self._go(2, src.at[b], full.at[dp, b], right)
        self.la = self._go(3, src.at[a], full.at[dp, a], left)
        self.own = self._go(4, src, full.at[dp], partner)

    def finish(self):
        dp, x, c, partner, right, left, across = ring_places()
        a, b = slice(0, CUT), slice(CUT, NS)
        full = self.full
        self.ra.wait_recv()
        fa = self._go(5, full.at[left, a], full.at[left, a], right)
        pa = self._go(6, full.at[left, a], full.at[left, a], partner)
        self.lb.wait_recv()
        fb = self._go(7, full.at[right, b], full.at[right, b], left)
        pb = self._go(8, full.at[right, b], full.at[right, b], partner)
        self.rb.wait_recv()
        pc = self._go(9, full.at[left, b], full.at[left, b], partner)
        self.la.wait_recv()
        pd = self._go(10, full.at[right, a], full.at[right, a], partner)
        fa.wait_recv()
        pe = self._go(11, full.at[across, a], full.at[across, a], partner)
        fb.wait_recv()
        pf = self._go(12, full.at[across, b], full.at[across, b], partner)
        for cp in (self.own, pa, pb, pc, pd, pe, pf):
            cp.wait_recv()

    def end(self):
        for cp in self.sent:
            cp.wait_send()


GATHER_SEMS = 13


def exchange_start(me, fetch, send, recv, ssem, rsem):
    def one(k, _):
        dest = (me + k) % NO
        send[k] = fetch(dest)
        remote(send.at[k], recv.at[me], ssem.at[k], rsem.at[k], {"owner": dest}).start()
        return 0

    lax.fori_loop(1, NO, one, 0)
    recv[me] = fetch(me)


def exchange_wait(me, send, recv, ssem, rsem):
    def one(k, _):
        came = (me + NO - k) % NO
        cp = remote(send.at[k], recv.at[came], ssem.at[k], rsem.at[k], {"owner": came})
        cp.wait_recv()
        cp.wait_send()
        return 0

    lax.fori_loop(1, NO, one, 0)


def out_kernel(block_of, source_of, g7, right_root, slots, rfull,
               send, recv, ssem, rsem, gsend, grecv, lsem):
    me = lax.axis_index("owner")
    dp, x, c, partner, right, left, across = ring_places()
    barrier = pltpu.get_barrier_semaphore()
    greet(barrier, (partner, right, left))
    greet_owners(barrier, me)
    pl.semaphore_wait(barrier, 3 + NO - 1)
    gather = Gather(right_root, rfull, gsend, grecv)
    gather.begin()
    local = pltpu.make_async_copy(right_root, rfull.at[dp], lsem)
    local.start()
    exchange_start(me, lambda dest: g7[block_of[dest]], send, recv, ssem, rsem)
    gather.finish()
    exchange_wait(me, send, recv, ssem, rsem)

    def pick(k, _):
        slots[k] = recv[source_of[k]]
        return 0

    lax.fori_loop(0, NS, pick, 0)
    gather.end()
    local.wait()


def to_owners(block_of, source_of, g7, right_root):
    return pl.pallas_call(
        out_kernel,
        out_shape=(
            jax.ShapeDtypeStruct((NS, SLOT, CH), i16),
            jax.ShapeDtypeStruct((ND, NS, SR, BO), bf16),
        ),
        in_specs=[
            pl.BlockSpec(memory_space=pltpu.SMEM),
            pl.BlockSpec(memory_space=pltpu.SMEM),
            pl.BlockSpec(memory_space=pltpu.VMEM),
            pl.BlockSpec(memory_space=pl.ANY),
        ],
        out_specs=(
            pl.BlockSpec(memory_space=pltpu.VMEM),
            pl.BlockSpec(memory_space=pl.ANY),
        ),
        scratch_shapes=[
            pltpu.VMEM((NO, SLOT, CH), i16),
            pltpu.VMEM((NO, SLOT, CH), i16),
            pltpu.SemaphoreType.DMA((NO,)),
            pltpu.SemaphoreType.DMA((NO,)),
            pltpu.SemaphoreType.DMA((GATHER_SEMS,)),
            pltpu.SemaphoreType.DMA((GATHER_SEMS,)),
            pltpu.SemaphoreType.DMA,
        ],
        compiler_params=pltpu.CompilerParams(
            collective_id=1, has_side_effects=True, vmem_limit_bytes=LIMIT),
        name="to_owners",
    )(block_of, source_of, g7, right_root)


def dot(a, b, dims=((1,), (0,))):
    return lax.dot_general(a, b, (dims, ((), ())), preferred_element_type=f32)


def split(v):
    hi = v.astype(bf16)
    return hi, (v - hi.astype(f32)).astype(bf16)


def back_kernel(slot_of, owner_of, weight, slots, rfull, left_root, left_stat, right_stat,
                left_new, right_new, update,
                codes, high, low, rv, lv, ls, rs, term, usl, send, recv,
                ssem, rsem, gsend, grecv, lsem, osem):
    me = lax.axis_index("owner")
    dp, x, c, partner, right, left, across = ring_places()
    loads = [
        pltpu.make_async_copy(slots, codes.at[dp], lsem.at[0]),
        pltpu.make_async_copy(left_root, lv, lsem.at[1]),
        pltpu.make_async_copy(rfull, rv, lsem.at[2]),
        pltpu.make_async_copy(left_stat, ls, lsem.at[3]),
        pltpu.make_async_copy(right_stat, rs, lsem.at[4]),
    ]
    for cp in loads:
        cp.start()
    barrier = pltpu.get_barrier_semaphore()
    greet(barrier, (partner, right, left))
    greet_owners(barrier, me)
    pl.semaphore_wait(barrier, 3 + NO - 1)
    gather = Gather(slots, codes, gsend, grecv)
    gather.begin()
    gather.finish()
    for cp in loads:
        cp.wait()

    row_id = lax.broadcasted_iota(i32, (16, CH), 0)

    def make_update(k, _):
        for t in range(ND):
            scales = scale_of(codes[t, k, 256:272, :])
            for n in range(4):
                v = widen(codes[t, k, n * SR:n * SR + SR, :]) * scales[n:n + 1, :]
                hi, lo = split(v)
                high[k, t * SR:t * SR + SR, n * CH:n * CH + CH] = hi
                low[k, t * SR:t * SR + SR, n * CH:n * CH + CH] = lo
        lrows = lv[k]
        projected = dot(lrows, high[k]) + dot(lrows, low[k])
        phi, plo = split(projected)
        both = dot(jnp.concatenate((phi, plo), axis=0), rv[:, k].reshape(BO, BO))
        u = both[:SR] + both[SR:]
        sc = jnp.zeros((16, CH), f32)
        for n in range(4):
            q, e = encode(u[:, n * CH:n * CH + CH])
            usl[k, n * SR:n * SR + SR, :] = q
            sc = jnp.where(row_id == n, e, sc)
        usl[k, 256:272, :] = sc.astype(i32).astype(i16)
        return 0

    lax.fori_loop(0, NS, make_update, 0)
    exchange_start(me, lambda dest: usl[slot_of[dest]], send, recv, ssem, rsem)

    rows = pl.ds(pl.multiple_of(dp * SR, SR), SR)
    lanes = pl.ds(pl.multiple_of(x * CH, CH), CH)
    side = pl.ds(pl.multiple_of(c * SR, SR), SR)

    def make_stats(k, _):
        w = weight[k]
        hi, lo = high[k], low[k]
        ohi, olo = high[k, rows, :], low[k, rows, :]
        facing = dot(jnp.concatenate((ohi, olo), axis=0), hi, ((1,), (1,)))
        facing = facing[:SR] + facing[SR:] + dot(ohi, lo, ((1,), (1,)))
        ls[k] = stat_decay * ls[k] + w * facing
        chi, clo = high[k, :, lanes], low[k, :, lanes]
        term[...] = (dot(chi, hi, ((0,), (0,))) + dot(clo, hi, ((0,), (0,)))
                     + dot(chi, lo, ((0,), (0,))))
        rs[k] = stat_decay * rs[k] + w * term[side, :]
        pltpu.make_async_copy(ls.at[k], left_new.at[k], osem.at[0, k]).start()
        pltpu.make_async_copy(rs.at[k], right_new.at[k], osem.at[1, k]).start()
        return 0

    lax.fori_loop(0, NS, make_stats, 0)
    exchange_wait(me, send, recv, ssem, rsem)

    def take(j, _):
        code = recv[owner_of[j]]
        scales = scale_of(code[256:272, :])
        for n in range(4):
            update[j, :, n * CH:n * CH + CH] = (
                widen(code[n * SR:n * SR + SR, :]) * scales[n:n + 1, :])
        return 0

    lax.fori_loop(0, NB, take, 0)

    def done(k, _):
        pltpu.make_async_copy(ls.at[k], left_new.at[k], osem.at[0, k]).wait()
        pltpu.make_async_copy(rs.at[k], right_new.at[k], osem.at[1, k]).wait()
        return 0

    lax.fori_loop(0, NS, done, 0)
    gather.end()


def back(slot_of, owner_of, weight, slots, rfull, left_root, left_stat, right_stat):
    smem = pl.BlockSpec(memory_space=pltpu.SMEM)
    hbm = pl.BlockSpec(memory_space=pl.ANY)
    return pl.pallas_call(
        back_kernel,
        out_shape=(
            jax.ShapeDtypeStruct((NS, SR, BO), f32),
            jax.ShapeDtypeStruct((NS, SR, BO), f32),
            jax.ShapeDtypeStruct((NB, SR, BO), f32),
        ),
        in_specs=[smem, smem, smem, hbm, hbm, hbm, hbm, hbm],
        out_specs=(hbm, hbm, pl.BlockSpec(memory_space=pltpu.VMEM)),
        scratch_shapes=[
            pltpu.VMEM((ND, NS, SLOT, CH), i16),
            pltpu.VMEM((NS, BO, BO), bf16),
            pltpu.VMEM((NS, BO, BO), bf16),
            pltpu.VMEM((ND, NS, SR, BO), bf16),
            pltpu.VMEM((NS, SR, BO), bf16),
            pltpu.VMEM((NS, SR, BO), f32),
            pltpu.VMEM((NS, SR, BO), f32),
            pltpu.VMEM((CH, BO), f32),
            pltpu.VMEM((NS, SLOT, CH), i16),
            pltpu.VMEM((NO, SLOT, CH), i16),
            pltpu.VMEM((NO, SLOT, CH), i16),
            pltpu.SemaphoreType.DMA((NO,)),
            pltpu.SemaphoreType.DMA((NO,)),
            pltpu.SemaphoreType.DMA((GATHER_SEMS,)),
            pltpu.SemaphoreType.DMA((GATHER_SEMS,)),
            pltpu.SemaphoreType.DMA((5,)),
            pltpu.SemaphoreType.DMA((2, NS)),
        ],
        compiler_params=pltpu.CompilerParams(
            collective_id=2, has_side_effects=True, vmem_limit_bytes=LIMIT),
        name="back",
    )(slot_of, owner_of, weight, slots, rfull, left_root, left_stat, right_stat)


def tables(plan):
    me = lax.axis_index("owner")
    table = plan.reshape(NO, NB)
    owner_of = lax.dynamic_index_in_dim(table, me, 0, keepdims=False)
    owners = jnp.arange(NO, dtype=i32)
    hit = (owners[:, None] == owner_of[None, :]).astype(i32)
    block_of = jnp.sum(hit * jnp.arange(NB, dtype=i32)[None, :], axis=1)
    holding = jnp.sum((table == me).astype(i32), axis=1)
    standing = jnp.cumsum(holding) - 1
    slot_of = jnp.clip(standing, 0, NS - 1)
    slot_ids = jnp.arange(NS, dtype=i32)
    match = ((slot_ids[:, None] == standing[None, :]) & (holding[None, :] > 0)).astype(i32)
    source_of = jnp.sum(match * owners[None, :], axis=1)
    weight = fresh_share * jnp.sum(match, axis=1).astype(f32)
    return owner_of, block_of, slot_of, source_of, weight


def local(grads, plan, left_stat, right_stat, left_root, right_root):
    owner_of, block_of, slot_of, source_of, weight = tables(plan)
    g7 = sum_over_dp(grads[0])
    slots, rfull = to_owners(block_of, source_of, g7, right_root[0])
    left_new, right_new, update = back(
        slot_of, owner_of, weight, slots, rfull, left_root[0], left_stat[0], right_stat[0])
    return left_new[None], right_new[None], update


def solution(mesh):
    return jax.shard_map(
        local,
        mesh=mesh,
        in_specs=(
            P("dp", "owner", None, None),
            P(),
            P("owner", None, "dp", None),
            P("owner", None, "dp", None),
            P("owner", None, "dp", None),
            P("owner", None, "dp", None),
        ),
        out_specs=(
            P("owner", None, "dp", None),
            P("owner", None, "dp", None),
            P("owner", "dp", None),
        ),
        check_vma=False,
    )
```

```python
import functools

import jax
import jax.numpy as jnp
from jax import lax
from jax.experimental import pallas as pl
from jax.experimental.pallas import tpu as pltpu
from jax.sharding import PartitionSpec as P

MESH = pl.DeviceIdType.MESH
f32 = jnp.float32
bf16 = jnp.bfloat16
i16 = jnp.int16
i32 = jnp.int32

stat_decay = 0.95
fresh_share = 0.05

NB = 7
NO = 32
NS = 13
ND = 8
SR = 64
BO = 512
CH = 128
SLOT = 272
UNIT = 912
CUT = 7
LIMIT = 60 * 1024 * 1024


def encode(x):
    m = jnp.maximum(jnp.max(jnp.abs(x), axis=0, keepdims=True), 2.0 ** -100)
    e = jnp.floor(jnp.log2(m) * 256.0) + 1.0
    q = jnp.round(x * (32700.0 * jnp.exp2(e * (-1.0 / 256.0))))
    return q.astype(i32).astype(i16), e


def scale_of(e16):
    return jnp.exp2(e16.astype(i32).astype(f32) * (1.0 / 256.0)) * (1.0 / 32700.0)


def widen(q):
    return q.astype(i32).astype(f32)


def remote(src, dst, send, recv, where):
    return pltpu.make_async_remote_copy(
        src_ref=src, dst_ref=dst, send_sem=send, recv_sem=recv,
        device_id=where, device_id_type=MESH)


def ring_places():
    dp = lax.axis_index("dp")
    x, c = dp // 2, dp % 2
    partner = x * 2 + 1 - c
    right = ((x + 1) % 4) * 2 + c
    left = ((x + 3) % 4) * 2 + c
    across = ((x + 2) % 4) * 2 + c
    return dp, x, c, partner, right, left, across


def greet(barrier, places):
    for place in places:
        pl.semaphore_signal(barrier, inc=1, device_id={"dp": place}, device_id_type=MESH)


def sum_kernel(grads, g7, own, par, snd, rcv, psend, precv, lsem, usend, urecv):
    dp, x, c, partner, right, left, across = ring_places()
    barrier = pltpu.get_barrier_semaphore()
    greet(barrier, (partner, right, left))
    pl.semaphore_wait(barrier, 3)
    pair, mine = [], []
    for n, off in enumerate((2, 1, 3, 0)):
        xd = (x + off) % 4
        there = pl.ds(pl.multiple_of((xd * 2 + 1 - c) * SR, SR), SR)
        here = pl.ds(pl.multiple_of((xd * 2 + c) * SR, SR), SR)
        cp = remote(grads.at[:, there, :], par.at[n], psend.at[n], precv.at[n], {"dp": partner})
        cp.start()
        pair.append(cp)
        lc = pltpu.make_async_copy(grads.at[:, here, :], own.at[n], lsem.at[n])
        lc.start()
        mine.append(lc)

    row_id = lax.broadcasted_iota(i32, (16, CH), 0)

    def pair_sum(n, j, k):
        cols = slice(k * CH, k * CH + CH)
        return own[n, j, :, cols].astype(f32) + par[n, j, :, cols].astype(f32)

    def unit_rows(j, kk):
        return pl.ds(pl.multiple_of(j * 128 + kk * SR, SR), SR)

    def received(u, j, kk):
        scales = scale_of(rcv[u, 896:912, :])
        row = jnp.sum(jnp.where(row_id == j * 2 + kk, scales, 0.0), axis=0, keepdims=True)
        return widen(rcv[u, unit_rows(j, kk), :]) * row

    def fill(u, value):
        def block(j, sc):
            for kk in range(2):
                q, e = encode(value(j, kk))
                snd[u, unit_rows(j, kk), :] = q
                sc = jnp.where(row_id == j * 2 + kk, e, sc)
            return sc

        sc = lax.fori_loop(0, NB, block, jnp.zeros((16, CH), f32))
        snd[u, 896:912, :] = sc.astype(i32).astype(i16)

    def ship(u, place):
        cp = remote(snd.at[u], rcv.at[u], usend.at[u], urecv.at[u], {"dp": place})
        cp.start()
        return cp

    def ready(n):
        mine[n].wait()
        pair[n].wait_recv()

    ready(0)
    fill(0, lambda j, kk: pair_sum(0, j, kk))
    c0 = ship(0, right)
    fill(1, lambda j, kk: pair_sum(0, j, 2 + kk))
    c1 = ship(1, left)
    ready(1)
    fill(2, lambda j, kk: pair_sum(1, j, 2 + kk))
    c2 = ship(2, right)
    ready(2)
    fill(3, lambda j, kk: pair_sum(2, j, kk))
    c3 = ship(3, left)
    c0.wait_recv()
    fill(4, lambda j, kk: pair_sum(1, j, kk) + received(0, j, kk))
    c4 = ship(4, right)
    c1.wait_recv()
    fill(5, lambda j, kk: pair_sum(2, j, 2 + kk) + received(1, j, kk))
    c5 = ship(5, left)
    ready(3)
    c2.wait_recv()
    c3.wait_recv()
    c4.wait_recv()
    c5.wait_recv()

    def total(j, _):
        sc = jnp.zeros((16, CH), f32)
        for k in range(4):
            kk = k % 2
            one, two = ((4, 3), (2, 5))[k // 2]
            v = pair_sum(3, j, k) + received(one, j, kk) + received(two, j, kk)
            q, e = encode(v)
            g7[j, k * SR:k * SR + SR, :] = q
            sc = jnp.where(row_id == k, e, sc)
        g7[j, 256:272, :] = sc.astype(i32).astype(i16)
        return 0

    lax.fori_loop(0, NB, total, 0)
    for cp in (c0, c1, c2, c3, c4, c5):
        cp.wait_send()
    for cp in pair:
        cp.wait_send()


def sum_over_dp(grads):
    return pl.pallas_call(
        sum_kernel,
        out_shape=jax.ShapeDtypeStruct((NB, SLOT, CH), i16),
        in_specs=[pl.BlockSpec(memory_space=pl.ANY)],
        out_specs=pl.BlockSpec(memory_space=pltpu.VMEM),
        scratch_shapes=[
            pltpu.VMEM((4, NB, SR, BO), bf16),
            pltpu.VMEM((4, NB, SR, BO), bf16),
            pltpu.VMEM((6, UNIT, CH), i16),
            pltpu.VMEM((6, UNIT, CH), i16),
            pltpu.SemaphoreType.DMA((4,)),
            pltpu.SemaphoreType.DMA((4,)),
            pltpu.SemaphoreType.DMA((4,)),
            pltpu.SemaphoreType.DMA((6,)),
            pltpu.SemaphoreType.DMA((6,)),
        ],
        compiler_params=pltpu.CompilerParams(
            collective_id=0, has_side_effects=True, vmem_limit_bytes=LIMIT),
        name="sum_over_dp",
    )(grads)


class Gather:
    def __init__(self, src, full, send, recv):
        self.src, self.full, self.send, self.recv = src, full, send, recv
        self.sent = []

    def _go(self, n, src, dst, place):
        cp = remote(src, dst, self.send.at[n], self.recv.at[n], {"dp": place})
        cp.start()
        self.sent.append(cp)
        return cp

    def begin(self):
        dp, x, c, partner, right, left, across = ring_places()
        a, b = slice(0, CUT), slice(CUT, NS)
        full, src = self.full, self.src
        self.ra = self._go(0, src.at[a], full.at[dp, a], right)
        self.lb = self._go(1, src.at[b], full.at[dp, b], left)
        self.rb = self._go(2, src.at[b], full.at[dp, b], right)
        self.la = self._go(3, src.at[a], full.at[dp, a], left)
        self.own = self._go(4, src, full.at[dp], partner)

    def stage(self, r):
        dp, x, c, partner, right, left, across = ring_places()
        a, b = slice(0, CUT), slice(CUT, NS)
        full = self.full
        if r == 0:
            self.ra.wait_recv()
            self.fa = self._go(5, full.at[left, a], full.at[left, a], right)
            pa = self._go(6, full.at[left, a], full.at[left, a], partner)
            self.lb.wait_recv()
            self.fb = self._go(7, full.at[right, b], full.at[right, b], left)
            pb = self._go(8, full.at[right, b], full.at[right, b], partner)
            self.given = [self.own, pa, pb]
        elif r == 1:
            self.rb.wait_recv()
            self.given.append(self._go(9, full.at[left, b], full.at[left, b], partner))
            self.la.wait_recv()
            self.given.append(self._go(10, full.at[right, a], full.at[right, a], partner))
        elif r == 2:
            self.fa.wait_recv()
            self.given.append(self._go(11, full.at[across, a], full.at[across, a], partner))
            self.fb.wait_recv()
            self.given.append(self._go(12, full.at[across, b], full.at[across, b], partner))
        else:
            for cp in self.given:
                cp.wait_recv()

    def finish(self):
        for r in range(4):
            self.stage(r)

    def end(self):
        for cp in self.sent:
            cp.wait_send()


GATHER_SEMS = 13


NY = 4
NZ = 8
FRONT = slice(0, 4)
REAR = slice(4, NB)


def plane():
    me = lax.axis_index("owner")
    z, y = me // NY, me % NY
    return me, z, y, ((z + 1) % NZ) * NY + y, ((z + NZ - 1) % NZ) * NY + y


def greet_plane(barrier):
    me, z, y, up, down = plane()
    places = [up, down] + [z * NY + (y + t) % NY for t in range(1, NY)]
    for place in places:
        pl.semaphore_signal(barrier, inc=1, device_id={"owner": place}, device_id_type=MESH)


PEERS = 3 + 2 + NY - 1


class Line:
    def __init__(self, send, recv, towards):
        self.send, self.recv, self.towards = send, recv, towards
        self.copies = {}

    def go(self, n, src, dst):
        cp = remote(src, dst, self.send.at[n], self.recv.at[n], {"owner": self.towards})
        cp.start()
        self.copies[n] = cp

    def came(self, *names):
        for n in names:
            self.copies[n].wait_recv()

    def end(self):
        for cp in self.copies.values():
            cp.wait_send()


def out_kernel(pick, source_of, g7, right_root, slots, rfull,
               u1, u2, u3, d1, d2, d3, far, ysend, recv,
               usem, ursem, dsem, drsem, ysem, yrsem, gsend, grecv, lsem):
    me, z, y, up, down = plane()
    dp, x, c, partner, right, left, across = ring_places()
    barrier = pltpu.get_barrier_semaphore()
    greet(barrier, (partner, right, left))
    greet_plane(barrier)
    pl.semaphore_wait(barrier, PEERS)
    ups, downs = Line(usem, ursem, up), Line(dsem, drsem, down)
    ups.go(0, g7.at[FRONT], u1.at[FRONT])
    downs.go(0, g7.at[REAR], d1.at[REAR])
    ups.go(1, g7.at[REAR], u1.at[REAR])
    downs.go(1, g7.at[FRONT], d1.at[FRONT])
    gather = Gather(right_root, rfull, gsend, grecv)
    gather.begin()
    local = pltpu.make_async_copy(right_root, rfull.at[dp], lsem)
    local.start()
    hand = []

    def pass_on(n, ref, rel):
        s = (z + rel) % NZ
        for t in range(1, NY):
            yy = (y + t) % NY
            ysend[n, t - 1] = ref[pick[s * NY + yy]]
            cp = remote(ysend.at[n, t - 1], recv.at[s * NY + y], ysem.at[n, t - 1],
                        yrsem.at[n, t - 1], {"owner": z * NY + yy})
            cp.start()
            hand.append(cp)
        recv[s * NY + y] = ref[pick[s * NY + y]]

    pass_on(0, g7, 0)
    steps = ((u1, u2, d1, d2, 7, 1), (u2, u3, d2, d3, 6, 2))
    for r, (ua, ub, da, db, below, above) in enumerate(steps):
        ups.came(2 * r)
        ups.go(2 * r + 2, ua.at[FRONT], ub.at[FRONT])
        downs.came(2 * r)
        downs.go(2 * r + 2, da.at[REAR], db.at[REAR])
        ups.came(2 * r + 1)
        ups.go(2 * r + 3, ua.at[REAR], ub.at[REAR])
        downs.came(2 * r + 1)
        downs.go(2 * r + 3, da.at[FRONT], db.at[FRONT])
        pass_on(2 * r + 1, ua, below)
        pass_on(2 * r + 2, da, above)
        gather.stage(r)
    ups.came(4)
    ups.go(6, u3.at[FRONT], far.at[FRONT])
    downs.came(4)
    downs.go(6, d3.at[REAR], far.at[REAR])
    ups.came(5)
    downs.came(5)
    pass_on(5, u3, 5)
    pass_on(6, d3, 3)
    gather.stage(2)
    ups.came(6)
    downs.came(6)
    pass_on(7, far, 4)
    gather.stage(3)
    for cp in hand:
        cp.wait_recv()

    def take(k, _):
        slots[k] = recv[source_of[k]]
        return 0

    lax.fori_loop(0, NS, take, 0)
    for cp in hand:
        cp.wait_send()
    ups.end()
    downs.end()
    gather.end()
    local.wait()


def to_owners(pick, source_of, g7, right_root):
    coded = pltpu.VMEM((NB, SLOT, CH), i16)
    return pl.pallas_call(
        out_kernel,
        out_shape=(
            jax.ShapeDtypeStruct((NS, SLOT, CH), i16),
            jax.ShapeDtypeStruct((ND, NS, SR, BO), bf16),
        ),
        in_specs=[
            pl.BlockSpec(memory_space=pltpu.SMEM),
            pl.BlockSpec(memory_space=pltpu.SMEM),
            pl.BlockSpec(memory_space=pltpu.VMEM),
            pl.BlockSpec(memory_space=pl.ANY),
        ],
        out_specs=(
            pl.BlockSpec(memory_space=pltpu.VMEM),
            pl.BlockSpec(memory_space=pl.ANY),
        ),
        scratch_shapes=[
            coded, coded, coded, coded, coded, coded, coded,
            pltpu.VMEM((NZ, NY - 1, SLOT, CH), i16),
            pltpu.VMEM((NO, SLOT, CH), i16),
            pltpu.SemaphoreType.DMA((7,)),
            pltpu.SemaphoreType.DMA((7,)),
            pltpu.SemaphoreType.DMA((7,)),
            pltpu.SemaphoreType.DMA((7,)),
            pltpu.SemaphoreType.DMA((NZ, NY - 1)),
            pltpu.SemaphoreType.DMA((NZ, NY - 1)),
            pltpu.SemaphoreType.DMA((GATHER_SEMS,)),
            pltpu.SemaphoreType.DMA((GATHER_SEMS,)),
            pltpu.SemaphoreType.DMA,
        ],
        compiler_params=pltpu.CompilerParams(
            collective_id=1, has_side_effects=True, vmem_limit_bytes=LIMIT),
        name="to_owners",
    )(pick, source_of, g7, right_root)


def dot(a, b, dims=((1,), (0,))):
    return lax.dot_general(a, b, (dims, ((), ())), preferred_element_type=f32)


def split(v):
    hi = v.astype(bf16)
    return hi, (v - hi.astype(f32)).astype(bf16)


def back_kernel(slot_of, mine, column, above, weight, slots, rfull, left_root, left_stat,
                right_stat, left_new, right_new, update,
                codes, high, low, rv, lv, ls, rs, term, usl,
                y0, y1, y2, y3, y4, y5, y6, y7, ysend,
                ur0, ur1, ur2, ur3, dr0, dr1, dr2, dr3, ush, dsh,
                usem, ursem, dsem, drsem, ysem, yrsem, gsend, grecv, lsem, osem):
    me, z, y, up, down = plane()
    dp, x, c, partner, right, left, across = ring_places()
    loads = [
        pltpu.make_async_copy(slots, codes.at[dp], lsem.at[0]),
        pltpu.make_async_copy(left_root, lv, lsem.at[1]),
        pltpu.make_async_copy(rfull, rv, lsem.at[2]),
        pltpu.make_async_copy(left_stat, ls, lsem.at[3]),
        pltpu.make_async_copy(right_stat, rs, lsem.at[4]),
    ]
    for cp in loads:
        cp.start()
    barrier = pltpu.get_barrier_semaphore()
    greet(barrier, (partner, right, left))
    greet_plane(barrier)
    pl.semaphore_wait(barrier, PEERS)
    gather = Gather(slots, codes, gsend, grecv)
    gather.begin()
    gather.finish()
    for cp in loads:
        cp.wait()

    row_id = lax.broadcasted_iota(i32, (16, CH), 0)

    def make_update(k, _):
        for t in range(ND):
            scales = scale_of(codes[t, k, 256:272, :])
            for n in range(4):
                v = widen(codes[t, k, n * SR:n * SR + SR, :]) * scales[n:n + 1, :]
                hi, lo = split(v)
                high[k, t * SR:t * SR + SR, n * CH:n * CH + CH] = hi
                low[k, t * SR:t * SR + SR, n * CH:n * CH + CH] = lo
        lrows = lv[k]
        projected = dot(lrows, high[k]) + dot(lrows, low[k])
        phi, plo = split(projected)
        both = dot(jnp.concatenate((phi, plo), axis=0), rv[:, k].reshape(BO, BO))
        u = both[:SR] + both[SR:]
        sc = jnp.zeros((16, CH), f32)
        for n in range(4):
            q, e = encode(u[:, n * CH:n * CH + CH])
            usl[k, n * SR:n * SR + SR, :] = q
            sc = jnp.where(row_id == n, e, sc)
        usl[k, 256:272, :] = sc.astype(i32).astype(i16)
        return 0

    lax.fori_loop(0, NS, make_update, 0)

    rows = pl.ds(pl.multiple_of(dp * SR, SR), SR)
    lanes = pl.ds(pl.multiple_of(x * CH, CH), CH)
    side = pl.ds(pl.multiple_of(c * SR, SR), SR)

    def make_stats(k, _):
        w = weight[k]
        hi, lo = high[k], low[k]
        ohi, olo = high[k, rows, :], low[k, rows, :]
        facing = dot(jnp.concatenate((ohi, olo), axis=0), hi, ((1,), (1,)))
        facing = facing[:SR] + facing[SR:] + dot(ohi, lo, ((1,), (1,)))
        ls[k] = stat_decay * ls[k] + w * facing
        chi, clo = high[k, :, lanes], low[k, :, lanes]
        term[...] = (dot(chi, hi, ((0,), (0,))) + dot(clo, hi, ((0,), (0,)))
                     + dot(chi, lo, ((0,), (0,))))
        rs[k] = stat_decay * rs[k] + w * term[side, :]
        pltpu.make_async_copy(ls.at[k], left_new.at[k], osem.at[0, k]).start()
        pltpu.make_async_copy(rs.at[k], right_new.at[k], osem.at[1, k]).start()
        return 0

    def stats(first, last):
        lax.fori_loop(first, last, make_stats, 0)

    ys = (y0, y1, y2, y3, y4, y5, y6, y7)
    hand = {}

    def across_y(n):
        d = (z + n) % NZ
        hand[n] = []
        for t in range(1, NY):
            yy = (y + t) % NY
            ysend[n, t - 1] = usl[slot_of[d * NY + yy]]
            cp = remote(ysend.at[n, t - 1], ys[n].at[y], ysem.at[n, t - 1],
                        yrsem.at[n, t - 1], {"owner": z * NY + yy})
            cp.start()
            hand[n].append(cp)
        ys[n][y] = usl[slot_of[d * NY + y]]

    def across_done(n):
        for cp in hand[n]:
            cp.wait_recv()

    ups, downs = Line(usem, ursem, up), Line(dsem, drsem, down)

    def train(n, out, blocks, came):
        d = (z + n) % NZ

        def one(j, _):
            here = ys[n][column[d * NB + j]]
            if came is not None:
                here = jnp.where(jnp.full((SLOT, CH), mine[d * NB + j], i32) > 0, here, came[j])
            out[j] = here
            return 0

        lax.fori_loop(blocks.start, blocks.stop, one, 0)

    across_y(4)
    across_y(3)
    across_y(5)
    across_done(4)
    train(4, ush.at[3], FRONT, None)
    ups.go(0, ush.at[3, FRONT], ur3.at[FRONT])
    train(4, dsh.at[3], REAR, None)
    downs.go(0, dsh.at[3, REAR], dr3.at[REAR])
    across_done(3)
    train(3, ush.at[2], REAR, None)
    ups.go(1, ush.at[2, REAR], ur2.at[REAR])
    across_done(5)
    train(5, dsh.at[2], FRONT, None)
    downs.go(1, dsh.at[2, FRONT], dr2.at[FRONT])
    across_y(2)
    across_y(6)
    stats(0, 3)
    ups.came(0)
    train(3, ush.at[2], FRONT, ur3)
    ups.go(2, ush.at[2, FRONT], ur2.at[FRONT])
    downs.came(0)
    train(5, dsh.at[2], REAR, dr3)
    downs.go(2, dsh.at[2, REAR], dr2.at[REAR])
    across_y(1)
    across_y(7)
    across_done(2)
    across_done(6)
    ups.came(1)
    train(2, ush.at[1], REAR, ur2)
    ups.go(3, ush.at[1, REAR], ur1.at[REAR])
    downs.came(1)
    train(6, dsh.at[1], FRONT, dr2)
    downs.go(3, dsh.at[1, FRONT], dr1.at[FRONT])
    stats(3, 6)
    ups.came(2)
    train(2, ush.at[1], FRONT, ur2)
    ups.go(4, ush.at[1, FRONT], ur1.at[FRONT])
    downs.came(2)
    train(6, dsh.at[1], REAR, dr2)
    downs.go(4, dsh.at[1, REAR], dr1.at[REAR])
    across_y(0)
    across_done(1)
    across_done(7)
    ups.came(3)
    train(1, ush.at[0], REAR, ur1)
    ups.go(5, ush.at[0, REAR], ur0.at[REAR])
    downs.came(3)
    train(7, dsh.at[0], FRONT, dr1)
    downs.go(5, dsh.at[0, FRONT], dr0.at[FRONT])
    stats(6, 9)
    ups.came(4)
    train(1, ush.at[0], FRONT, ur1)
    ups.go(6, ush.at[0, FRONT], ur0.at[FRONT])
    downs.came(4)
    train(7, dsh.at[0], REAR, dr1)
    downs.go(6, dsh.at[0, REAR], dr0.at[REAR])
    stats(9, NS)
    across_done(0)
    ups.came(5, 6)
    downs.came(5, 6)

    def take(j, _):
        shape = jnp.zeros((SLOT, CH), i32)
        code = jnp.where(shape + above[j] > 0, dr0[j], ur0[j])
        code = jnp.where(shape + mine[z * NB + j] > 0, y0[column[z * NB + j]], code)
        scales = scale_of(code[256:272, :])
        for n in range(4):
            update[j, :, n * CH:n * CH + CH] = (
                widen(code[n * SR:n * SR + SR, :]) * scales[n:n + 1, :])
        return 0

    lax.fori_loop(0, NB, take, 0)

    def done(k, _):
        pltpu.make_async_copy(ls.at[k], left_new.at[k], osem.at[0, k]).wait()
        pltpu.make_async_copy(rs.at[k], right_new.at[k], osem.at[1, k]).wait()
        return 0

    lax.fori_loop(0, NS, done, 0)
    for n in range(NZ):
        for cp in hand[n]:
            cp.wait_send()
    ups.end()
    downs.end()
    gather.end()


def back(slot_of, mine, column, above, weight, slots, rfull, left_root, left_stat, right_stat):
    coded = pltpu.VMEM((NB, SLOT, CH), i16)
    column_of = pltpu.VMEM((NY, SLOT, CH), i16)
    smem = pl.BlockSpec(memory_space=pltpu.SMEM)
    hbm = pl.BlockSpec(memory_space=pl.ANY)
    return pl.pallas_call(
        back_kernel,
        out_shape=(
            jax.ShapeDtypeStruct((NS, SR, BO), f32),
            jax.ShapeDtypeStruct((NS, SR, BO), f32),
            jax.ShapeDtypeStruct((NB, SR, BO), f32),
        ),
        in_specs=[smem, smem, smem, smem, smem, hbm, hbm, hbm, hbm, hbm],
        out_specs=(hbm, hbm, pl.BlockSpec(memory_space=pltpu.VMEM)),
        scratch_shapes=[
            pltpu.VMEM((ND, NS, SLOT, CH), i16),
            pltpu.VMEM((NS, BO, BO), bf16),
            pltpu.VMEM((NS, BO, BO), bf16),
            pltpu.VMEM((ND, NS, SR, BO), bf16),
            pltpu.VMEM((NS, SR, BO), bf16),
            pltpu.VMEM((NS, SR, BO), f32),
            pltpu.VMEM((NS, SR, BO), f32),
            pltpu.VMEM((CH, BO), f32),
            pltpu.VMEM((NS, SLOT, CH), i16),
            column_of, column_of, column_of, column_of,
            column_of, column_of, column_of, column_of,
            pltpu.VMEM((NZ, NY - 1, SLOT, CH), i16),
            coded, coded, coded, coded, coded, coded, coded, coded,
            pltpu.VMEM((4, NB, SLOT, CH), i16),
            pltpu.VMEM((4, NB, SLOT, CH), i16),
            pltpu.SemaphoreType.DMA((7,)),
            pltpu.SemaphoreType.DMA((7,)),
            pltpu.SemaphoreType.DMA((7,)),
            pltpu.SemaphoreType.DMA((7,)),
            pltpu.SemaphoreType.DMA((NZ, NY - 1)),
            pltpu.SemaphoreType.DMA((NZ, NY - 1)),
            pltpu.SemaphoreType.DMA((GATHER_SEMS,)),
            pltpu.SemaphoreType.DMA((GATHER_SEMS,)),
            pltpu.SemaphoreType.DMA((5,)),
            pltpu.SemaphoreType.DMA((2, NS)),
        ],
        compiler_params=pltpu.CompilerParams(
            collective_id=2, has_side_effects=True, vmem_limit_bytes=LIMIT),
        name="back",
    )(slot_of, mine, column, above, weight, slots, rfull, left_root, left_stat, right_stat)


def tables(plan):
    me = lax.axis_index("owner")
    z, y = me // NY, me % NY
    table = plan.reshape(NO, NB)
    owners = jnp.arange(NO, dtype=i32)
    blocks = jnp.arange(NB, dtype=i32)
    lane = lax.dynamic_index_in_dim(plan.reshape(NZ, NY, NB), y, 1, keepdims=False)
    to_plane = z * NY + jnp.arange(NY, dtype=i32)
    hit = (lane[:, None, :] == to_plane[None, :, None]).astype(i32)
    pick = jnp.sum(hit * blocks[None, None, :], axis=2).reshape(-1)
    mine = (lane // NY == z).astype(i32)
    column = lane % NY
    off = (lax.dynamic_index_in_dim(lane, z, 0, keepdims=False) // NY - z) % NZ
    above = ((off < 4) | ((off == 4) & (blocks >= 4))).astype(i32)
    holding = jnp.sum((table == me).astype(i32), axis=1)
    standing = jnp.cumsum(holding) - 1
    slot_of = jnp.clip(standing, 0, NS - 1)
    slot_ids = jnp.arange(NS, dtype=i32)
    match = ((slot_ids[:, None] == standing[None, :]) & (holding[None, :] > 0)).astype(i32)
    source_of = jnp.sum(match * owners[None, :], axis=1)
    weight = fresh_share * jnp.sum(match, axis=1).astype(f32)
    return pick, mine.reshape(-1), column.reshape(-1), above, slot_of, source_of, weight


def local(grads, plan, left_stat, right_stat, left_root, right_root):
    pick, mine, column, above, slot_of, source_of, weight = tables(plan)
    g7 = sum_over_dp(grads[0])
    slots, rfull = to_owners(pick, source_of, g7, right_root[0])
    left_new, right_new, update = back(
        slot_of, mine, column, above, weight,
        slots, rfull, left_root[0], left_stat[0], right_stat[0])
    return left_new[None], right_new[None], update


def solution(mesh):
    return jax.shard_map(
        local,
        mesh=mesh,
        in_specs=(
            P("dp", "owner", None, None),
            P(),
            P("owner", None, "dp", None),
            P("owner", None, "dp", None),
            P("owner", None, "dp", None),
            P("owner", None, "dp", None),
        ),
        out_specs=(
            P("owner", None, "dp", None),
            P("owner", None, "dp", None),
            P("owner", "dp", None),
        ),
        check_vma=False,
    )
```

```python
import functools

import jax
import jax.numpy as jnp
from jax import lax
from jax.experimental import pallas as pl
from jax.experimental.pallas import tpu as pltpu
from jax.sharding import PartitionSpec as P

MESH = pl.DeviceIdType.MESH
f32 = jnp.float32
bf16 = jnp.bfloat16
i16 = jnp.int16
i32 = jnp.int32

stat_decay = 0.95
fresh_share = 0.05

NB = 7
NO = 32
NS = 13
ND = 8
SR = 64
BO = 512
CH = 128
NY = 4
NZ = 8
HALF = 144
SLOT = 272
UNIT = 912
FRONT = slice(0, 512)
REAR = slice(512, UNIT)
BACK = slice(512, 896)
SCALES = slice(896, UNIT)
LIMIT = 60 * 1024 * 1024


def encode(x):
    m = jnp.maximum(jnp.max(jnp.abs(x), axis=0, keepdims=True), 2.0 ** -100)
    e = jnp.floor(jnp.log2(m) * 256.0) + 1.0
    q = jnp.round(x * (32700.0 * jnp.exp2(e * (-1.0 / 256.0))))
    return q.astype(i32).astype(i16), e


def scale_of(e16):
    return jnp.exp2(e16.astype(i32).astype(f32) * (1.0 / 256.0)) * (1.0 / 32700.0)


def widen(q):
    return q.astype(i32).astype(f32)


def remote(src, dst, send, recv, where):
    return pltpu.make_async_remote_copy(
        src_ref=src, dst_ref=dst, send_sem=send, recv_sem=recv,
        device_id=where, device_id_type=MESH)


def dot(a, b, dims=((1,), (0,))):
    return lax.dot_general(a, b, (dims, ((), ())), preferred_element_type=f32)


def split(v):
    hi = v.astype(bf16)
    return hi, (v - hi.astype(f32)).astype(bf16)


def rows_of(t, n=SR):
    return pl.ds(pl.multiple_of(t * n, n), n)


def shampoo_kernel(plan, grads, left_stat, right_stat, left_root, right_root,
                   left_new, right_new, update, *scratch):
    it = iter(scratch)
    slot_of, source_of, block_at, weight = (next(it) for _ in range(4))
    own, par, snd, rcv = (next(it) for _ in range(4))
    unit = [next(it) for _ in range(2)]
    hops = [[next(it) for _ in range(7)] for _ in range(2)]
    ysend, got, xs, gx = ([next(it) for _ in range(2)] for _ in range(4))
    lf, rf, ghi, glo, phi, plo = (next(it) for _ in range(6))
    xu, ux = ([next(it) for _ in range(2)] for _ in range(2))
    ybuf = [[next(it) for _ in range(8)] for _ in range(2)]
    yback = [next(it) for _ in range(2)]
    ur = [[next(it) for _ in range(4)] for _ in range(2)]
    dr = [[next(it) for _ in range(4)] for _ in range(2)]
    ush = [next(it) for _ in range(2)]
    dsh = [next(it) for _ in range(2)]
    sx, sr = ([next(it) for _ in range(2)] for _ in range(2))
    ls, rs, shelf = next(it), next(it), next(it)
    pair_sem, load_sem, unit_sem, line_sem, y_sem, x_sem, out_sem = (next(it) for _ in range(7))

    me = lax.axis_index("owner")
    z, y = me // NY, me % NY
    up, down = ((z + 1) % NZ) * NY + y, ((z + NZ - 1) % NZ) * NY + y
    dp = lax.axis_index("dp")
    x, c = dp // 2, dp % 2
    partner = x * 2 + 1 - c
    right = ((x + 1) % 4) * 2 + c
    left = ((x + 3) % 4) * 2 + c
    row_id = lax.broadcasted_iota(i32, (16, CH), 0)
    sent = []

    mine = {}
    for n, off in ((0, 2), (2, 3), (1, 1), (3, 0)):
        t = ((x + off) % 4) * 2 + c
        mine[n] = pltpu.make_async_copy(grads.at[:, rows_of(t), :], own.at[n], load_sem.at[n])
        mine[n].start()
    stat_in = [pltpu.make_async_copy(left_stat, ls, load_sem.at[4]),
               pltpu.make_async_copy(right_stat, rs, load_sem.at[5])]
    root_in = []
    for i in range(2):
        k = (dp + 8 * i) % NS
        root_in.append(pltpu.make_async_copy(
            left_root.at[k], lf.at[i, rows_of(dp)], load_sem.at[6 + i]))
        root_in.append(pltpu.make_async_copy(
            right_root.at[k], rf.at[i, rows_of(dp)], load_sem.at[8 + i]))

    barrier = pltpu.get_barrier_semaphore()
    for t in range(1, ND):
        pl.semaphore_signal(
            barrier, inc=1, device_id={"dp": (dp + t) % ND}, device_id_type=MESH)
    for place in [up, down] + [z * NY + (y + t) % NY for t in range(1, NY)]:
        pl.semaphore_signal(barrier, inc=1, device_id={"owner": place}, device_id_type=MESH)
    pl.semaphore_wait(barrier, ND - 1 + 2 + NY - 1)

    pair = {}
    for n, off in ((0, 2), (2, 3), (1, 1), (3, 0)):
        t = ((x + off) % 4) * 2 + 1 - c
        pair[n] = remote(grads.at[:, rows_of(t), :], par.at[n],
                         pair_sem.at[0, n], pair_sem.at[1, n], {"dp": partner})
        pair[n].start()
        sent.append(pair[n])
    for cp in root_in + stat_in:
        cp.start()

    def stand(i, count):
        hold, which = jnp.int32(0), jnp.int32(0)
        for j in range(NB):
            hit = (plan[i * NB + j] == me).astype(i32)
            hold = hold + hit * (1 - hold)
            which = which + hit * (j - which)
        slot_of[i] = count * (count < NS).astype(i32)
        source_of[NS + i] = hold * (count + 1) - 1
        block_at[NS + i] = which
        return count + hold

    count = lax.fori_loop(0, NO, stand, jnp.int32(0))

    def place(k, _):
        def look(i, found):
            hit = (source_of[NS + i] == k).astype(i32)
            return found[0] + hit * (i - found[0]), found[1] + hit * (block_at[NS + i] - found[1])

        src, blk = lax.fori_loop(0, NO, look, (jnp.int32(0), jnp.int32(0)))
        source_of[k] = src
        block_at[k] = blk
        weight[k] = fresh_share * (k < count).astype(i32).astype(f32)
        return 0

    lax.fori_loop(0, NS, place, 0)

    def pair_sum(n, j, k):
        cols = slice(k * CH, k * CH + CH)
        return own[n, j, :, cols].astype(f32) + par[n, j, :, cols].astype(f32)

    def unit_rows(j, kk):
        return pl.ds(pl.multiple_of(j * 128 + kk * SR, SR), SR)

    def scale_row(scales, r):
        return jnp.sum(jnp.where(row_id == r, scales, 0.0), axis=0, keepdims=True)

    def received(u, j, kk):
        row = scale_row(scale_of(rcv[u, 896:912, :]), j * 2 + kk)
        return widen(rcv[u, unit_rows(j, kk), :]) * row

    def fill(out, value):
        def block(j, sc):
            for kk in range(2):
                q, e = encode(value(j, kk))
                out[unit_rows(j, kk), :] = q
                sc = jnp.where(row_id == j * 2 + kk, e, sc)
            return sc

        sc = lax.fori_loop(0, NB, block, jnp.zeros((16, CH), f32))
        out[896:912, :] = sc.astype(i32).astype(i16)

    def ship(u, to):
        cp = remote(snd.at[u], rcv.at[u], unit_sem.at[0, u], unit_sem.at[1, u], {"dp": to})
        cp.start()
        sent.append(cp)
        return cp

    def ready(n):
        mine[n].wait()
        pair[n].wait_recv()

    class Line:
        def __init__(self, h, way, towards):
            self.h, self.way, self.towards = h, way, towards
            self.copies = {}

        def go(self, n, src, dst):
            cp = remote(src, dst, line_sem.at[self.h, self.way, 0, n],
                        line_sem.at[self.h, self.way, 1, n], {"owner": self.towards})
            cp.start()
            sent.append(cp)
            self.copies[n] = cp

        def came(self, *names):
            for n in names:
                self.copies[n].wait_recv()

    class Outward:
        def __init__(self, h):
            self.h = h
            self.u1, self.u2, self.u3, self.d1, self.d2, self.d3, self.far = hops[h]
            self.ups, self.downs = Line(h, 0, up), Line(h, 1, down)
            self.hand, self.given = [], []

        def pass_on(self, n, ref, rel):
            h = self.h
            s = (z + rel) % NZ
            src = s * NY + y

            def code(yy):
                j = jnp.int32(0)
                for b in range(NB):
                    j = j + (plan[src * NB + b] == z * NY + yy).astype(i32) * (b - j)
                return shelf[j]

            for b in range(NB):
                shelf[b] = ref[b * 128:b * 128 + 128, :]
            scales = ref[896:912, :]
            for t in range(1, NY):
                yy = (y + t) % NY
                ysend[h][n, t - 1, 0:128, :] = code(yy)
                ysend[h][n, t - 1, 128:HALF, :] = scales
                cp = remote(ysend[h].at[n, t - 1], got[h].at[src], y_sem.at[h, 0, n, t - 1],
                            y_sem.at[h, 1, n, t - 1], {"owner": z * NY + yy})
                cp.start()
                sent.append(cp)
                self.hand.append(cp)
            got[h][src, 0:128, :] = code(y)
            got[h][src, 128:HALF, :] = scales

        def start(self):
            g = unit[self.h]
            self.ups.go(0, g.at[FRONT], self.u1.at[FRONT])
            self.downs.go(0, g.at[REAR], self.d1.at[REAR])
            self.ups.go(1, g.at[REAR], self.u1.at[REAR])
            self.downs.go(1, g.at[FRONT], self.d1.at[FRONT])
            self.pass_on(0, g, 0)

        def step(self, r):
            ups, downs = self.ups, self.downs
            if r < 3:
                ua, ub = ((self.u1, self.u2), (self.u2, self.u3))[r - 1]
                da, db = ((self.d1, self.d2), (self.d2, self.d3))[r - 1]
                ups.came(2 * r - 2)
                ups.go(2 * r, ua.at[FRONT], ub.at[FRONT])
                downs.came(2 * r - 2)
                downs.go(2 * r, da.at[REAR], db.at[REAR])
                ups.came(2 * r - 1)
                ups.go(2 * r + 1, ua.at[REAR], ub.at[REAR])
                downs.came(2 * r - 1)
                downs.go(2 * r + 1, da.at[FRONT], db.at[FRONT])
                self.pass_on(2 * r - 1, ua, NZ - r)
                self.pass_on(2 * r, da, r)
            else:
                ups.came(4)
                ups.go(6, self.u3.at[FRONT], self.far.at[FRONT])
                downs.came(4)
                downs.go(6, self.d3.at[REAR], self.far.at[REAR])
                ups.came(5)
                downs.came(5)
                self.pass_on(5, self.u3, 5)
                self.pass_on(6, self.d3, 3)

        def last(self):
            self.ups.came(6)
            self.downs.came(6)
            self.pass_on(7, self.far, 4)

        def spread(self):
            h = self.h
            for cp in self.hand:
                cp.wait_recv()
            for i in range(2):
                for t in (4, 3, 5, 2, 6, 1, 7, 0):
                    to = (dp + t) % ND
                    k = (to + 8 * i) % NS
                    if t == 0:
                        gx[h][i, dp] = got[h][source_of[k]]
                        continue
                    xs[h][i, t] = got[h][source_of[k]]
                    cp = remote(xs[h].at[i, t], gx[h].at[i, dp], x_sem.at[h, 0, i, t],
                                x_sem.at[h, 1, i, t], {"dp": to})
                    cp.start()
                    sent.append(cp)
                    self.given.append(cp)

        def open(self):
            h = self.h
            for cp in self.given:
                cp.wait_recv()
            for i in range(2):
                blk = block_at[(dp + 8 * i) % NS]

                def stripe(t, _):
                    scales = scale_of(gx[h][i, t, 128:HALF, :])
                    for kk in range(2):
                        v = (widen(gx[h][i, t, kk * SR:kk * SR + SR, :])
                             * scale_row(scales, blk * 2 + kk))
                        hi, lo = split(v)
                        cols = slice((2 * h + kk) * CH, (2 * h + kk + 1) * CH)
                        ghi[i, rows_of(t), cols] = hi
                        glo[i, rows_of(t), cols] = lo
                    return 0

                lax.fori_loop(0, ND, stripe, 0)

        def project(self):
            cols = slice(256 * self.h, 256 * self.h + 256)

            def part(m, _):
                i, rows = m // 2, rows_of(m % 2, 256)
                p = dot(lf[i, rows, :], ghi[i, :, cols]) + dot(lf[i, rows, :], glo[i, :, cols])
                hi, lo = split(p)
                phi[i, rows, cols] = hi
                plo[i, rows, cols] = lo
                return 0

            lax.fori_loop(0, 4, part, 0)

    class Train:
        def __init__(self, h, way, towards, land, out, ascending):
            self.h, self.land, self.out, self.ascending = h, land, out, ascending
            self.line = Line(h, way, towards)

        def place(self, r):
            return r if self.ascending else NZ - r

        def part(self, r, front, came):
            h, out = self.h, self.out
            src = ((z + self.place(r)) % NZ) * NY + y
            first, last, cut = (0, 4, FRONT) if front else (4, NB, BACK)

            def one(j, _):
                rows = pl.ds(pl.multiple_of(j * 128, 128), 128)
                o = plan[src * NB + j]
                new = ybuf[h][self.place(r)][lax.rem(o, NY)][0:128, :]
                if came is not None:
                    at = jnp.full((128, CH), (lax.div(o, NY) == z).astype(i32), i32)
                    new = jnp.where(at > 0, new.astype(i32), came[rows, :].astype(i32)).astype(i16)
                out[r - 1, rows, :] = new
                return 0

            lax.fori_loop(first, last, one, 0)
            return out.at[r - 1, cut], self.land[r - 1].at[cut]

        def scales(self, r, came):
            h, out = self.h, self.out
            src = ((z + self.place(r)) % NZ) * NY + y
            tile = jnp.zeros((16, CH), i32) if came is None else came[SCALES, :].astype(i32)
            for j in range(NB):
                o = plan[src * NB + j]
                new = ybuf[h][self.place(r)][lax.rem(o, NY)][128:HALF, :].astype(i32)
                at = (row_id // 2 == j).astype(i32) * (lax.div(o, NY) == z).astype(i32)
                tile = jnp.where(at > 0, new, tile)
            out[r - 1, SCALES, :] = tile.astype(i16)
            return out.at[r - 1, SCALES], self.land[r - 1].at[SCALES]

        def head(self, r):
            came = None
            if r < 3:
                self.line.came(2 * (2 - r) + 1)
                came = self.land[r]
            self.line.go(2 * (3 - r) + 1, *self.part(r, not self.ascending, came))

        def tail(self, r):
            came = None
            if r < 4:
                self.line.came(2 * (2 - r) + 2, 10 - r)
                came = self.land[r]
            self.line.go(2 * (3 - r) + 2, *self.part(r, self.ascending, came))
            self.line.go(11 - r, *self.scales(r, came))

        def arrived(self):
            self.line.came(5, 6, 10)

    class Inward:
        def __init__(self, h):
            self.h = h
            self.ups = Train(h, 2, up, ur[h], ush[h], True)
            self.downs = Train(h, 3, down, dr[h], dsh[h], False)
            self.hand, self.given = {}, []

        def multiply(self):
            h = self.h
            cols = slice(256 * h, 256 * h + 256)
            for i in range(2):
                def pairs(m, _):
                    b = (x + 2 + m) % 4
                    rows = rows_of(b, 128)
                    r = dot(jnp.concatenate((phi[i, rows, :], plo[i, rows, :]), axis=0),
                            rf[i, :, cols])
                    u = r[:128] + r[128:]
                    for cc in range(2):
                        sc = jnp.zeros((16, CH), f32)
                        for kk in range(2):
                            q, e = encode(u[cc * SR:cc * SR + SR, kk * CH:kk * CH + CH])
                            xu[h][i, b * 2 + cc, kk * SR:kk * SR + SR, :] = q
                            sc = jnp.where(row_id % 2 == kk, e, sc)
                        xu[h][i, b * 2 + cc, 128:HALF, :] = sc.astype(i32).astype(i16)
                    return 0

                lax.fori_loop(0, 4, pairs, 0)
                ux[h][dp + 8 * i] = xu[h][i, dp]
                for t in (4, 3, 5, 2, 6, 1, 7):
                    to = (dp + t) % ND
                    cp = remote(xu[h].at[i, to], ux[h].at[dp + 8 * i], x_sem.at[2 + h, 0, i, t],
                                x_sem.at[2 + h, 1, i, t], {"dp": to})
                    cp.start()
                    sent.append(cp)
                    self.given.append(cp)

        def arrive(self):
            for cp in self.given:
                cp.wait_recv()

        def across(self, n):
            h = self.h
            d = (z + n) % NZ
            self.hand[n] = []
            for t in range(1, NY):
                yy = (y + t) % NY
                yback[h][n, t - 1] = ux[h][slot_of[d * NY + yy]]
                cp = remote(yback[h].at[n, t - 1], ybuf[h][n].at[y], y_sem.at[2 + h, 0, n, t - 1],
                            y_sem.at[2 + h, 1, n, t - 1], {"owner": z * NY + yy})
                cp.start()
                sent.append(cp)
                self.hand[n].append(cp)
            ybuf[h][n][y] = ux[h][slot_of[d * NY + y]]

        def crossed(self, n):
            for cp in self.hand[n]:
                cp.wait_recv()

        def begin(self):
            self.across(4)
            self.across(3)
            self.across(5)

        def one(self):
            self.crossed(4)
            self.ups.tail(4)
            self.downs.tail(4)
            self.crossed(3)
            self.ups.head(3)
            self.crossed(5)
            self.downs.head(3)
            self.across(2)
            self.across(6)

        def two(self):
            self.ups.tail(3)
            self.downs.tail(3)
            self.across(1)
            self.across(7)
            self.crossed(2)
            self.ups.head(2)
            self.crossed(6)
            self.downs.head(2)

        def three(self):
            self.ups.tail(2)
            self.downs.tail(2)
            self.across(0)
            self.crossed(1)
            self.ups.head(1)
            self.crossed(7)
            self.downs.head(1)

        def four(self):
            self.ups.tail(1)
            self.downs.tail(1)

        def finish(self):
            h = self.h
            self.crossed(0)
            self.ups.arrived()
            self.downs.arrived()

            def take(j, _):
                o = plan[me * NB + j]
                near = ybuf[h][0][lax.rem(o, NY)]
                off = lax.rem(lax.div(o, NY) + NZ - z, NZ)
                above = (off < 4).astype(i32) + (off == 4).astype(i32) * (j >= 4).astype(i32)
                full = jnp.zeros((128, CH), i32)
                rows = pl.ds(pl.multiple_of(j * 128, 128), 128)
                local = (off == 0).astype(i32)
                code = jnp.where(full + above > 0, dr[h][0][rows, :].astype(i32),
                                 ur[h][0][rows, :].astype(i32))
                code = jnp.where(full + local > 0,
                                 near[0:128, :].astype(i32), code)
                tile = jnp.where(row_id * 0 + above > 0, dr[h][0][SCALES, :].astype(i32),
                                 ur[h][0][SCALES, :].astype(i32))
                tile = jnp.where(row_id * 0 + local > 0,
                                 near[128:HALF, :].astype(i32), tile)
                tile = scale_of(tile)
                for kk in range(2):
                    update[j, :, (2 * h + kk) * CH:(2 * h + kk + 1) * CH] = (
                        code[kk * SR:kk * SR + SR].astype(f32) * scale_row(tile, j * 2 + kk))
                return 0

            lax.fori_loop(0, NB, take, 0)

    stat_came = [[], []]

    def stat(which, i):
        def block(m, _):
            b = (x + 1 + m) % 4
            if which == 0:
                ohi, olo = ghi[i, rows_of(b, 128), :], glo[i, rows_of(b, 128), :]
                f = dot(jnp.concatenate((ohi, olo), axis=0), ghi[i], ((1,), (1,)))
                f = f[:128] + f[128:] + dot(ohi, glo[i], ((1,), (1,)))
            else:
                chi, clo = ghi[i, :, rows_of(b, 128)], glo[i, :, rows_of(b, 128)]
                f = (dot(chi, ghi[i], ((0,), (0,))) + dot(clo, ghi[i], ((0,), (0,)))
                     + dot(chi, glo[i], ((0,), (0,))))
            for cc in range(2):
                sc = jnp.zeros((16, CH), f32)
                for n in range(4):
                    q, e = encode(f[cc * SR:cc * SR + SR, n * CH:n * CH + CH])
                    sx[which][i, b * 2 + cc, n * SR:n * SR + SR, :] = q
                    sc = jnp.where(row_id == n, e, sc)
                sx[which][i, b * 2 + cc, 256:SLOT, :] = sc.astype(i32).astype(i16)
            return 0

        lax.fori_loop(0, 4, block, 0)
        sr[which][dp + 8 * i] = sx[which][i, dp]
        for t in (4, 3, 5, 2, 6, 1, 7):
            to = (dp + t) % ND
            cp = remote(sx[which].at[i, to], sr[which].at[dp + 8 * i], x_sem.at[4 + which, 0, i, t],
                        x_sem.at[4 + which, 1, i, t], {"dp": to})
            cp.start()
            sent.append(cp)
            stat_came[which].append(cp)

    def renew(which, held, out):
        for cp in stat_came[which]:
            cp.wait_recv()

        def slot(k, _):
            w = weight[k]
            scales = scale_of(sr[which][k, 256:SLOT, :])
            for n in range(4):
                cols = slice(n * CH, n * CH + CH)
                term = widen(sr[which][k, n * SR:n * SR + SR, :]) * scales[n:n + 1, :]
                held[k, :, cols] = stat_decay * held[k, :, cols] + w * term
            pltpu.make_async_copy(held.at[k], out.at[k], out_sem.at[which, k]).start()
            return 0

        lax.fori_loop(0, NS, slot, 0)

    out0, out1, in0, in1 = Outward(0), Outward(1), Inward(0), Inward(1)

    ready(0)
    fill(snd.at[0], lambda j, kk: pair_sum(0, j, kk))
    c0 = ship(0, right)
    ready(2)
    fill(snd.at[3], lambda j, kk: pair_sum(2, j, kk))
    c3 = ship(3, left)
    fill(snd.at[1], lambda j, kk: pair_sum(0, j, 2 + kk))
    c1 = ship(1, left)
    ready(1)
    c0.wait_recv()
    fill(snd.at[4], lambda j, kk: pair_sum(1, j, kk) + received(0, j, kk))
    c4 = ship(4, right)
    fill(snd.at[2], lambda j, kk: pair_sum(1, j, 2 + kk))
    c2 = ship(2, right)
    c1.wait_recv()
    fill(snd.at[5], lambda j, kk: pair_sum(2, j, 2 + kk) + received(1, j, kk))
    c5 = ship(5, left)
    ready(3)
    c3.wait_recv()
    c4.wait_recv()
    fill(unit[0], lambda j, kk: pair_sum(3, j, kk) + received(4, j, kk) + received(3, j, kk))
    out0.start()
    c2.wait_recv()
    c5.wait_recv()
    fill(unit[1], lambda j, kk: pair_sum(3, j, 2 + kk) + received(2, j, kk) + received(5, j, kk))
    roots = []
    for which, (src, dst) in enumerate(((left_root, lf), (right_root, rf))):
        for i in range(2):
            for t in range(1, ND):
                to = (dp + t) % ND
                cp = remote(src.at[(to + 8 * i) % NS], dst.at[i, rows_of(dp)],
                            x_sem.at[6 + which, 0, i, t], x_sem.at[6 + which, 1, i, t], {"dp": to})
                cp.start()
                sent.append(cp)
                roots.append(cp)
    out0.step(1)
    out0.step(2)
    out0.step(3)
    out1.start()
    out0.last()
    out1.step(1)
    out0.spread()
    out1.step(2)
    out0.open()
    out1.step(3)
    for cp in root_in:
        cp.wait()
    for cp in roots:
        cp.wait_recv()
    out0.project()
    out1.last()
    out1.spread()
    out1.open()
    out1.project()
    in0.multiply()
    in1.multiply()
    in0.arrive()
    in0.begin()
    in0.one()
    in1.arrive()
    stat(0, 0)
    in0.two()
    stat(1, 0)
    in0.three()
    stat(0, 1)
    in0.four()
    in1.begin()
    in1.one()
    stat(1, 1)
    in0.finish()
    in1.two()
    for cp in stat_in:
        cp.wait()
    renew(0, ls, left_new)
    in1.three()
    renew(1, rs, right_new)
    in1.four()
    in1.finish()

    def done(k, _):
        pltpu.make_async_copy(ls.at[k], left_new.at[k], out_sem.at[0, k]).wait()
        pltpu.make_async_copy(rs.at[k], right_new.at[k], out_sem.at[1, k]).wait()
        return 0

    lax.fori_loop(0, NS, done, 0)
    for cp in sent:
        cp.wait_send()


def shampoo(plan, grads, left_stat, right_stat, left_root, right_root):
    hbm = pl.BlockSpec(memory_space=pl.ANY)
    vmem = pltpu.VMEM
    unit = vmem((UNIT, CH), i16)
    return pl.pallas_call(
        shampoo_kernel,
        out_shape=(
            jax.ShapeDtypeStruct((NS, SR, BO), f32),
            jax.ShapeDtypeStruct((NS, SR, BO), f32),
            jax.ShapeDtypeStruct((NB, SR, BO), f32),
        ),
        in_specs=[pl.BlockSpec(memory_space=pltpu.SMEM), hbm, hbm, hbm, hbm, hbm],
        out_specs=(hbm, hbm, pl.BlockSpec(memory_space=vmem)),
        scratch_shapes=[
            pltpu.SMEM((NO,), i32),
            pltpu.SMEM((NS + NO,), i32),
            pltpu.SMEM((NS + NO,), i32),
            pltpu.SMEM((NS,), f32),
            vmem((4, NB, SR, BO), bf16),
            vmem((4, NB, SR, BO), bf16),
            vmem((6, UNIT, CH), i16),
            vmem((6, UNIT, CH), i16),
            *[unit] * 2,
            *[unit] * 14,
            *[vmem((NZ, NY - 1, HALF, CH), i16)] * 2,
            *[vmem((NO, HALF, CH), i16)] * 2,
            *[vmem((2, ND, HALF, CH), i16)] * 2,
            *[vmem((2, ND, HALF, CH), i16)] * 2,
            *[vmem((2, BO, BO), bf16)] * 6,
            *[vmem((2, ND, HALF, CH), i16)] * 2,
            *[vmem((2 * ND, HALF, CH), i16)] * 2,
            *[vmem((NY, HALF, CH), i16)] * 16,
            *[vmem((NZ, NY - 1, HALF, CH), i16)] * 2,
            *[unit] * 16,
            *[vmem((4, UNIT, CH), i16)] * 4,
            *[vmem((2, ND, SLOT, CH), i16)] * 2,
            *[vmem((2 * ND, SLOT, CH), i16)] * 2,
            vmem((NS, SR, BO), f32),
            vmem((NS, SR, BO), f32),
            vmem((NB, 128, CH), i16),
            pltpu.SemaphoreType.DMA((2, 4)),
            pltpu.SemaphoreType.DMA((10,)),
            pltpu.SemaphoreType.DMA((2, 6)),
            pltpu.SemaphoreType.DMA((2, 4, 2, 11)),
            pltpu.SemaphoreType.DMA((4, 2, NZ, NY - 1)),
            pltpu.SemaphoreType.DMA((8, 2, 2, ND)),
            pltpu.SemaphoreType.DMA((2, NS)),
        ],
        compiler_params=pltpu.CompilerParams(
            collective_id=0, has_side_effects=True, vmem_limit_bytes=LIMIT),
        name="shampoo",
    )(plan, grads, left_stat, right_stat, left_root, right_root)


def local(grads, plan, left_stat, right_stat, left_root, right_root):
    left_new, right_new, update = shampoo(
        plan, grads[0], left_stat[0], right_stat[0], left_root[0], right_root[0])
    return left_new[None], right_new[None], update


def solution(mesh):
    return jax.shard_map(
        local,
        mesh=mesh,
        in_specs=(
            P("dp", "owner", None, None),
            P(),
            P("owner", None, "dp", None),
            P("owner", None, "dp", None),
            P("owner", None, "dp", None),
            P("owner", None, "dp", None),
        ),
        out_specs=(
            P("owner", None, "dp", None),
            P("owner", None, "dp", None),
            P("owner", "dp", None),
        ),
        check_vma=False,
    )
```

```python
import functools

import jax
import jax.numpy as jnp
from jax import lax
from jax.experimental import pallas as pl
from jax.experimental.pallas import tpu as pltpu
from jax.sharding import PartitionSpec as P

MESH = pl.DeviceIdType.MESH
f32 = jnp.float32
bf16 = jnp.bfloat16
i16 = jnp.int16
i32 = jnp.int32

stat_decay = 0.95
fresh_share = 0.05

NB = 7
NO = 32
NS = 13
ND = 8
SR = 64
BO = 512
CH = 128
NY = 4
NZ = 8
SLOT = 272
UNIT = 464
LIMIT = 60 * 1024 * 1024


def encode(x):
    m = jnp.maximum(jnp.max(jnp.abs(x), axis=0, keepdims=True), 2.0 ** -100)
    e = jnp.floor(jnp.log2(m) * 256.0) + 1.0
    q = jnp.round(x * (32700.0 * jnp.exp2(e * (-1.0 / 256.0))))
    return q.astype(i32).astype(i16), e


def scale_of(e16):
    return jnp.exp2(e16.astype(i32).astype(f32) * (1.0 / 256.0)) * (1.0 / 32700.0)


def widen(q):
    return q.astype(i32).astype(f32)


def remote(src, dst, send, recv, where):
    return pltpu.make_async_remote_copy(
        src_ref=src, dst_ref=dst, send_sem=send, recv_sem=recv,
        device_id=where, device_id_type=MESH)


def dot(a, b, dims=((1,), (0,))):
    return lax.dot_general(a, b, (dims, ((), ())), preferred_element_type=f32)


class Part:
    def __init__(self, p, chunks):
        w = len(chunks)
        self.p, self.chunks, self.w = p, chunks, w
        self.cols = slice(chunks[0] * CH, (chunks[-1] + 1) * CH)
        self.rows = SR * w
        self.unit = NB * SR * w + 16
        self.message = SR * w + 16
        self.front = slice(0, 4 * SR * w)
        self.rear = slice(4 * SR * w, self.unit)
        self.back = slice(4 * SR * w, NB * SR * w)
        self.scales = slice(NB * SR * w, self.unit)
        self.data = slice(0, SR * w)
        self.tail = slice(SR * w, self.message)


PARTS = (Part(0, (0,)), Part(1, (1, 2)), Part(2, (3,)))
NP = len(PARTS)


def split(v):
    hi = v.astype(bf16)
    return hi, (v - hi.astype(f32)).astype(bf16)


def rows_of(t, n=SR):
    return pl.ds(pl.multiple_of(t * n, n), n)


def shampoo_kernel(plan, grads, left_stat, right_stat, left_root, right_root,
                   left_new, right_new, update, *scratch):
    it = iter(scratch)
    slot_of, source_of, block_at, weight = (next(it) for _ in range(4))
    own, par, snd, rcv = (next(it) for _ in range(4))
    unit = [next(it) for _ in PARTS]
    hops = [[next(it) for _ in range(7)] for _ in PARTS]
    ysend, got, xs, gx = ([next(it) for _ in PARTS] for _ in range(4))
    lf, rf, ghi, glo, phi, plo = (next(it) for _ in range(6))
    xu, ux = ([next(it) for _ in PARTS] for _ in range(2))
    ybuf = [[next(it) for _ in range(8)] for _ in PARTS]
    yback = [next(it) for _ in PARTS]
    ur = [[next(it) for _ in range(4)] for _ in PARTS]
    dr = [[next(it) for _ in range(4)] for _ in PARTS]
    ush = [next(it) for _ in PARTS]
    dsh = [next(it) for _ in PARTS]
    sx, sr = ([next(it) for _ in range(2)] for _ in range(2))
    ls, rs = next(it), next(it)
    shelves = [next(it) for _ in PARTS]
    pair_sem, load_sem, unit_sem, line_sem, y_sem, x_sem, out_sem = (next(it) for _ in range(7))

    me = lax.axis_index("owner")
    z, y = me // NY, me % NY
    up, down = ((z + 1) % NZ) * NY + y, ((z + NZ - 1) % NZ) * NY + y
    dp = lax.axis_index("dp")
    x, c = dp // 2, dp % 2
    partner = x * 2 + 1 - c
    right = ((x + 1) % 4) * 2 + c
    left = ((x + 3) % 4) * 2 + c
    row_id = lax.broadcasted_iota(i32, (16, CH), 0)
    sent = []

    mine = {}
    for n, off in ((0, 2), (2, 3), (1, 1), (3, 0)):
        t = ((x + off) % 4) * 2 + c
        mine[n] = pltpu.make_async_copy(grads.at[:, rows_of(t), :], own.at[n], load_sem.at[n])
        mine[n].start()
    stat_in = [pltpu.make_async_copy(left_stat, ls, load_sem.at[4]),
               pltpu.make_async_copy(right_stat, rs, load_sem.at[5])]
    root_in = []
    for i in range(2):
        k = (dp + 8 * i) % NS
        root_in.append(pltpu.make_async_copy(
            left_root.at[k], lf.at[i, rows_of(dp)], load_sem.at[6 + i]))
        root_in.append(pltpu.make_async_copy(
            right_root.at[k], rf.at[i, rows_of(dp)], load_sem.at[8 + i]))

    barrier = pltpu.get_barrier_semaphore()
    for t in range(1, ND):
        pl.semaphore_signal(
            barrier, inc=1, device_id={"dp": (dp + t) % ND}, device_id_type=MESH)
    for place in [up, down] + [z * NY + (y + t) % NY for t in range(1, NY)]:
        pl.semaphore_signal(barrier, inc=1, device_id={"owner": place}, device_id_type=MESH)
    pl.semaphore_wait(barrier, ND - 1 + 2 + NY - 1)

    pair = {}
    for n, off in ((0, 2), (2, 3), (1, 1), (3, 0)):
        t = ((x + off) % 4) * 2 + 1 - c
        pair[n] = remote(grads.at[:, rows_of(t), :], par.at[n],
                         pair_sem.at[0, n], pair_sem.at[1, n], {"dp": partner})
        pair[n].start()
        sent.append(pair[n])
    for cp in root_in + stat_in:
        cp.start()

    def stand(i, count):
        hold, which = jnp.int32(0), jnp.int32(0)
        for j in range(NB):
            hit = (plan[i * NB + j] == me).astype(i32)
            hold = hold + hit * (1 - hold)
            which = which + hit * (j - which)
        slot_of[i] = count * (count < NS).astype(i32)
        source_of[NS + i] = hold * (count + 1) - 1
        block_at[NS + i] = which
        return count + hold

    count = lax.fori_loop(0, NO, stand, jnp.int32(0))

    def place_slots():
        def place(k, _):
            src, blk = jnp.int32(0), jnp.int32(0)
            for i in range(NO):
                hit = (source_of[NS + i] == k).astype(i32)
                src = src + hit * (i - src)
                blk = blk + hit * (block_at[NS + i] - blk)
            source_of[k] = src
            block_at[k] = blk
            weight[k] = fresh_share * (k < count).astype(i32).astype(f32)
            return 0

        lax.fori_loop(0, NS, place, 0)

    def pair_sum(n, j, k):
        cols = slice(k * CH, k * CH + CH)
        return own[n, j, :, cols].astype(f32) + par[n, j, :, cols].astype(f32)

    def scale_row(scales, r):
        return jnp.sum(jnp.where(row_id == r, scales, 0.0), axis=0, keepdims=True)

    def received(u, j):
        scales = scale_of(rcv[u, NB * SR:UNIT, :])
        return widen(rcv[u, j * SR:j * SR + SR, :]) * scales[j:j + 1, :]

    def fill(out, w, value):
        sc = jnp.zeros((16, CH), f32)
        for j in range(NB):
            for kk in range(w):
                r = j * w + kk
                q, e = encode(value(j, kk))
                out[r * SR:r * SR + SR, :] = q
                sc = jnp.where(row_id == r, e, sc)
        out[NB * SR * w:NB * SR * w + 16, :] = sc.astype(i32).astype(i16)

    def ship(u, to):
        cp = remote(snd.at[u], rcv.at[u], unit_sem.at[0, u], unit_sem.at[1, u], {"dp": to})
        cp.start()
        sent.append(cp)
        return cp

    def ready(n):
        mine[n].wait()
        pair[n].wait_recv()

    class Line:
        def __init__(self, p, way, towards):
            self.p, self.way, self.towards = p, way, towards
            self.copies = {}

        def go(self, n, src, dst):
            cp = remote(src, dst, line_sem.at[self.p, self.way, 0, n],
                        line_sem.at[self.p, self.way, 1, n], {"owner": self.towards})
            cp.start()
            sent.append(cp)
            self.copies[n] = cp

        def came(self, *names):
            for n in names:
                self.copies[n].wait_recv()

    class Outward:
        def __init__(self, part):
            self.part, self.p = part, part.p
            self.u1, self.u2, self.u3, self.d1, self.d2, self.d3, self.far = hops[part.p]
            self.ups, self.downs = Line(part.p, 0, up), Line(part.p, 1, down)
            self.hand, self.given = [], []

        def pass_on(self, n, ref, rel):
            part, p = self.part, self.p
            shelf = shelves[p]
            src = ((z + rel) % NZ) * NY + y

            def code(yy):
                j = jnp.int32(0)
                for b in range(NB):
                    j = j + (plan[src * NB + b] == z * NY + yy).astype(i32) * (b - j)
                return shelf[j]

            for b in range(NB):
                shelf[b] = ref[b * part.rows:(b + 1) * part.rows, :]
            scales = ref[part.scales, :]
            for t in range(1, NY):
                yy = (y + t) % NY
                ysend[p][n, t - 1, part.data, :] = code(yy)
                ysend[p][n, t - 1, part.tail, :] = scales
                cp = remote(ysend[p].at[n, t - 1], got[p].at[src], y_sem.at[p, 0, n, t - 1],
                            y_sem.at[p, 1, n, t - 1], {"owner": z * NY + yy})
                cp.start()
                sent.append(cp)
                self.hand.append(cp)
            got[p][src, part.data, :] = code(y)
            got[p][src, part.tail, :] = scales

        def start(self):
            front, rear = self.part.front, self.part.rear
            g = unit[self.p]
            self.ups.go(0, g.at[front], self.u1.at[front])
            self.downs.go(0, g.at[rear], self.d1.at[rear])
            self.ups.go(1, g.at[rear], self.u1.at[rear])
            self.downs.go(1, g.at[front], self.d1.at[front])
            self.pass_on(0, g, 0)

        def step(self, r):
            ups, downs = self.ups, self.downs
            front, rear = self.part.front, self.part.rear
            if r < 3:
                ua, ub = ((self.u1, self.u2), (self.u2, self.u3))[r - 1]
                da, db = ((self.d1, self.d2), (self.d2, self.d3))[r - 1]
                ups.came(2 * r - 2)
                ups.go(2 * r, ua.at[front], ub.at[front])
                downs.came(2 * r - 2)
                downs.go(2 * r, da.at[rear], db.at[rear])
                ups.came(2 * r - 1)
                ups.go(2 * r + 1, ua.at[rear], ub.at[rear])
                downs.came(2 * r - 1)
                downs.go(2 * r + 1, da.at[front], db.at[front])
                self.pass_on(2 * r - 1, ua, NZ - r)
                self.pass_on(2 * r, da, r)
            else:
                ups.came(4)
                ups.go(6, self.u3.at[front], self.far.at[front])
                downs.came(4)
                downs.go(6, self.d3.at[rear], self.far.at[rear])
                ups.came(5)
                downs.came(5)
                self.pass_on(5, self.u3, 5)
                self.pass_on(6, self.d3, 3)

        def last(self):
            self.ups.came(6)
            self.downs.came(6)
            self.pass_on(7, self.far, 4)

        def spread(self):
            p = self.p
            for cp in self.hand:
                cp.wait_recv()
            for t in (4, 3, 5, 2, 6, 1, 7, 0):
                for i in range(2):
                    to = (dp + t) % ND
                    k = (to + 8 * i) % NS
                    if t == 0:
                        gx[p][i, dp] = got[p][source_of[k]]
                        continue
                    xs[p][i, t] = got[p][source_of[k]]
                    cp = remote(xs[p].at[i, t], gx[p].at[i, dp], x_sem.at[p, 0, i, t],
                                x_sem.at[p, 1, i, t], {"dp": to})
                    cp.start()
                    sent.append(cp)
                    self.given.append(cp)

        def open(self):
            part, p = self.part, self.p
            for cp in self.given:
                cp.wait_recv()
            for i in range(2):
                blk = block_at[(dp + 8 * i) % NS]
                for t in range(ND):
                    scales = scale_of(gx[p][i, t, part.tail, :])
                    for kk, n in enumerate(part.chunks):
                        v = (widen(gx[p][i, t, kk * SR:kk * SR + SR, :])
                             * scale_row(scales, blk * part.w + kk))
                        hi, lo = split(v)
                        ghi[i, t * SR:t * SR + SR, n * CH:n * CH + CH] = hi
                        glo[i, t * SR:t * SR + SR, n * CH:n * CH + CH] = lo

        def project(self):
            cols = self.part.cols

            def part(m, _):
                i, rows = m // 2, rows_of(m % 2, 256)
                p = dot(lf[i, rows, :], ghi[i, :, cols]) + dot(lf[i, rows, :], glo[i, :, cols])
                hi, lo = split(p)
                phi[i, rows, cols] = hi
                plo[i, rows, cols] = lo
                return 0

            lax.fori_loop(0, 4, part, 0, unroll=True)

    class Train:
        def __init__(self, part, way, towards, land, out, ascending):
            self.part, self.p, self.land, self.out = part, part.p, land, out
            self.ascending = ascending
            self.line = Line(part.p, way, towards)

        def place(self, r):
            return r if self.ascending else NZ - r

        def blocks(self, r, front, came):
            p, part, out = self.p, self.part, self.out
            src = ((z + self.place(r)) % NZ) * NY + y
            first, last, cut = (0, 4, part.front) if front else (4, NB, part.back)
            for j in range(first, last):
                rows = slice(j * part.rows, (j + 1) * part.rows)
                o = plan[src * NB + j]
                new = ybuf[p][self.place(r)][lax.rem(o, NY)][part.data, :]
                if came is not None:
                    at = jnp.full((part.rows, CH), (lax.div(o, NY) == z).astype(i32), i32)
                    new = jnp.where(at > 0, new.astype(i32), came[rows, :].astype(i32)).astype(i16)
                out[r - 1, rows, :] = new
            return out.at[r - 1, cut], self.land[r - 1].at[cut]

        def scales(self, r, came):
            p, part, out = self.p, self.part, self.out
            src = ((z + self.place(r)) % NZ) * NY + y
            tile = jnp.zeros((16, CH), i32) if came is None else came[part.scales, :].astype(i32)
            for j in range(NB):
                o = plan[src * NB + j]
                new = ybuf[p][self.place(r)][lax.rem(o, NY)][part.tail, :].astype(i32)
                at = (row_id // part.w == j).astype(i32) * (lax.div(o, NY) == z).astype(i32)
                tile = jnp.where(at > 0, new, tile)
            out[r - 1, part.scales, :] = tile.astype(i16)
            return out.at[r - 1, part.scales], self.land[r - 1].at[part.scales]

        def head(self, r):
            came = None
            if r < 3:
                self.line.came(2 * (2 - r) + 1)
                came = self.land[r]
            self.line.go(2 * (3 - r) + 1, *self.blocks(r, not self.ascending, came))

        def tail(self, r):
            came = None
            if r < 4:
                self.line.came(2 * (2 - r) + 2, 10 - r)
                came = self.land[r]
            self.line.go(2 * (3 - r) + 2, *self.blocks(r, self.ascending, came))
            self.line.go(11 - r, *self.scales(r, came))

        def arrived(self):
            self.line.came(5, 6, 10)

    class Inward:
        def __init__(self, part):
            self.part, self.p = part, part.p
            self.ups = Train(part, 2, up, ur[part.p], ush[part.p], True)
            self.downs = Train(part, 3, down, dr[part.p], dsh[part.p], False)
            self.hand, self.given = {}, []

        def multiply(self, i):
            part, p = self.part, self.p

            def pairs(m, _):
                b = (x + 2 + m) % 4
                rows = rows_of(b, 128)
                r = dot(jnp.concatenate((phi[i, rows, :], plo[i, rows, :]), axis=0),
                        rf[i, :, part.cols])
                u = r[:128] + r[128:]
                for cc in range(2):
                    sc = jnp.zeros((16, CH), f32)
                    for kk in range(part.w):
                        q, e = encode(u[cc * SR:cc * SR + SR, kk * CH:kk * CH + CH])
                        xu[p][i, b * 2 + cc, kk * SR:kk * SR + SR, :] = q
                        sc = jnp.where(row_id % part.w == kk, e, sc)
                    xu[p][i, b * 2 + cc, part.tail, :] = sc.astype(i32).astype(i16)
                return 0

            lax.fori_loop(0, 4, pairs, 0, unroll=True)

        def hand_out(self, i):
            p = self.p
            ux[p][dp + 8 * i] = xu[p][i, dp]
            for t in (4, 3, 5, 2, 6, 1, 7):
                to = (dp + t) % ND
                cp = remote(xu[p].at[i, to], ux[p].at[dp + 8 * i], x_sem.at[NP + p, 0, i, t],
                            x_sem.at[NP + p, 1, i, t], {"dp": to})
                cp.start()
                sent.append(cp)
                self.given.append(cp)

        def arrive(self):
            for cp in self.given:
                cp.wait_recv()

        def across(self, n):
            p = self.p
            d = (z + n) % NZ
            self.hand[n] = []
            for t in range(1, NY):
                yy = (y + t) % NY
                yback[p][n, t - 1] = ux[p][slot_of[d * NY + yy]]
                cp = remote(yback[p].at[n, t - 1], ybuf[p][n].at[y],
                            y_sem.at[NP + p, 0, n, t - 1], y_sem.at[NP + p, 1, n, t - 1],
                            {"owner": z * NY + yy})
                cp.start()
                sent.append(cp)
                self.hand[n].append(cp)
            ybuf[p][n][y] = ux[p][slot_of[d * NY + y]]

        def crossed(self, n):
            for cp in self.hand[n]:
                cp.wait_recv()

        def begin(self):
            self.across(4)
            self.across(3)
            self.across(5)

        def one(self):
            self.crossed(4)
            self.ups.tail(4)
            self.downs.tail(4)
            self.crossed(3)
            self.ups.head(3)
            self.crossed(5)
            self.downs.head(3)
            self.across(2)
            self.across(6)

        def two(self):
            self.ups.tail(3)
            self.downs.tail(3)
            self.across(1)
            self.across(7)
            self.crossed(2)
            self.ups.head(2)
            self.crossed(6)
            self.downs.head(2)

        def three(self):
            self.ups.tail(2)
            self.downs.tail(2)
            self.across(0)
            self.crossed(1)
            self.ups.head(1)
            self.crossed(7)
            self.downs.head(1)

        def four(self):
            self.ups.tail(1)
            self.downs.tail(1)

        def finish(self):
            part, p = self.part, self.p
            self.crossed(0)
            self.ups.arrived()
            self.downs.arrived()
            for j in range(NB):
                o = plan[me * NB + j]
                near = ybuf[p][0][lax.rem(o, NY)].astype(i32)
                off = lax.rem(lax.div(o, NY) + NZ - z, NZ)
                above = (off < 4).astype(i32)
                if j >= 4:
                    above = above + (off == 4).astype(i32)
                local = (off == 0).astype(i32)
                rows = slice(j * part.rows, (j + 1) * part.rows)
                full = jnp.zeros((part.rows, CH), i32)
                code = jnp.where(full + above > 0, dr[p][0][rows, :].astype(i32),
                                 ur[p][0][rows, :].astype(i32))
                code = jnp.where(full + local > 0, near[part.data, :], code)
                tile = jnp.where(row_id * 0 + above > 0, dr[p][0][part.scales, :].astype(i32),
                                 ur[p][0][part.scales, :].astype(i32))
                tile = jnp.where(row_id * 0 + local > 0, near[part.tail, :], tile)
                tile = scale_of(tile)
                for kk, n in enumerate(part.chunks):
                    r = j * part.w + kk
                    update[j, :, n * CH:n * CH + CH] = (
                        code[kk * SR:kk * SR + SR].astype(f32) * tile[r:r + 1, :])

    stat_came = [[], []]

    def stat(which, i):
        def block(m, _):
            b = (x + 1 + m) % 4
            if which == 0:
                ohi, olo = ghi[i, rows_of(b, 128), :], glo[i, rows_of(b, 128), :]
                f = dot(jnp.concatenate((ohi, olo), axis=0), ghi[i], ((1,), (1,)))
                f = f[:128] + f[128:] + dot(ohi, glo[i], ((1,), (1,)))
            else:
                chi, clo = ghi[i, :, rows_of(b, 128)], glo[i, :, rows_of(b, 128)]
                f = (dot(chi, ghi[i], ((0,), (0,))) + dot(clo, ghi[i], ((0,), (0,)))
                     + dot(chi, glo[i], ((0,), (0,))))
            for cc in range(2):
                sc = jnp.zeros((16, CH), f32)
                for n in range(4):
                    q, e = encode(f[cc * SR:cc * SR + SR, n * CH:n * CH + CH])
                    sx[which][i, b * 2 + cc, n * SR:n * SR + SR, :] = q
                    sc = jnp.where(row_id == n, e, sc)
                sx[which][i, b * 2 + cc, 256:SLOT, :] = sc.astype(i32).astype(i16)
            return 0

        lax.fori_loop(0, 4, block, 0, unroll=2)
        sr[which][dp + 8 * i] = sx[which][i, dp]
        for t in (4, 3, 5, 2, 6, 1, 7):
            to = (dp + t) % ND
            cp = remote(sx[which].at[i, to], sr[which].at[dp + 8 * i], x_sem.at[2 * NP + which, 0, i, t],
                        x_sem.at[2 * NP + which, 1, i, t], {"dp": to})
            cp.start()
            sent.append(cp)
            stat_came[which].append(cp)

    def renew(which, held, out):
        for cp in stat_came[which]:
            cp.wait_recv()

        def slot(k, _):
            w = weight[k]
            scales = scale_of(sr[which][k, 256:SLOT, :])
            for n in range(4):
                cols = slice(n * CH, n * CH + CH)
                term = widen(sr[which][k, n * SR:n * SR + SR, :]) * scales[n:n + 1, :]
                held[k, :, cols] = stat_decay * held[k, :, cols] + w * term
            pltpu.make_async_copy(held.at[k], out.at[k], out_sem.at[which, k]).start()
            return 0

        lax.fori_loop(0, NS, slot, 0)

    out0, out1, out2 = (Outward(part) for part in PARTS)
    in0, in1, in2 = (Inward(part) for part in PARTS)
    right_far, left_far, right_straight, left_straight, right_both, left_both = {}, {}, {}, {}, {}, {}

    def far(k):
        fill(snd.at[k], 1, lambda j, kk: pair_sum(0, j, k))
        if k < 2:
            right_far[k] = ship(k, right)
        else:
            left_far[k] = ship(k, left)

    def straight(k):
        if k >= 2:
            fill(snd.at[4 + k], 1, lambda j, kk: pair_sum(1, j, k))
            right_straight[k] = ship(4 + k, right)
        else:
            fill(snd.at[4 + k], 1, lambda j, kk: pair_sum(2, j, k))
            left_straight[k] = ship(4 + k, left)

    def both(k):
        if k < 2:
            right_far[k].wait_recv()
            fill(snd.at[8 + k], 1, lambda j, kk: pair_sum(1, j, k) + received(k, j))
            right_both[k] = ship(8 + k, right)
        else:
            left_far[k].wait_recv()
            fill(snd.at[8 + k], 1, lambda j, kk: pair_sum(2, j, k) + received(k, j))
            left_both[k] = ship(8 + k, left)

    def total(part):
        for k in part.chunks:
            for cps in (right_straight, left_straight, right_both, left_both):
                if k in cps:
                    cps[k].wait_recv()
        fill(unit[part.p], part.w, lambda j, kk: (
            pair_sum(3, j, part.chunks[kk]) + received(4 + part.chunks[kk], j)
            + received(8 + part.chunks[kk], j)))

    ready(0)
    far(0)
    far(1)
    ready(2)
    straight(0)
    far(2)
    far(3)
    ready(1)
    both(0)
    straight(1)
    both(1)
    straight(2)
    straight(3)
    ready(3)
    total(PARTS[0])
    out0.start()
    both(2)
    both(3)
    out0.step(1)
    total(PARTS[1])
    out1.start()
    out0.step(2)
    total(PARTS[2])
    roots = []
    for which, (src, dst) in enumerate(((left_root, lf), (right_root, rf))):
        for i in range(2):
            for t in range(1, ND):
                to = (dp + t) % ND
                cp = remote(src.at[(to + 8 * i) % NS], dst.at[i, rows_of(dp)],
                            x_sem.at[2 * NP + 2 + which, 0, i, t],
                            x_sem.at[2 * NP + 2 + which, 1, i, t], {"dp": to})
                cp.start()
                sent.append(cp)
                roots.append(cp)
    out0.step(3)
    out1.step(1)
    place_slots()
    out0.last()
    out1.step(2)
    out0.spread()
    out1.step(3)
    out2.start()
    out0.open()
    out1.last()
    out2.step(1)
    out1.spread()
    out2.step(2)
    for cp in root_in:
        cp.wait()
    for cp in roots:
        cp.wait_recv()
    out0.project()
    out2.step(3)
    out1.open()
    out1.project()
    out2.last()
    out2.spread()
    out2.open()
    out2.project()
    in0.multiply(0)
    in0.hand_out(0)
    in0.multiply(1)
    in0.hand_out(1)
    in1.multiply(0)
    in1.multiply(1)
    in0.arrive()
    in0.begin()
    in1.hand_out(0)
    in1.hand_out(1)
    in0.one()
    in2.multiply(0)
    in2.multiply(1)
    in0.two()
    in1.arrive()
    in1.begin()
    in2.hand_out(0)
    in2.hand_out(1)
    in1.one()
    in0.three()
    stat(0, 0)
    in0.four()
    in1.two()
    stat(1, 0)
    in2.arrive()
    in2.begin()
    in1.three()
    in2.one()
    stat(0, 1)
    in1.four()
    in0.finish()
    in2.two()
    stat(1, 1)
    in2.three()
    for cp in stat_in:
        cp.wait()
    in1.finish()
    in2.four()
    renew(0, ls, left_new)
    renew(1, rs, right_new)
    in2.finish()

    def done(k, _):
        pltpu.make_async_copy(ls.at[k], left_new.at[k], out_sem.at[0, k]).wait()
        pltpu.make_async_copy(rs.at[k], right_new.at[k], out_sem.at[1, k]).wait()
        return 0

    lax.fori_loop(0, NS, done, 0)
    for cp in sent:
        cp.wait_send()


def shampoo(plan, grads, left_stat, right_stat, left_root, right_root):
    hbm = pl.BlockSpec(memory_space=pl.ANY)
    vmem = pltpu.VMEM

    def each(lead, rows, times=1):
        return [vmem((*lead, rows(part), CH), i16) for part in PARTS for _ in range(times)]

    def unit(part):
        return part.unit

    def message(part):
        return part.message

    return pl.pallas_call(
        shampoo_kernel,
        out_shape=(
            jax.ShapeDtypeStruct((NS, SR, BO), f32),
            jax.ShapeDtypeStruct((NS, SR, BO), f32),
            jax.ShapeDtypeStruct((NB, SR, BO), f32),
        ),
        in_specs=[pl.BlockSpec(memory_space=pltpu.SMEM), hbm, hbm, hbm, hbm, hbm],
        out_specs=(hbm, hbm, pl.BlockSpec(memory_space=vmem)),
        scratch_shapes=[
            pltpu.SMEM((NO,), i32),
            pltpu.SMEM((NS + NO,), i32),
            pltpu.SMEM((NS + NO,), i32),
            pltpu.SMEM((NS,), f32),
            vmem((4, NB, SR, BO), bf16),
            vmem((4, NB, SR, BO), bf16),
            vmem((12, UNIT, CH), i16),
            vmem((12, UNIT, CH), i16),
            *each((), unit),
            *each((), unit, 7),
            *each((NZ, NY - 1), message),
            *each((NO,), message),
            *each((2, ND), message),
            *each((2, ND), message),
            *[vmem((2, BO, BO), bf16)] * 6,
            *each((2, ND), message),
            *each((2 * ND,), message),
            *each((NY,), message, NZ),
            *each((NZ, NY - 1), message),
            *each((), unit, 4),
            *each((), unit, 4),
            *each((4,), unit),
            *each((4,), unit),
            *[vmem((2, ND, SLOT, CH), i16)] * 2,
            *[vmem((2 * ND, SLOT, CH), i16)] * 2,
            vmem((NS, SR, BO), f32),
            vmem((NS, SR, BO), f32),
            *[vmem((NB, part.rows, CH), i16) for part in PARTS],
            pltpu.SemaphoreType.DMA((2, 4)),
            pltpu.SemaphoreType.DMA((10,)),
            pltpu.SemaphoreType.DMA((2, 12)),
            pltpu.SemaphoreType.DMA((NP, 4, 2, 11)),
            pltpu.SemaphoreType.DMA((2 * NP, 2, NZ, NY - 1)),
            pltpu.SemaphoreType.DMA((2 * NP + 4, 2, 2, ND)),
            pltpu.SemaphoreType.DMA((2, NS)),
        ],
        compiler_params=pltpu.CompilerParams(
            collective_id=0, has_side_effects=True, vmem_limit_bytes=LIMIT),
        name="shampoo",
    )(plan, grads, left_stat, right_stat, left_root, right_root)


def local(grads, plan, left_stat, right_stat, left_root, right_root):
    left_new, right_new, update = shampoo(
        plan, grads[0], left_stat[0], right_stat[0], left_root[0], right_root[0])
    return left_new[None], right_new[None], update


def solution(mesh):
    return jax.shard_map(
        local,
        mesh=mesh,
        in_specs=(
            P("dp", "owner", None, None),
            P(),
            P("owner", None, "dp", None),
            P("owner", None, "dp", None),
            P("owner", None, "dp", None),
            P("owner", None, "dp", None),
        ),
        out_specs=(
            P("owner", None, "dp", None),
            P("owner", None, "dp", None),
            P("owner", "dp", None),
        ),
        check_vma=False,
    )
```

```python
import functools

import jax
import jax.numpy as jnp
from jax import lax
from jax.experimental import pallas as pl
from jax.experimental.pallas import tpu as pltpu
from jax.sharding import PartitionSpec as P

MESH = pl.DeviceIdType.MESH
f32 = jnp.float32
bf16 = jnp.bfloat16
i16 = jnp.int16
i32 = jnp.int32

stat_decay = 0.95
fresh_share = 0.05

NB = 7
NO = 32
NS = 13
ND = 8
SR = 64
BO = 512
CH = 128
NY = 4
NZ = 8
SLOT = 272
UNIT = 464
LIMIT = 60 * 1024 * 1024


def encode(x):
    m = jnp.maximum(jnp.max(jnp.abs(x), axis=0, keepdims=True), 2.0 ** -100)
    e = jnp.floor(jnp.log2(m) * 256.0) + 1.0
    q = jnp.round(x * (32700.0 * jnp.exp2(e * (-1.0 / 256.0))))
    return q.astype(i32).astype(i16), e


def scale_of(e16):
    return jnp.exp2(e16.astype(i32).astype(f32) * (1.0 / 256.0)) * (1.0 / 32700.0)


def widen(q):
    return q.astype(i32).astype(f32)


def remote(src, dst, send, recv, where):
    return pltpu.make_async_remote_copy(
        src_ref=src, dst_ref=dst, send_sem=send, recv_sem=recv,
        device_id=where, device_id_type=MESH)


def dot(a, b, dims=((1,), (0,))):
    return lax.dot_general(a, b, (dims, ((), ())), preferred_element_type=f32)


class Part:
    def __init__(self, p, chunks):
        w = len(chunks)
        self.p, self.chunks, self.w = p, chunks, w
        self.cols = slice(chunks[0] * CH, (chunks[-1] + 1) * CH)
        self.rows = SR * w
        self.unit = NB * SR * w + 16
        self.message = SR * w + 16
        self.front = slice(0, 4 * SR * w)
        self.rear = slice(4 * SR * w, self.unit)
        self.back = slice(4 * SR * w, NB * SR * w)
        self.scales = slice(NB * SR * w, self.unit)
        self.data = slice(0, SR * w)
        self.tail = slice(SR * w, self.message)
        self.far = 2 * SR * w + 16
        self.six = 6 * SR * w + 16


PARTS = (Part(0, (0,)), Part(1, (1, 2)), Part(2, (3,)))
NP = len(PARTS)


def split(v):
    hi = v.astype(bf16)
    return hi, (v - hi.astype(f32)).astype(bf16)


def rows_of(t, n=SR):
    return pl.ds(pl.multiple_of(t * n, n), n)


def shampoo_kernel(plan, grads, left_stat, right_stat, left_root, right_root,
                   left_new, right_new, update, *scratch):
    it = iter(scratch)
    slot_of, source_of, block_at, weight = (next(it) for _ in range(4))
    own, par, snd, rcv = (next(it) for _ in range(4))
    unit = [next(it) for _ in PARTS]
    hops = [[next(it) for _ in range(9)] for _ in PARTS]
    ysend, got, xs, gx = ([next(it) for _ in PARTS] for _ in range(4))
    lf, rf, ghi, glo, phi, plo = (next(it) for _ in range(6))
    xu, ux = ([next(it) for _ in PARTS] for _ in range(2))
    ybuf = [[next(it) for _ in range(8)] for _ in PARTS]
    yback = [next(it) for _ in PARTS]
    ur = [[next(it) for _ in range(7)] for _ in PARTS]
    dr = [[next(it) for _ in range(7)] for _ in PARTS]
    sx, sr = ([next(it) for _ in range(2)] for _ in range(2))
    ls, rs = next(it), next(it)
    shelves = [next(it) for _ in PARTS]
    pair_sem, load_sem, unit_sem, line_sem, y_sem, back_sem, x_sem, out_sem = (
        next(it) for _ in range(8))

    me = lax.axis_index("owner")
    z, y = me // NY, me % NY
    up, down = ((z + 1) % NZ) * NY + y, ((z + NZ - 1) % NZ) * NY + y
    dp = lax.axis_index("dp")
    x, c = dp // 2, dp % 2
    partner = x * 2 + 1 - c
    right = ((x + 1) % 4) * 2 + c
    left = ((x + 3) % 4) * 2 + c
    row_id = lax.broadcasted_iota(i32, (16, CH), 0)
    sent = []
    group = []

    def whole(ref, sems):
        cp = remote(ref, ref, sems.at[0], sems.at[1], {"dp": partner})
        group.append(cp)
        return cp

    mine = {}
    for n, off in ((0, 2), (2, 3), (1, 1), (3, 0)):
        t = ((x + off) % 4) * 2 + c
        mine[n] = pltpu.make_async_copy(grads.at[:, rows_of(t), :], own.at[n], load_sem.at[n])
        mine[n].start()
    stat_in = [pltpu.make_async_copy(left_stat, ls, load_sem.at[4]),
               pltpu.make_async_copy(right_stat, rs, load_sem.at[5])]
    root_in = []
    for i in range(2):
        k = (dp + 8 * i) % NS
        root_in.append(pltpu.make_async_copy(
            left_root.at[k], lf.at[i, rows_of(dp)], load_sem.at[6 + i]))
        root_in.append(pltpu.make_async_copy(
            right_root.at[k], rf.at[i, rows_of(dp)], load_sem.at[8 + i]))

    barrier = pltpu.get_barrier_semaphore()
    for t in range(1, ND):
        pl.semaphore_signal(
            barrier, inc=1, device_id={"dp": (dp + t) % ND}, device_id_type=MESH)
    for place in [up, down] + [z * NY + (y + t) % NY for t in range(1, NY)]:
        pl.semaphore_signal(barrier, inc=1, device_id={"owner": place}, device_id_type=MESH)
    pl.semaphore_wait(barrier, ND - 1 + 2 + NY - 1)

    pair = {}
    for n, off in ((0, 2), (2, 3), (1, 1), (3, 0)):
        t = ((x + off) % 4) * 2 + 1 - c
        pair[n] = remote(grads.at[:, rows_of(t), :], par.at[n],
                         pair_sem.at[0, n], pair_sem.at[1, n], {"dp": partner})
        pair[n].start()
        sent.append(pair[n])
    for cp in root_in + stat_in:
        cp.start()

    def stand(i, count):
        hold, which = jnp.int32(0), jnp.int32(0)
        for j in range(NB):
            hit = plan[i * NB + j] == me
            hold = jnp.where(hit, 1, hold)
            which = jnp.where(hit, j, which)
        slot_of[i] = jnp.minimum(count, NS - 1)
        source_of[NS + i] = jnp.where(hold > 0, count, -1)
        block_at[NS + i] = which
        return count + hold

    def place_slots():
        count = lax.fori_loop(0, NO, stand, jnp.int32(0))

        def place(k, _):
            src, blk = jnp.int32(0), jnp.int32(0)
            for i in range(NO):
                hit = source_of[NS + i] == k
                src = jnp.where(hit, i, src)
                blk = jnp.where(hit, block_at[NS + i], blk)
            source_of[k] = src
            block_at[k] = blk
            weight[k] = jnp.where(k < count, fresh_share, 0.0).astype(f32)
            return 0

        lax.fori_loop(0, NS, place, 0)

    def pair_sum(n, j, k):
        cols = slice(k * CH, k * CH + CH)
        return own[n, j, :, cols].astype(f32) + par[n, j, :, cols].astype(f32)

    def scale_row(scales, r):
        return jnp.sum(jnp.where(row_id == r, scales, 0.0), axis=0, keepdims=True)

    def received(u, j):
        scales = scale_of(rcv[u, NB * SR:UNIT, :])
        return widen(rcv[u, j * SR:j * SR + SR, :]) * scales[j:j + 1, :]

    def fill(out, w, value):
        sc = jnp.zeros((16, CH), f32)
        for j in range(NB):
            for kk in range(w):
                r = j * w + kk
                q, e = encode(value(j, kk))
                out[r * SR:r * SR + SR, :] = q
                sc = jnp.where(row_id == r, e, sc)
        out[NB * SR * w:NB * SR * w + 16, :] = sc.astype(i32).astype(i16)

    def ship(u, to):
        cp = remote(snd.at[u], rcv.at[u], unit_sem.at[0, u], unit_sem.at[1, u], {"dp": to})
        cp.start()
        sent.append(cp)
        return cp

    def ready(n):
        mine[n].wait()
        pair[n].wait_recv()

    class Line:
        def __init__(self, p, way, towards):
            self.p, self.way, self.towards = p, way, towards
            self.copies = {}

        def go(self, n, src, dst):
            cp = remote(src, dst, line_sem.at[self.p, self.way, 0, n],
                        line_sem.at[self.p, self.way, 1, n], {"owner": self.towards})
            cp.start()
            sent.append(cp)
            self.copies[n] = cp

        def came(self, *names):
            for n in names:
                self.copies[n].wait_recv()

    class Outward:
        def __init__(self, part):
            self.part, self.p = part, part.p
            (self.u1, self.u2, self.d1, self.d2, self.u3, self.d3, self.far,
             self.su, self.sd) = hops[part.p]
            self.ups, self.downs = Line(part.p, 0, up), Line(part.p, 1, down)

        def shelve(self, ref):
            shelf = shelves[self.p]
            for b in range(NB):
                shelf[b] = ref[b * self.part.rows:(b + 1) * self.part.rows, :]

        def find(self, src, owner):
            j = jnp.int32(0)
            for b in range(NB):
                j = jnp.where(plan[src * NB + b] == owner, b, j)
            return shelves[self.p][j]

        def hand(self, n, src, code, scales):
            part, p = self.part, self.p
            for t in range(1, NY):
                yy = (y + t) % NY
                ysend[p][n, t - 1, part.data, :] = code(yy)
                ysend[p][n, t - 1, part.tail, :] = scales(yy)
                remote(ysend[p].at[n, t - 1], got[p].at[src], y_sem.at[p, 0],
                       y_sem.at[p, 1], {"owner": z * NY + yy}).start()
            got[p][src, part.data, :] = code(y)
            got[p][src, part.tail, :] = scales(y)

        def pass_on(self, n, ref, rel):
            src = ((z + rel) % NZ) * NY + y
            self.shelve(ref)
            scales = ref[self.part.scales, :]
            self.hand(n, src, lambda yy: self.find(src, z * NY + yy), lambda yy: scales)

        def pack(self, out, ref, rel, way, first):
            rows = self.part.rows
            src = ((z + rel) % NZ) * NY + y
            self.shelve(ref)
            one, two = ((z + way) % NZ) * NY, ((z + 2 * way) % NZ) * NY
            for q in range(2):
                out[q * rows:q * rows + rows, :] = self.find(src, two + first + q)
            out[2 * rows:2 * rows + 16, :] = ref[self.part.scales, :]
            for q in range(NY):
                at = self.part.far + q * rows
                out[at:at + rows, :] = self.find(src, one + q)

        def start(self):
            front, rear = self.part.front, self.part.rear
            g = unit[self.p]
            self.ups.go(0, g.at[front], self.u1.at[front])
            self.downs.go(0, g.at[rear], self.d1.at[rear])
            self.ups.go(1, g.at[rear], self.u1.at[rear])
            self.downs.go(1, g.at[front], self.d1.at[front])
            self.pass_on(0, g, 0)

        def step(self, r):
            ups, downs = self.ups, self.downs
            front, rear = self.part.front, self.part.rear
            far, six, rows = self.part.far, self.part.six, self.part.rows
            if r == 1:
                ups.came(0)
                ups.go(2, self.u1.at[front], self.u2.at[front])
                downs.came(0)
                downs.go(2, self.d1.at[rear], self.d2.at[rear])
                ups.came(1)
                ups.go(3, self.u1.at[rear], self.u2.at[rear])
                downs.came(1)
                downs.go(3, self.d1.at[front], self.d2.at[front])
                self.pass_on(1, self.u1, 7)
                self.pass_on(2, self.d1, 1)
            elif r == 2:
                ups.came(2, 3)
                self.pack(self.su, self.u2, 6, 1, 0)
                ups.go(4, self.su.at[0:far], self.u3.at[0:far])
                ups.go(5, self.su.at[far:six], self.u3.at[far:six])
                downs.came(2, 3)
                self.pack(self.sd, self.d2, 2, NZ - 1, 2)
                downs.go(4, self.sd.at[0:far], self.d3.at[0:far])
                downs.go(5, self.sd.at[far:six], self.d3.at[far:six])
                self.pass_on(3, self.u2, 6)
                self.pass_on(4, self.d2, 2)
            else:
                ups.came(4)
                ups.go(6, self.u3.at[0:far], self.far.at[0:far])
                downs.came(4)
                downs.go(6, self.d3.at[0:far], self.far.at[far:2 * far])
                for line, ref, n, rel in ((ups, self.u3, 5, 5), (downs, self.d3, 6, 3)):
                    line.came(5)

                    def code(yy, ref=ref):
                        return ref[pl.ds(pl.multiple_of(far + yy * rows, 16), rows), :]

                    def scales(yy, ref=ref):
                        return ref[2 * rows:far, :]

                    self.hand(n, ((z + rel) % NZ) * NY + y, code, scales)

        def last(self):
            far, rows = self.part.far, self.part.rows
            self.ups.came(6)
            self.downs.came(6)

            def code(yy):
                at = (yy // 2) * far + (yy % 2) * rows
                return self.far[pl.ds(pl.multiple_of(at, 16), rows), :]

            def scales(yy):
                return self.far[pl.ds(pl.multiple_of((yy // 2) * far + 2 * rows, 16), 16), :]

            self.hand(7, ((z + 4) % NZ) * NY + y, code, scales)

        def spread(self):
            p = self.p
            whole(ysend[p], y_sem.at[p]).wait_recv()
            for t in (4, 3, 5, 2, 6, 1, 7, 0):
                for i in range(2):
                    to = (dp + t) % ND
                    k = (to + 8 * i) % NS
                    if t == 0:
                        gx[p][i, dp] = got[p][source_of[k]]
                        continue
                    xs[p][i, t] = got[p][source_of[k]]
                    remote(xs[p].at[i, t], gx[p].at[i, dp], x_sem.at[p, 0],
                           x_sem.at[p, 1], {"dp": to}).start()

        def open(self):
            part, p = self.part, self.p
            whole(xs[p].at[:, 1:ND], x_sem.at[p]).wait_recv()
            for i in range(2):
                blk = block_at[(dp + 8 * i) % NS]
                for t in range(ND):
                    scales = scale_of(gx[p][i, t, part.tail, :])
                    for kk, n in enumerate(part.chunks):
                        v = (widen(gx[p][i, t, kk * SR:kk * SR + SR, :])
                             * scale_row(scales, blk * part.w + kk))
                        hi, lo = split(v)
                        ghi[i, t * SR:t * SR + SR, n * CH:n * CH + CH] = hi
                        glo[i, t * SR:t * SR + SR, n * CH:n * CH + CH] = lo

        def project(self):
            cols = self.part.cols

            def part(m, _):
                i, rows = m // 2, rows_of(m % 2, 256)
                p = dot(lf[i, rows, :], ghi[i, :, cols]) + dot(lf[i, rows, :], glo[i, :, cols])
                hi, lo = split(p)
                phi[i, rows, cols] = hi
                plo[i, rows, cols] = lo
                return 0

            lax.fori_loop(0, 4, part, 0, unroll=True)

    class Train:
        def __init__(self, part, way, towards, refs, ascending):
            self.part, self.p, self.ascending = part, part.p, ascending
            self.near, self.far, self.later, self.one, self.zero, self.out2, self.out1 = refs
            self.line = Line(part.p, way, towards)

        def place(self, r):
            return r if self.ascending else NZ - r

        def four(self):
            some = slice(0, 2) if self.ascending else slice(2, 4)
            self.line.go(0, ybuf[self.p][4].at[some], self.far)

        def three(self):
            self.line.go(1, ybuf[self.p][self.place(3)], self.near)

        def three_far(self):
            self.line.came(0)
            self.line.go(2, self.far, self.later)

        def code(self, r, j, part_rows, old):
            src = ((z + self.place(r)) % NZ) * NY + y
            o = plan[src * NB + j]
            oz, oy = lax.shift_right_logical(o, 2), lax.bitwise_and(o, NY - 1)
            new = ybuf[self.p][self.place(r)][oy][part_rows, :].astype(i32)
            if r == 2:
                before = (z + (NZ - 1 if self.ascending else 1)) % NZ
                near = self.near[oy][part_rows, :].astype(i32)
                far = self.later[lax.bitwise_and(o, 1)][part_rows, :].astype(i32)
                at = jnp.full(near.shape, (oz == before).astype(i32), i32)
                old = jnp.where(at > 0, near, far)
            at = jnp.full(new.shape, (oz == z).astype(i32), i32)
            return jnp.where(at > 0, new, old)

        def blocks(self, r, first, last, out, came):
            part = self.part
            for j in range(first, last):
                rows = slice(j * part.rows, (j + 1) * part.rows)
                old = None if r == 2 else came[rows, :].astype(i32)
                out[rows, :] = self.code(r, j, part.data, old).astype(i16)

        def scales(self, r, out, came):
            part = self.part
            tile = jnp.zeros((16, CH), i32) if r == 2 else came[part.scales, :].astype(i32)
            for j in range(NB):
                new = self.code(r, j, part.tail, tile)
                tile = jnp.where(row_id // part.w == j, new, tile)
            out[part.scales, :] = tile.astype(i16)

        def two(self):
            part = self.part
            self.line.came(1, 2)
            self.blocks(2, 0, 4, self.out2, None)
            self.line.go(3, self.out2.at[part.front], self.one.at[part.front])
            self.blocks(2, 4, NB, self.out2, None)
            self.scales(2, self.out2, None)
            self.line.go(4, self.out2.at[part.rear], self.one.at[part.rear])

        def last(self):
            part = self.part
            self.line.came(3)
            self.blocks(1, 0, 4, self.out1, self.one)
            self.line.go(5, self.out1.at[part.front], self.zero.at[part.front])
            self.line.came(4)
            self.blocks(1, 4, NB, self.out1, self.one)
            self.scales(1, self.out1, self.one)
            self.line.go(6, self.out1.at[part.rear], self.zero.at[part.rear])

        def arrived(self):
            self.line.came(5, 6)

    class Inward:
        def __init__(self, part):
            self.part, self.p = part, part.p
            self.ups = Train(part, 2, up, ur[part.p], True)
            self.downs = Train(part, 3, down, dr[part.p], False)

        def multiply(self, i):
            part, p = self.part, self.p

            def pairs(m, _):
                b = (x + 2 + m) % 4
                rows = rows_of(b, 128)
                r = dot(jnp.concatenate((phi[i, rows, :], plo[i, rows, :]), axis=0),
                        rf[i, :, part.cols])
                u = r[:128] + r[128:]
                for cc in range(2):
                    sc = jnp.zeros((16, CH), f32)
                    for kk in range(part.w):
                        q, e = encode(u[cc * SR:cc * SR + SR, kk * CH:kk * CH + CH])
                        xu[p][i, b * 2 + cc, kk * SR:kk * SR + SR, :] = q
                        sc = jnp.where(row_id % part.w == kk, e, sc)
                    xu[p][i, b * 2 + cc, part.tail, :] = sc.astype(i32).astype(i16)
                return 0

            lax.fori_loop(0, 4, pairs, 0, unroll=True)

        def hand_out(self, i):
            p = self.p
            ux[p][dp + 8 * i] = xu[p][i, dp]
            for t in (4, 3, 5, 2, 6, 1, 7):
                to = (dp + t) % ND
                remote(xu[p].at[i, to], ux[p].at[dp + 8 * i], x_sem.at[NP + p, 0],
                       x_sem.at[NP + p, 1], {"dp": to}).start()

        def arrive(self):
            whole(xu[self.p].at[:, 1:ND], x_sem.at[NP + self.p]).wait_recv()

        def across(self, n):
            p = self.p
            d = (z + n) % NZ
            for t in range(1, NY):
                yy = (y + t) % NY
                yback[p][n, t - 1] = ux[p][slot_of[d * NY + yy]]
                remote(yback[p].at[n, t - 1], ybuf[p][n].at[y], back_sem.at[p, n, 0],
                       back_sem.at[p, n, 1], {"owner": z * NY + yy}).start()
            ybuf[p][n][y] = ux[p][slot_of[d * NY + y]]

        def crossed(self, n):
            whole(yback[self.p].at[n], back_sem.at[self.p, n]).wait_recv()

        def begin(self):
            self.across(4)
            self.across(3)
            self.across(5)

        def one(self):
            self.crossed(4)
            self.ups.four()
            self.downs.four()
            self.crossed(3)
            self.ups.three()
            self.crossed(5)
            self.downs.three()
            self.across(2)
            self.across(6)

        def two(self):
            self.ups.three_far()
            self.downs.three_far()
            self.across(1)
            self.across(7)

        def three(self):
            self.crossed(2)
            self.ups.two()
            self.crossed(6)
            self.downs.two()
            self.across(0)

        def four(self):
            self.crossed(1)
            self.ups.last()
            self.crossed(7)
            self.downs.last()

        def finish(self):
            part, p = self.part, self.p
            self.crossed(0)
            self.ups.arrived()
            self.downs.arrived()
            for j in range(NB):
                o = plan[me * NB + j]
                near = ybuf[p][0][lax.bitwise_and(o, NY - 1)].astype(i32)
                off = lax.bitwise_and(lax.shift_right_logical(o, 2) + NZ - z, NZ - 1)
                above = jnp.where(off < 4, 1, jnp.where(
                    off == 4, lax.shift_right_logical(lax.bitwise_and(o, NY - 1), 1), 0))
                local = (off == 0).astype(i32)
                rows = slice(j * part.rows, (j + 1) * part.rows)
                full = jnp.zeros((part.rows, CH), i32)
                code = jnp.where(full + above > 0, dr[p][4][rows, :].astype(i32),
                                 ur[p][4][rows, :].astype(i32))
                code = jnp.where(full + local > 0, near[part.data, :], code)
                tile = jnp.where(row_id * 0 + above > 0, dr[p][4][part.scales, :].astype(i32),
                                 ur[p][4][part.scales, :].astype(i32))
                tile = jnp.where(row_id * 0 + local > 0, near[part.tail, :], tile)
                tile = scale_of(tile)
                for kk, n in enumerate(part.chunks):
                    r = j * part.w + kk
                    update[j, :, n * CH:n * CH + CH] = (
                        code[kk * SR:kk * SR + SR].astype(f32) * tile[r:r + 1, :])

    def stat(which, i):
        def block(m, _):
            b = (x + 1 + m) % 4
            if which == 0:
                ohi, olo = ghi[i, rows_of(b, 128), :], glo[i, rows_of(b, 128), :]
                f = dot(jnp.concatenate((ohi, olo), axis=0), ghi[i], ((1,), (1,)))
                f = f[:128] + f[128:] + dot(ohi, glo[i], ((1,), (1,)))
            else:
                chi, clo = ghi[i, :, rows_of(b, 128)], glo[i, :, rows_of(b, 128)]
                f = (dot(chi, ghi[i], ((0,), (0,))) + dot(clo, ghi[i], ((0,), (0,)))
                     + dot(chi, glo[i], ((0,), (0,))))
            for cc in range(2):
                sc = jnp.zeros((16, CH), f32)
                for n in range(4):
                    q, e = encode(f[cc * SR:cc * SR + SR, n * CH:n * CH + CH])
                    sx[which][i, b * 2 + cc, n * SR:n * SR + SR, :] = q
                    sc = jnp.where(row_id == n, e, sc)
                sx[which][i, b * 2 + cc, 256:SLOT, :] = sc.astype(i32).astype(i16)
            return 0

        lax.fori_loop(0, 4, block, 0, unroll=2)
        sr[which][dp + 8 * i] = sx[which][i, dp]
        for t in (4, 3, 5, 2, 6, 1, 7):
            to = (dp + t) % ND
            remote(sx[which].at[i, to], sr[which].at[dp + 8 * i], x_sem.at[2 * NP + which, 0],
                   x_sem.at[2 * NP + which, 1], {"dp": to}).start()

    def renew(which, held, out):
        whole(sx[which].at[:, 1:ND], x_sem.at[2 * NP + which]).wait_recv()

        def slot(k, _):
            w = weight[k]
            scales = scale_of(sr[which][k, 256:SLOT, :])
            for n in range(4):
                cols = slice(n * CH, n * CH + CH)
                term = widen(sr[which][k, n * SR:n * SR + SR, :]) * scales[n:n + 1, :]
                held[k, :, cols] = stat_decay * held[k, :, cols] + w * term
            pltpu.make_async_copy(held.at[k], out.at[k], out_sem.at[which]).start()
            return 0

        lax.fori_loop(0, NS, slot, 0)

    out0, out1, out2 = (Outward(part) for part in PARTS)
    in0, in1, in2 = (Inward(part) for part in PARTS)
    right_far, left_far, right_straight, left_straight, right_both, left_both = {}, {}, {}, {}, {}, {}

    def far(k):
        fill(snd.at[k], 1, lambda j, kk: pair_sum(0, j, k))
        if k < 2:
            right_far[k] = ship(k, right)
        else:
            left_far[k] = ship(k, left)

    def straight(k):
        if k >= 2:
            fill(snd.at[4 + k], 1, lambda j, kk: pair_sum(1, j, k))
            right_straight[k] = ship(4 + k, right)
        else:
            fill(snd.at[4 + k], 1, lambda j, kk: pair_sum(2, j, k))
            left_straight[k] = ship(4 + k, left)

    def both(k):
        if k < 2:
            right_far[k].wait_recv()
            fill(snd.at[8 + k], 1, lambda j, kk: pair_sum(1, j, k) + received(k, j))
            right_both[k] = ship(8 + k, right)
        else:
            left_far[k].wait_recv()
            fill(snd.at[8 + k], 1, lambda j, kk: pair_sum(2, j, k) + received(k, j))
            left_both[k] = ship(8 + k, left)

    def total(part):
        for k in part.chunks:
            for cps in (right_straight, left_straight, right_both, left_both):
                if k in cps:
                    cps[k].wait_recv()
        fill(unit[part.p], part.w, lambda j, kk: (
            pair_sum(3, j, part.chunks[kk]) + received(4 + part.chunks[kk], j)
            + received(8 + part.chunks[kk], j)))

    ready(0)
    far(0)
    far(1)
    ready(2)
    straight(0)
    far(2)
    far(3)
    ready(1)
    both(0)
    straight(1)
    both(1)
    straight(2)
    straight(3)
    ready(3)
    total(PARTS[0])
    out0.start()
    both(2)
    both(3)
    out0.step(1)
    total(PARTS[1])
    out1.start()
    out0.step(2)
    total(PARTS[2])
    for which, (src, dst) in enumerate(((left_root, lf), (right_root, rf))):
        for i in range(2):
            for t in range(1, ND):
                to = (dp + t) % ND
                remote(src.at[(to + 8 * i) % NS], dst.at[i, rows_of(dp)],
                       x_sem.at[2 * NP + 2 + which, 0],
                       x_sem.at[2 * NP + 2 + which, 1], {"dp": to}).start()
    out0.step(3)
    out1.step(1)
    place_slots()
    out0.last()
    out1.step(2)
    out0.spread()
    out1.step(3)
    out2.start()
    out0.open()
    out1.last()
    out2.step(1)
    out1.spread()
    out2.step(2)
    for cp in root_in:
        cp.wait()
    whole(lf.at[:, 0:7 * SR], x_sem.at[2 * NP + 2]).wait_recv()
    whole(rf.at[:, 0:7 * SR], x_sem.at[2 * NP + 3]).wait_recv()
    out0.project()
    out2.step(3)
    out1.open()
    out1.project()
    out2.last()
    out2.spread()
    out2.open()
    out2.project()
    in0.multiply(0)
    in0.hand_out(0)
    in0.multiply(1)
    in0.hand_out(1)
    in1.multiply(0)
    in1.multiply(1)
    in0.arrive()
    in0.begin()
    in1.hand_out(0)
    in1.hand_out(1)
    in0.one()
    in2.multiply(0)
    in2.multiply(1)
    in0.two()
    in1.arrive()
    in1.begin()
    in2.hand_out(0)
    in2.hand_out(1)
    in1.one()
    in0.three()
    stat(0, 0)
    in0.four()
    in1.two()
    stat(1, 0)
    in2.arrive()
    in2.begin()
    in1.three()
    in2.one()
    stat(0, 1)
    in1.four()
    in0.finish()
    in2.two()
    stat(1, 1)
    in2.three()
    for cp in stat_in:
        cp.wait()
    in1.finish()
    in2.four()
    renew(0, ls, left_new)
    renew(1, rs, right_new)
    in2.finish()

    pltpu.make_async_copy(ls, left_new, out_sem.at[0]).wait()
    pltpu.make_async_copy(rs, right_new, out_sem.at[1]).wait()
    for cp in sent + group:
        cp.wait_send()


def shampoo(plan, grads, left_stat, right_stat, left_root, right_root):
    hbm = pl.BlockSpec(memory_space=pl.ANY)
    vmem = pltpu.VMEM

    def each(lead, rows, times=1):
        return [vmem((*lead, rows(part), CH), i16) for part in PARTS for _ in range(times)]

    def unit(part):
        return part.unit

    def message(part):
        return part.message

    train = [vmem(shape, i16) for part in PARTS for shape in (
        (NY, part.message, CH), (2, part.message, CH), (2, part.message, CH),
        *[(part.unit, CH)] * 4)]

    return pl.pallas_call(
        shampoo_kernel,
        out_shape=(
            jax.ShapeDtypeStruct((NS, SR, BO), f32),
            jax.ShapeDtypeStruct((NS, SR, BO), f32),
            jax.ShapeDtypeStruct((NB, SR, BO), f32),
        ),
        in_specs=[pl.BlockSpec(memory_space=pltpu.SMEM), hbm, hbm, hbm, hbm, hbm],
        out_specs=(hbm, hbm, pl.BlockSpec(memory_space=vmem)),
        scratch_shapes=[
            pltpu.SMEM((NO,), i32),
            pltpu.SMEM((NS + NO,), i32),
            pltpu.SMEM((NS + NO,), i32),
            pltpu.SMEM((NS,), f32),
            vmem((4, NB, SR, BO), bf16),
            vmem((4, NB, SR, BO), bf16),
            vmem((12, UNIT, CH), i16),
            vmem((12, UNIT, CH), i16),
            *each((), unit),
            *[vmem((rows, CH), i16) for part in PARTS for rows in (
                *[part.unit] * 4, part.six, part.six, 2 * part.far, part.six, part.six)],
            *each((NZ, NY - 1), message),
            *each((NO,), message),
            *each((2, ND), message),
            *each((2, ND), message),
            *[vmem((2, BO, BO), bf16)] * 6,
            *each((2, ND), message),
            *each((2 * ND,), message),
            *each((NY,), message, NZ),
            *each((NZ, NY - 1), message),
            *train,
            *train,
            *[vmem((2, ND, SLOT, CH), i16)] * 2,
            *[vmem((2 * ND, SLOT, CH), i16)] * 2,
            vmem((NS, SR, BO), f32),
            vmem((NS, SR, BO), f32),
            *[vmem((NB, part.rows, CH), i16) for part in PARTS],
            pltpu.SemaphoreType.DMA((2, 4)),
            pltpu.SemaphoreType.DMA((10,)),
            pltpu.SemaphoreType.DMA((2, 12)),
            pltpu.SemaphoreType.DMA((NP, 4, 2, 7)),
            pltpu.SemaphoreType.DMA((NP, 2)),
            pltpu.SemaphoreType.DMA((NP, NZ, 2)),
            pltpu.SemaphoreType.DMA((2 * NP + 4, 2)),
            pltpu.SemaphoreType.DMA((2,)),
        ],
        compiler_params=pltpu.CompilerParams(
            collective_id=0, has_side_effects=True, vmem_limit_bytes=LIMIT),
        name="shampoo",
    )(plan, grads, left_stat, right_stat, left_root, right_root)


def local(grads, plan, left_stat, right_stat, left_root, right_root):
    left_new, right_new, update = shampoo(
        plan, grads[0], left_stat[0], right_stat[0], left_root[0], right_root[0])
    return left_new[None], right_new[None], update


def solution(mesh):
    return jax.shard_map(
        local,
        mesh=mesh,
        in_specs=(
            P("dp", "owner", None, None),
            P(),
            P("owner", None, "dp", None),
            P("owner", None, "dp", None),
            P("owner", None, "dp", None),
            P("owner", None, "dp", None),
        ),
        out_specs=(
            P("owner", None, "dp", None),
            P("owner", None, "dp", None),
            P("owner", "dp", None),
        ),
        check_vma=False,
    )
```

```python
import functools

import jax
import jax.numpy as jnp
from jax import lax
from jax.experimental import pallas as pl
from jax.experimental.pallas import tpu as pltpu
from jax.sharding import PartitionSpec as P

MESH = pl.DeviceIdType.MESH
f32 = jnp.float32
bf16 = jnp.bfloat16
i16 = jnp.int16
i32 = jnp.int32

stat_decay = 0.95
fresh_share = 0.05

NB = 7
NO = 32
NS = 13
ND = 8
SR = 64
BO = 512
CH = 128
NY = 4
NZ = 8
SLOT = 272
UNIT = 464
LIMIT = 60 * 1024 * 1024


def encode(x):
    m = jnp.maximum(jnp.max(jnp.abs(x), axis=0, keepdims=True), 2.0 ** -100)
    e = jnp.floor(jnp.log2(m) * 256.0) + 1.0
    q = jnp.round(x * (32700.0 * jnp.exp2(e * (-1.0 / 256.0))))
    return q.astype(i32).astype(i16), e


def scale_of(e16):
    return jnp.exp2(e16.astype(i32).astype(f32) * (1.0 / 256.0)) * (1.0 / 32700.0)


def widen(q):
    return q.astype(i32).astype(f32)


def remote(src, dst, send, recv, where):
    return pltpu.make_async_remote_copy(
        src_ref=src, dst_ref=dst, send_sem=send, recv_sem=recv,
        device_id=where, device_id_type=MESH)


def dot(a, b, dims=((1,), (0,))):
    return lax.dot_general(a, b, (dims, ((), ())), preferred_element_type=f32)


class Part:
    def __init__(self, p, chunks):
        w = len(chunks)
        self.p, self.chunks, self.w = p, chunks, w
        self.cols = slice(chunks[0] * CH, (chunks[-1] + 1) * CH)
        self.rows = SR * w
        self.unit = NB * SR * w + 16
        self.message = SR * w + 16
        self.front = slice(0, 4 * SR * w)
        self.rear = slice(4 * SR * w, self.unit)
        self.back = slice(4 * SR * w, NB * SR * w)
        self.scales = slice(NB * SR * w, self.unit)
        self.data = slice(0, SR * w)
        self.tail = slice(SR * w, self.message)
        self.far = 2 * SR * w + 16
        self.six = 6 * SR * w + 16


PARTS = (Part(0, (0, 1)), Part(1, (2, 3)))
NP = len(PARTS)


def split(v):
    hi = v.astype(bf16)
    return hi, (v - hi.astype(f32)).astype(bf16)


def rows_of(t, n=SR):
    return pl.ds(pl.multiple_of(t * n, n), n)


def shampoo_kernel(plan, grads, left_stat, right_stat, left_root, right_root,
                   left_new, right_new, update, *scratch):
    it = iter(scratch)
    slot_of, source_of, block_at, weight = (next(it) for _ in range(4))
    own, par, snd, rcv = (next(it) for _ in range(4))
    unit = [next(it) for _ in PARTS]
    hops = [[next(it) for _ in range(9)] for _ in PARTS]
    ysend, got, xs, gx = ([next(it) for _ in PARTS] for _ in range(4))
    lf, rf, ghi, glo, phi, plo = (next(it) for _ in range(6))
    xu, ux = ([next(it) for _ in PARTS] for _ in range(2))
    ybuf = [[next(it) for _ in range(8)] for _ in PARTS]
    yback = [next(it) for _ in PARTS]
    ur = [[next(it) for _ in range(7)] for _ in PARTS]
    dr = [[next(it) for _ in range(7)] for _ in PARTS]
    sx, sr = ([next(it) for _ in range(2)] for _ in range(2))
    ls, rs = next(it), next(it)
    shelves = [next(it) for _ in PARTS]
    pair_sem, load_sem, unit_sem, line_sem, y_sem, back_sem, x_sem, out_sem = (
        next(it) for _ in range(8))

    me = lax.axis_index("owner")
    z, y = me // NY, me % NY
    up, down = ((z + 1) % NZ) * NY + y, ((z + NZ - 1) % NZ) * NY + y
    dp = lax.axis_index("dp")
    x, c = dp // 2, dp % 2
    partner = x * 2 + 1 - c
    right = ((x + 1) % 4) * 2 + c
    left = ((x + 3) % 4) * 2 + c
    row_id = lax.broadcasted_iota(i32, (16, CH), 0)
    sent = []
    group = []

    def whole(ref, sems):
        cp = remote(ref, ref, sems.at[0], sems.at[1], {"dp": partner})
        group.append(cp)
        return cp

    mine = {}
    for n, off in ((0, 2), (2, 3), (1, 1), (3, 0)):
        t = ((x + off) % 4) * 2 + c
        mine[n] = pltpu.make_async_copy(grads.at[:, rows_of(t), :], own.at[n], load_sem.at[n])
        mine[n].start()
    stat_in = [pltpu.make_async_copy(left_stat, ls, load_sem.at[4]),
               pltpu.make_async_copy(right_stat, rs, load_sem.at[5])]
    root_in = []
    for i in range(2):
        k = (dp + 8 * i) % NS
        root_in.append(pltpu.make_async_copy(
            left_root.at[k], lf.at[i, rows_of(dp)], load_sem.at[6 + i]))
        root_in.append(pltpu.make_async_copy(
            right_root.at[k], rf.at[i, rows_of(dp)], load_sem.at[8 + i]))

    barrier = pltpu.get_barrier_semaphore()
    for t in range(1, ND):
        pl.semaphore_signal(
            barrier, inc=1, device_id={"dp": (dp + t) % ND}, device_id_type=MESH)
    for place in [up, down] + [z * NY + (y + t) % NY for t in range(1, NY)]:
        pl.semaphore_signal(barrier, inc=1, device_id={"owner": place}, device_id_type=MESH)
    pl.semaphore_wait(barrier, ND - 1 + 2 + NY - 1)

    pair = {}
    for n, off in ((0, 2), (2, 3), (1, 1), (3, 0)):
        t = ((x + off) % 4) * 2 + 1 - c
        pair[n] = remote(grads.at[:, rows_of(t), :], par.at[n],
                         pair_sem.at[0, n], pair_sem.at[1, n], {"dp": partner})
        sent.append(pair[n])
    pair[0].start()

    def stand(i, count):
        hold, which = jnp.int32(0), jnp.int32(0)
        for j in range(NB):
            hit = plan[i * NB + j] == me
            hold = jnp.where(hit, 1, hold)
            which = jnp.where(hit, j, which)
        slot_of[i] = jnp.minimum(count, NS - 1)
        source_of[NS + i] = jnp.where(hold > 0, count, -1)
        block_at[NS + i] = which
        return count + hold

    def place_slots():
        count = lax.fori_loop(0, NO, stand, jnp.int32(0))

        def place(k, _):
            src, blk = jnp.int32(0), jnp.int32(0)
            for i in range(NO):
                hit = source_of[NS + i] == k
                src = jnp.where(hit, i, src)
                blk = jnp.where(hit, block_at[NS + i], blk)
            source_of[k] = src
            block_at[k] = blk
            weight[k] = jnp.where(k < count, fresh_share, 0.0).astype(f32)
            return 0

        lax.fori_loop(0, NS, place, 0)

    def pair_sum(n, j, k):
        cols = slice(k * CH, k * CH + CH)
        return own[n, j, :, cols].astype(f32) + par[n, j, :, cols].astype(f32)

    def scale_row(scales, r):
        return jnp.sum(jnp.where(row_id == r, scales, 0.0), axis=0, keepdims=True)

    def received(u, j):
        scales = scale_of(rcv[u, NB * SR:UNIT, :])
        return widen(rcv[u, j * SR:j * SR + SR, :]) * scales[j:j + 1, :]

    def fill(out, w, value):
        sc = jnp.zeros((16, CH), f32)
        for j in range(NB):
            for kk in range(w):
                r = j * w + kk
                q, e = encode(value(j, kk))
                out[r * SR:r * SR + SR, :] = q
                sc = jnp.where(row_id == r, e, sc)
        out[NB * SR * w:NB * SR * w + 16, :] = sc.astype(i32).astype(i16)

    def ship(u, to):
        cp = remote(snd.at[u], rcv.at[u], unit_sem.at[0, u], unit_sem.at[1, u], {"dp": to})
        cp.start()
        sent.append(cp)
        return cp

    def ready(n):
        mine[n].wait()
        pair[n].wait_recv()

    class Line:
        def __init__(self, p, way, towards):
            self.p, self.way, self.towards = p, way, towards
            self.copies = {}

        def go(self, n, src, dst):
            cp = remote(src, dst, line_sem.at[self.p, self.way, 0, n],
                        line_sem.at[self.p, self.way, 1, n], {"owner": self.towards})
            cp.start()
            sent.append(cp)
            self.copies[n] = cp

        def came(self, *names):
            for n in names:
                self.copies[n].wait_recv()

    class Outward:
        def __init__(self, part):
            self.part, self.p = part, part.p
            (self.u1, self.u2, self.d1, self.d2, self.u3, self.d3, self.far,
             self.su, self.sd) = hops[part.p]
            self.ups, self.downs = Line(part.p, 0, up), Line(part.p, 1, down)

        def shelve(self, ref):
            shelf = shelves[self.p]
            for b in range(NB):
                shelf[b] = ref[b * self.part.rows:(b + 1) * self.part.rows, :]

        def find(self, src, owner):
            j = jnp.int32(0)
            for b in range(NB):
                j = jnp.where(plan[src * NB + b] == owner, b, j)
            return shelves[self.p][j]

        def hand(self, n, src, code, scales):
            part, p = self.part, self.p
            for t in range(1, NY):
                yy = (y + t) % NY
                ysend[p][n, t - 1, part.data, :] = code(yy)
                ysend[p][n, t - 1, part.tail, :] = scales(yy)
                remote(ysend[p].at[n, t - 1], got[p].at[src], y_sem.at[p, 0],
                       y_sem.at[p, 1], {"owner": z * NY + yy}).start()
            got[p][src, part.data, :] = code(y)
            got[p][src, part.tail, :] = scales(y)

        def pass_on(self, n, ref, rel):
            src = ((z + rel) % NZ) * NY + y
            self.shelve(ref)
            scales = ref[self.part.scales, :]
            self.hand(n, src, lambda yy: self.find(src, z * NY + yy), lambda yy: scales)

        def pack(self, out, ref, rel, way, first):
            rows = self.part.rows
            src = ((z + rel) % NZ) * NY + y
            self.shelve(ref)
            one, two = ((z + way) % NZ) * NY, ((z + 2 * way) % NZ) * NY
            for q in range(2):
                out[q * rows:q * rows + rows, :] = self.find(src, two + first + q)
            out[2 * rows:2 * rows + 16, :] = ref[self.part.scales, :]
            for q in range(NY):
                at = self.part.far + q * rows
                out[at:at + rows, :] = self.find(src, one + q)

        def start(self):
            front, rear = self.part.front, self.part.rear
            g = unit[self.p]
            self.ups.go(0, g.at[front], self.u1.at[front])
            self.downs.go(0, g.at[rear], self.d1.at[rear])
            self.ups.go(1, g.at[rear], self.u1.at[rear])
            self.downs.go(1, g.at[front], self.d1.at[front])
            self.pass_on(0, g, 0)

        def step(self, r):
            ups, downs = self.ups, self.downs
            front, rear = self.part.front, self.part.rear
            far, six, rows = self.part.far, self.part.six, self.part.rows
            if r == 1:
                ups.came(0)
                ups.go(2, self.u1.at[front], self.u2.at[front])
                downs.came(0)
                downs.go(2, self.d1.at[rear], self.d2.at[rear])
                ups.came(1)
                ups.go(3, self.u1.at[rear], self.u2.at[rear])
                downs.came(1)
                downs.go(3, self.d1.at[front], self.d2.at[front])
                self.pass_on(1, self.u1, 7)
                self.pass_on(2, self.d1, 1)
            elif r == 2:
                ups.came(2, 3)
                self.pack(self.su, self.u2, 6, 1, 0)
                ups.go(4, self.su.at[0:far], self.u3.at[0:far])
                ups.go(5, self.su.at[far:six], self.u3.at[far:six])
                downs.came(2, 3)
                self.pack(self.sd, self.d2, 2, NZ - 1, 2)
                downs.go(4, self.sd.at[0:far], self.d3.at[0:far])
                downs.go(5, self.sd.at[far:six], self.d3.at[far:six])
                self.pass_on(3, self.u2, 6)
                self.pass_on(4, self.d2, 2)
            else:
                ups.came(4)
                ups.go(6, self.u3.at[0:far], self.far.at[0:far])
                downs.came(4)
                downs.go(6, self.d3.at[0:far], self.far.at[far:2 * far])
                for line, ref, n, rel in ((ups, self.u3, 5, 5), (downs, self.d3, 6, 3)):
                    line.came(5)

                    def code(yy, ref=ref):
                        return ref[pl.ds(pl.multiple_of(far + yy * rows, 16), rows), :]

                    def scales(yy, ref=ref):
                        return ref[2 * rows:far, :]

                    self.hand(n, ((z + rel) % NZ) * NY + y, code, scales)

        def last(self):
            far, rows = self.part.far, self.part.rows
            self.ups.came(6)
            self.downs.came(6)

            def code(yy):
                at = (yy // 2) * far + (yy % 2) * rows
                return self.far[pl.ds(pl.multiple_of(at, 16), rows), :]

            def scales(yy):
                return self.far[pl.ds(pl.multiple_of((yy // 2) * far + 2 * rows, 16), 16), :]

            self.hand(7, ((z + 4) % NZ) * NY + y, code, scales)

        def spread(self):
            p = self.p
            whole(ysend[p], y_sem.at[p]).wait_recv()
            for t in (4, 3, 5, 2, 6, 1, 7, 0):
                for i in range(2):
                    to = (dp + t) % ND
                    k = (to + 8 * i) % NS
                    if t == 0:
                        gx[p][i, dp] = got[p][source_of[k]]
                        continue
                    xs[p][i, t] = got[p][source_of[k]]
                    remote(xs[p].at[i, t], gx[p].at[i, dp], x_sem.at[p, 0],
                           x_sem.at[p, 1], {"dp": to}).start()

        def open(self):
            part, p = self.part, self.p
            whole(xs[p].at[:, 1:ND], x_sem.at[p]).wait_recv()
            for i in range(2):
                blk = block_at[(dp + 8 * i) % NS]
                for t in range(ND):
                    scales = scale_of(gx[p][i, t, part.tail, :])
                    for kk, n in enumerate(part.chunks):
                        v = (widen(gx[p][i, t, kk * SR:kk * SR + SR, :])
                             * scale_row(scales, blk * part.w + kk))
                        hi, lo = split(v)
                        ghi[i, t * SR:t * SR + SR, n * CH:n * CH + CH] = hi
                        glo[i, t * SR:t * SR + SR, n * CH:n * CH + CH] = lo

        def project(self):
            cols = self.part.cols

            def part(m, _):
                i, rows = m // 2, rows_of(m % 2, 256)
                p = dot(lf[i, rows, :], ghi[i, :, cols]) + dot(lf[i, rows, :], glo[i, :, cols])
                hi, lo = split(p)
                phi[i, rows, cols] = hi
                plo[i, rows, cols] = lo
                return 0

            lax.fori_loop(0, 4, part, 0, unroll=True)

    class Train:
        def __init__(self, part, way, towards, refs, ascending):
            self.part, self.p, self.ascending = part, part.p, ascending
            self.near, self.far, self.later, self.one, self.zero, self.out2, self.out1 = refs
            self.line = Line(part.p, way, towards)

        def place(self, r):
            return r if self.ascending else NZ - r

        def four(self):
            some = slice(0, 2) if self.ascending else slice(2, 4)
            self.line.go(0, ybuf[self.p][4].at[some], self.far)

        def three(self):
            self.line.go(1, ybuf[self.p][self.place(3)], self.near)

        def three_far(self):
            self.line.came(0)
            self.line.go(2, self.far, self.later)

        def code(self, r, j, part_rows, old):
            src = ((z + self.place(r)) % NZ) * NY + y
            o = plan[src * NB + j]
            oz, oy = lax.shift_right_logical(o, 2), lax.bitwise_and(o, NY - 1)
            new = ybuf[self.p][self.place(r)][oy][part_rows, :].astype(i32)
            if r == 2:
                before = (z + (NZ - 1 if self.ascending else 1)) % NZ
                near = self.near[oy][part_rows, :].astype(i32)
                far = self.later[lax.bitwise_and(o, 1)][part_rows, :].astype(i32)
                at = jnp.full(near.shape, (oz == before).astype(i32), i32)
                old = jnp.where(at > 0, near, far)
            at = jnp.full(new.shape, (oz == z).astype(i32), i32)
            return jnp.where(at > 0, new, old)

        def blocks(self, r, first, last, out, came):
            part = self.part
            for j in range(first, last):
                rows = slice(j * part.rows, (j + 1) * part.rows)
                old = None if r == 2 else came[rows, :].astype(i32)
                out[rows, :] = self.code(r, j, part.data, old).astype(i16)

        def scales(self, r, out, came):
            part = self.part
            tile = jnp.zeros((16, CH), i32) if r == 2 else came[part.scales, :].astype(i32)
            for j in range(NB):
                new = self.code(r, j, part.tail, tile)
                tile = jnp.where(row_id // part.w == j, new, tile)
            out[part.scales, :] = tile.astype(i16)

        def two(self):
            part = self.part
            self.line.came(1, 2)
            self.blocks(2, 0, 4, self.out2, None)
            self.line.go(3, self.out2.at[part.front], self.one.at[part.front])
            self.blocks(2, 4, NB, self.out2, None)
            self.scales(2, self.out2, None)
            self.line.go(4, self.out2.at[part.rear], self.one.at[part.rear])

        def last(self):
            part = self.part
            self.line.came(3)
            self.blocks(1, 0, 4, self.out1, self.one)
            self.line.go(5, self.out1.at[part.front], self.zero.at[part.front])
            self.line.came(4)
            self.blocks(1, 4, NB, self.out1, self.one)
            self.scales(1, self.out1, self.one)
            self.line.go(6, self.out1.at[part.rear], self.zero.at[part.rear])

        def arrived(self):
            self.line.came(5, 6)

    class Inward:
        def __init__(self, part):
            self.part, self.p = part, part.p
            self.ups = Train(part, 2, up, ur[part.p], True)
            self.downs = Train(part, 3, down, dr[part.p], False)

        def multiply(self, i):
            part, p = self.part, self.p

            def pairs(m, _):
                b = (x + 2 + m) % 4
                rows = rows_of(b, 128)
                r = dot(jnp.concatenate((phi[i, rows, :], plo[i, rows, :]), axis=0),
                        rf[i, :, part.cols])
                u = r[:128] + r[128:]
                for cc in range(2):
                    sc = jnp.zeros((16, CH), f32)
                    for kk in range(part.w):
                        q, e = encode(u[cc * SR:cc * SR + SR, kk * CH:kk * CH + CH])
                        xu[p][i, b * 2 + cc, kk * SR:kk * SR + SR, :] = q
                        sc = jnp.where(row_id % part.w == kk, e, sc)
                    xu[p][i, b * 2 + cc, part.tail, :] = sc.astype(i32).astype(i16)
                return 0

            lax.fori_loop(0, 4, pairs, 0, unroll=True)

        def hand_out(self, i):
            p = self.p
            ux[p][dp + 8 * i] = xu[p][i, dp]
            for t in (4, 3, 5, 2, 6, 1, 7):
                to = (dp + t) % ND
                remote(xu[p].at[i, to], ux[p].at[dp + 8 * i], x_sem.at[NP + p, 0],
                       x_sem.at[NP + p, 1], {"dp": to}).start()

        def arrive(self):
            whole(xu[self.p].at[:, 1:ND], x_sem.at[NP + self.p]).wait_recv()

        def across(self, n):
            p = self.p
            d = (z + n) % NZ
            for t in range(1, NY):
                yy = (y + t) % NY
                yback[p][n, t - 1] = ux[p][slot_of[d * NY + yy]]
                remote(yback[p].at[n, t - 1], ybuf[p][n].at[y], back_sem.at[p, n, 0],
                       back_sem.at[p, n, 1], {"owner": z * NY + yy}).start()
            ybuf[p][n][y] = ux[p][slot_of[d * NY + y]]

        def crossed(self, n):
            whole(yback[self.p].at[n], back_sem.at[self.p, n]).wait_recv()

        def begin(self):
            self.across(4)
            self.across(3)
            self.across(5)

        def one(self):
            self.crossed(4)
            self.ups.four()
            self.downs.four()
            self.crossed(3)
            self.ups.three()
            self.crossed(5)
            self.downs.three()
            self.across(2)
            self.across(6)

        def two(self):
            self.ups.three_far()
            self.downs.three_far()
            self.across(1)
            self.across(7)

        def three(self):
            self.crossed(2)
            self.ups.two()
            self.crossed(6)
            self.downs.two()
            self.across(0)

        def four(self):
            self.crossed(1)
            self.ups.last()
            self.crossed(7)
            self.downs.last()

        def finish(self):
            part, p = self.part, self.p
            self.crossed(0)
            self.ups.arrived()
            self.downs.arrived()
            for j in range(NB):
                o = plan[me * NB + j]
                near = ybuf[p][0][lax.bitwise_and(o, NY - 1)].astype(i32)
                off = lax.bitwise_and(lax.shift_right_logical(o, 2) + NZ - z, NZ - 1)
                above = jnp.where(off < 4, 1, jnp.where(
                    off == 4, lax.shift_right_logical(lax.bitwise_and(o, NY - 1), 1), 0))
                local = (off == 0).astype(i32)
                rows = slice(j * part.rows, (j + 1) * part.rows)
                full = jnp.zeros((part.rows, CH), i32)
                code = jnp.where(full + above > 0, dr[p][4][rows, :].astype(i32),
                                 ur[p][4][rows, :].astype(i32))
                code = jnp.where(full + local > 0, near[part.data, :], code)
                tile = jnp.where(row_id * 0 + above > 0, dr[p][4][part.scales, :].astype(i32),
                                 ur[p][4][part.scales, :].astype(i32))
                tile = jnp.where(row_id * 0 + local > 0, near[part.tail, :], tile)
                tile = scale_of(tile)
                for kk, n in enumerate(part.chunks):
                    r = j * part.w + kk
                    update[j, :, n * CH:n * CH + CH] = (
                        code[kk * SR:kk * SR + SR].astype(f32) * tile[r:r + 1, :])

    def stat(which, i):
        def block(m, _):
            b = (x + 1 + m) % 4
            if which == 0:
                ohi, olo = ghi[i, rows_of(b, 128), :], glo[i, rows_of(b, 128), :]
                f = dot(jnp.concatenate((ohi, olo), axis=0), ghi[i], ((1,), (1,)))
                f = f[:128] + f[128:] + dot(ohi, glo[i], ((1,), (1,)))
            else:
                chi, clo = ghi[i, :, rows_of(b, 128)], glo[i, :, rows_of(b, 128)]
                f = (dot(chi, ghi[i], ((0,), (0,))) + dot(clo, ghi[i], ((0,), (0,)))
                     + dot(chi, glo[i], ((0,), (0,))))
            for cc in range(2):
                sc = jnp.zeros((16, CH), f32)
                for n in range(4):
                    q, e = encode(f[cc * SR:cc * SR + SR, n * CH:n * CH + CH])
                    sx[which][i, b * 2 + cc, n * SR:n * SR + SR, :] = q
                    sc = jnp.where(row_id == n, e, sc)
                sx[which][i, b * 2 + cc, 256:SLOT, :] = sc.astype(i32).astype(i16)
            return 0

        lax.fori_loop(0, 4, block, 0, unroll=2)
        sr[which][dp + 8 * i] = sx[which][i, dp]
        for t in (4, 3, 5, 2, 6, 1, 7):
            to = (dp + t) % ND
            remote(sx[which].at[i, to], sr[which].at[dp + 8 * i], x_sem.at[2 * NP + which, 0],
                   x_sem.at[2 * NP + which, 1], {"dp": to}).start()

    def renew(which, held, out):
        whole(sx[which].at[:, 1:ND], x_sem.at[2 * NP + which]).wait_recv()

        def slot(k, _):
            w = weight[k]
            scales = scale_of(sr[which][k, 256:SLOT, :])
            for n in range(4):
                cols = slice(n * CH, n * CH + CH)
                term = widen(sr[which][k, n * SR:n * SR + SR, :]) * scales[n:n + 1, :]
                held[k, :, cols] = stat_decay * held[k, :, cols] + w * term
            pltpu.make_async_copy(held.at[k], out.at[k], out_sem.at[which]).start()
            return 0

        lax.fori_loop(0, NS, slot, 0)

    out0, out1 = (Outward(part) for part in PARTS)
    in0, in1 = (Inward(part) for part in PARTS)
    right_far, left_far, right_straight, left_straight, right_both, left_both = {}, {}, {}, {}, {}, {}

    def far(k):
        fill(snd.at[k], 1, lambda j, kk: pair_sum(0, j, k))
        if k % 2 == 0:
            right_far[k] = ship(k, right)
        else:
            left_far[k] = ship(k, left)

    def straight(k):
        if k % 2 == 1:
            fill(snd.at[4 + k], 1, lambda j, kk: pair_sum(1, j, k))
            right_straight[k] = ship(4 + k, right)
        else:
            fill(snd.at[4 + k], 1, lambda j, kk: pair_sum(2, j, k))
            left_straight[k] = ship(4 + k, left)

    def both(k):
        if k % 2 == 0:
            right_far[k].wait_recv()
            fill(snd.at[8 + k], 1, lambda j, kk: pair_sum(1, j, k) + received(k, j))
            right_both[k] = ship(8 + k, right)
        else:
            left_far[k].wait_recv()
            fill(snd.at[8 + k], 1, lambda j, kk: pair_sum(2, j, k) + received(k, j))
            left_both[k] = ship(8 + k, left)

    def total(part):
        for k in part.chunks:
            for cps in (right_straight, left_straight, right_both, left_both):
                if k in cps:
                    cps[k].wait_recv()
        fill(unit[part.p], part.w, lambda j, kk: (
            pair_sum(3, j, part.chunks[kk]) + received(4 + part.chunks[kk], j)
            + received(8 + part.chunks[kk], j)))

    ready(0)
    pair[2].start()
    pair[1].start()
    pair[3].start()
    for cp in root_in + stat_in:
        cp.start()
    far(0)
    far(1)
    ready(2)
    straight(0)
    ready(1)
    straight(1)
    both(0)
    both(1)
    far(2)
    far(3)
    straight(2)
    straight(3)
    ready(3)
    total(PARTS[0])
    out0.start()
    both(2)
    both(3)
    total(PARTS[1])
    for which, (src, dst) in enumerate(((left_root, lf), (right_root, rf))):
        for i in range(2):
            for t in range(1, ND):
                to = (dp + t) % ND
                remote(src.at[(to + 8 * i) % NS], dst.at[i, rows_of(dp)],
                       x_sem.at[2 * NP + 2 + which, 0],
                       x_sem.at[2 * NP + 2 + which, 1], {"dp": to}).start()
    out0.step(1)
    place_slots()
    out0.step(2)
    out0.step(3)
    out1.start()
    out0.last()
    out1.step(1)
    out0.spread()
    out1.step(2)
    out0.open()
    out1.step(3)
    for cp in root_in:
        cp.wait()
    whole(lf.at[:, 0:7 * SR], x_sem.at[2 * NP + 2]).wait_recv()
    whole(rf.at[:, 0:7 * SR], x_sem.at[2 * NP + 3]).wait_recv()
    out0.project()
    out1.last()
    out1.spread()
    out1.open()
    out1.project()
    in0.multiply(0)
    in0.hand_out(0)
    in0.multiply(1)
    in0.hand_out(1)
    in1.multiply(0)
    in1.multiply(1)
    in0.arrive()
    in0.begin()
    in0.one()
    in1.hand_out(0)
    in1.hand_out(1)
    in0.two()
    stat(0, 0)
    in0.three()
    in1.arrive()
    in1.begin()
    stat(1, 0)
    in0.four()
    in1.one()
    stat(0, 1)
    in0.finish()
    in1.two()
    stat(1, 1)
    in1.three()
    for cp in stat_in:
        cp.wait()
    renew(0, ls, left_new)
    in1.four()
    renew(1, rs, right_new)
    in1.finish()

    pltpu.make_async_copy(ls, left_new, out_sem.at[0]).wait()
    pltpu.make_async_copy(rs, right_new, out_sem.at[1]).wait()
    for cp in sent + group:
        cp.wait_send()


def shampoo(plan, grads, left_stat, right_stat, left_root, right_root):
    hbm = pl.BlockSpec(memory_space=pl.ANY)
    vmem = pltpu.VMEM

    def each(lead, rows, times=1):
        return [vmem((*lead, rows(part), CH), i16) for part in PARTS for _ in range(times)]

    def unit(part):
        return part.unit

    def message(part):
        return part.message

    train = [vmem(shape, i16) for part in PARTS for shape in (
        (NY, part.message, CH), (2, part.message, CH), (2, part.message, CH),
        *[(part.unit, CH)] * 4)]

    return pl.pallas_call(
        shampoo_kernel,
        out_shape=(
            jax.ShapeDtypeStruct((NS, SR, BO), f32),
            jax.ShapeDtypeStruct((NS, SR, BO), f32),
            jax.ShapeDtypeStruct((NB, SR, BO), f32),
        ),
        in_specs=[pl.BlockSpec(memory_space=pltpu.SMEM), hbm, hbm, hbm, hbm, hbm],
        out_specs=(hbm, hbm, pl.BlockSpec(memory_space=vmem)),
        scratch_shapes=[
            pltpu.SMEM((NO,), i32),
            pltpu.SMEM((NS + NO,), i32),
            pltpu.SMEM((NS + NO,), i32),
            pltpu.SMEM((NS,), f32),
            vmem((4, NB, SR, BO), bf16),
            vmem((4, NB, SR, BO), bf16),
            vmem((12, UNIT, CH), i16),
            vmem((12, UNIT, CH), i16),
            *each((), unit),
            *[vmem((rows, CH), i16) for part in PARTS for rows in (
                *[part.unit] * 4, part.six, part.six, 2 * part.far, part.six, part.six)],
            *each((NZ, NY - 1), message),
            *each((NO,), message),
            *each((2, ND), message),
            *each((2, ND), message),
            *[vmem((2, BO, BO), bf16)] * 6,
            *each((2, ND), message),
            *each((2 * ND,), message),
            *each((NY,), message, NZ),
            *each((NZ, NY - 1), message),
            *train,
            *train,
            *[vmem((2, ND, SLOT, CH), i16)] * 2,
            *[vmem((2 * ND, SLOT, CH), i16)] * 2,
            vmem((NS, SR, BO), f32),
            vmem((NS, SR, BO), f32),
            *[vmem((NB, part.rows, CH), i16) for part in PARTS],
            pltpu.SemaphoreType.DMA((2, 4)),
            pltpu.SemaphoreType.DMA((10,)),
            pltpu.SemaphoreType.DMA((2, 12)),
            pltpu.SemaphoreType.DMA((NP, 4, 2, 7)),
            pltpu.SemaphoreType.DMA((NP, 2)),
            pltpu.SemaphoreType.DMA((NP, NZ, 2)),
            pltpu.SemaphoreType.DMA((2 * NP + 4, 2)),
            pltpu.SemaphoreType.DMA((2,)),
        ],
        compiler_params=pltpu.CompilerParams(
            collective_id=0, has_side_effects=True, vmem_limit_bytes=LIMIT),
        name="shampoo",
    )(plan, grads, left_stat, right_stat, left_root, right_root)


def local(grads, plan, left_stat, right_stat, left_root, right_root):
    left_new, right_new, update = shampoo(
        plan, grads[0], left_stat[0], right_stat[0], left_root[0], right_root[0])
    return left_new[None], right_new[None], update


def solution(mesh):
    return jax.shard_map(
        local,
        mesh=mesh,
        in_specs=(
            P("dp", "owner", None, None),
            P(),
            P("owner", None, "dp", None),
            P("owner", None, "dp", None),
            P("owner", None, "dp", None),
            P("owner", None, "dp", None),
        ),
        out_specs=(
            P("owner", None, "dp", None),
            P("owner", None, "dp", None),
            P("owner", "dp", None),
        ),
        check_vma=False,
    )
```

```python
import functools

import jax
import jax.numpy as jnp
from jax import lax
from jax.experimental import pallas as pl
from jax.experimental.pallas import tpu as pltpu
from jax.sharding import PartitionSpec as P

MESH = pl.DeviceIdType.MESH
f32 = jnp.float32
bf16 = jnp.bfloat16
i16 = jnp.int16
i32 = jnp.int32

stat_decay = 0.95
fresh_share = 0.05

NB = 7
NO = 32
NS = 13
ND = 8
SR = 64
BO = 512
CH = 128
NY = 4
NZ = 8
SLOT = 272
UNIT = 464
LIMIT = 60 * 1024 * 1024


def encode(x):
    m = jnp.maximum(jnp.max(jnp.abs(x), axis=0, keepdims=True), 2.0 ** -100)
    e = jnp.floor(jnp.log2(m) * 256.0) + 1.0
    q = jnp.round(x * (32700.0 * jnp.exp2(e * (-1.0 / 256.0))))
    return q.astype(i32).astype(i16), e


def scale_of(e16):
    return jnp.exp2(e16.astype(i32).astype(f32) * (1.0 / 256.0)) * (1.0 / 32700.0)


def widen(q):
    return q.astype(i32).astype(f32)


def remote(src, dst, send, recv, where):
    return pltpu.make_async_remote_copy(
        src_ref=src, dst_ref=dst, send_sem=send, recv_sem=recv,
        device_id=where, device_id_type=MESH)


def dot(a, b, dims=((1,), (0,))):
    return lax.dot_general(a, b, (dims, ((), ())), preferred_element_type=f32)


class Part:
    def __init__(self, p, chunks):
        w = len(chunks)
        self.p, self.chunks, self.w = p, chunks, w
        self.cols = slice(chunks[0] * CH, (chunks[-1] + 1) * CH)
        self.rows = SR * w
        self.unit = NB * SR * w + 16
        self.message = SR * w + 16
        self.front = slice(0, 4 * SR * w)
        self.rear = slice(4 * SR * w, self.unit)
        self.back = slice(4 * SR * w, NB * SR * w)
        self.scales = slice(NB * SR * w, self.unit)
        self.data = slice(0, SR * w)
        self.tail = slice(SR * w, self.message)
        self.far = 2 * SR * w + 16
        self.six = 6 * SR * w + 16


PARTS = (Part(0, (0, 1)), Part(1, (2, 3)))
NP = len(PARTS)


def split(v):
    hi = v.astype(bf16)
    return hi, (v - hi.astype(f32)).astype(bf16)


def rows_of(t, n=SR):
    return pl.ds(pl.multiple_of(t * n, n), n)


def shampoo_kernel(plan, grads, left_stat, right_stat, left_root, right_root,
                   left_new, right_new, update, *scratch):
    it = iter(scratch)
    slot_of, source_of, block_at, weight = (next(it) for _ in range(4))
    own, par, snd, rcv = (next(it) for _ in range(4))
    unit = [next(it) for _ in PARTS]
    hops = [[next(it) for _ in range(9)] for _ in PARTS]
    ysend, got, xs, gx = ([next(it) for _ in PARTS] for _ in range(4))
    lf, rf, ghi, glo, phi, plo = (next(it) for _ in range(6))
    xu, ux = ([next(it) for _ in PARTS] for _ in range(2))
    ybuf = [[next(it) for _ in range(8)] for _ in PARTS]
    yback = [next(it) for _ in PARTS]
    ur = [[next(it) for _ in range(7)] for _ in PARTS]
    dr = [[next(it) for _ in range(7)] for _ in PARTS]
    sx, sr = ([next(it) for _ in range(2)] for _ in range(2))
    ls, rs = next(it), next(it)
    shelves = [next(it) for _ in PARTS]
    pair_sem, load_sem, unit_sem, line_sem, y_sem, back_sem, x_sem, out_sem = (
        next(it) for _ in range(8))

    me = lax.axis_index("owner")
    z, y = me // NY, me % NY
    up, down = ((z + 1) % NZ) * NY + y, ((z + NZ - 1) % NZ) * NY + y
    dp = lax.axis_index("dp")
    x, c = dp // 2, dp % 2
    partner = x * 2 + 1 - c
    right = ((x + 1) % 4) * 2 + c
    left = ((x + 3) % 4) * 2 + c
    row_id = lax.broadcasted_iota(i32, (16, CH), 0)
    sent = []
    group = []

    def whole(ref, sems):
        cp = remote(ref, ref, sems.at[0], sems.at[1], {"dp": partner})
        group.append(cp)
        return cp

    mine = {}
    for n, off in ((0, 2), (2, 3), (1, 1), (3, 0)):
        t = ((x + off) % 4) * 2 + c
        mine[n] = pltpu.make_async_copy(grads.at[:, rows_of(t), :], own.at[n], load_sem.at[n])
        mine[n].start()
    stat_in = [pltpu.make_async_copy(left_stat, ls, load_sem.at[4]),
               pltpu.make_async_copy(right_stat, rs, load_sem.at[5])]
    root_in = []
    for i in range(2):
        k = (dp + 8 * i) % NS
        root_in.append(pltpu.make_async_copy(
            left_root.at[k], lf.at[i, rows_of(dp)], load_sem.at[6 + i]))
        root_in.append(pltpu.make_async_copy(
            right_root.at[k], rf.at[i, rows_of(dp)], load_sem.at[8 + i]))

    barrier = pltpu.get_barrier_semaphore()
    for t in range(1, ND):
        pl.semaphore_signal(
            barrier, inc=1, device_id={"dp": (dp + t) % ND}, device_id_type=MESH)
    for place in [up, down] + [z * NY + (y + t) % NY for t in range(1, NY)]:
        pl.semaphore_signal(barrier, inc=1, device_id={"owner": place}, device_id_type=MESH)
    pl.semaphore_wait(barrier, ND - 1 + 2 + NY - 1)

    pair = {}
    for n, off in ((0, 2), (2, 3), (1, 1), (3, 0)):
        t = ((x + off) % 4) * 2 + 1 - c
        pair[n] = remote(grads.at[:, rows_of(t), :], par.at[n],
                         pair_sem.at[0, n], pair_sem.at[1, n], {"dp": partner})
        sent.append(pair[n])
    pair[0].start()

    def stand(i, count):
        hold, which = jnp.int32(0), jnp.int32(0)
        for j in range(NB):
            hit = plan[i * NB + j] == me
            hold = jnp.where(hit, 1, hold)
            which = jnp.where(hit, j, which)
        slot_of[i] = jnp.minimum(count, NS - 1)
        source_of[NS + i] = jnp.where(hold > 0, count, -1)
        block_at[NS + i] = which
        return count + hold

    def place_slots():
        count = lax.fori_loop(0, NO, stand, jnp.int32(0))

        def place(k, _):
            src, blk = jnp.int32(0), jnp.int32(0)
            for i in range(NO):
                hit = source_of[NS + i] == k
                src = jnp.where(hit, i, src)
                blk = jnp.where(hit, block_at[NS + i], blk)
            source_of[k] = src
            block_at[k] = blk
            weight[k] = jnp.where(k < count, fresh_share, 0.0).astype(f32)
            return 0

        lax.fori_loop(0, NS, place, 0)

    def pair_sum(n, j, k):
        cols = slice(k * CH, k * CH + CH)
        return own[n, j, :, cols].astype(f32) + par[n, j, :, cols].astype(f32)

    def scale_row(scales, r):
        return jnp.sum(jnp.where(row_id == r, scales, 0.0), axis=0, keepdims=True)

    def received(u, j):
        scales = scale_of(rcv[u, NB * SR:UNIT, :])
        return widen(rcv[u, j * SR:j * SR + SR, :]) * scales[j:j + 1, :]

    def fill(out, w, value):
        sc = jnp.zeros((16, CH), f32)
        for j in range(NB):
            for kk in range(w):
                r = j * w + kk
                q, e = encode(value(j, kk))
                out[r * SR:r * SR + SR, :] = q
                sc = jnp.where(row_id == r, e, sc)
        out[NB * SR * w:NB * SR * w + 16, :] = sc.astype(i32).astype(i16)

    def ship(u, to):
        cp = remote(snd.at[u], rcv.at[u], unit_sem.at[0, u], unit_sem.at[1, u], {"dp": to})
        cp.start()
        sent.append(cp)
        return cp

    def ready(n):
        mine[n].wait()
        pair[n].wait_recv()

    class Line:
        def __init__(self, p, way, towards):
            self.p, self.way, self.towards = p, way, towards
            self.copies = {}

        def go(self, n, src, dst):
            cp = remote(src, dst, line_sem.at[self.p, self.way, 0, n],
                        line_sem.at[self.p, self.way, 1, n], {"owner": self.towards})
            cp.start()
            sent.append(cp)
            self.copies[n] = cp

        def came(self, *names):
            for n in names:
                self.copies[n].wait_recv()

    class Outward:
        def __init__(self, part):
            self.part, self.p = part, part.p
            (self.u1, self.u2, self.d1, self.d2, self.u3, self.d3, self.far,
             self.su, self.sd) = hops[part.p]
            self.ups, self.downs = Line(part.p, 0, up), Line(part.p, 1, down)

        def shelve(self, ref):
            shelf = shelves[self.p]
            for b in range(NB):
                shelf[b] = ref[b * self.part.rows:(b + 1) * self.part.rows, :]

        def find(self, src, owner):
            j = jnp.int32(0)
            for b in range(NB):
                j = jnp.where(plan[src * NB + b] == owner, b, j)
            return shelves[self.p][j]

        def hand(self, n, src, code, scales):
            part, p = self.part, self.p
            for t in range(1, NY):
                yy = (y + t) % NY
                ysend[p][n, t - 1, part.data, :] = code(yy)
                ysend[p][n, t - 1, part.tail, :] = scales(yy)
                remote(ysend[p].at[n, t - 1], got[p].at[src], y_sem.at[p, 0],
                       y_sem.at[p, 1], {"owner": z * NY + yy}).start()
            got[p][src, part.data, :] = code(y)
            got[p][src, part.tail, :] = scales(y)

        def pass_on(self, n, ref, rel):
            src = ((z + rel) % NZ) * NY + y
            self.shelve(ref)
            scales = ref[self.part.scales, :]
            self.hand(n, src, lambda yy: self.find(src, z * NY + yy), lambda yy: scales)

        def pack(self, out, ref, rel, way, first):
            rows = self.part.rows
            src = ((z + rel) % NZ) * NY + y
            self.shelve(ref)
            one, two = ((z + way) % NZ) * NY, ((z + 2 * way) % NZ) * NY
            for q in range(2):
                out[q * rows:q * rows + rows, :] = self.find(src, two + first + q)
            out[2 * rows:2 * rows + 16, :] = ref[self.part.scales, :]
            for q in range(NY):
                at = self.part.far + q * rows
                out[at:at + rows, :] = self.find(src, one + q)

        def start(self):
            front, rear = self.part.front, self.part.rear
            g = unit[self.p]
            self.ups.go(0, g.at[front], self.u1.at[front])
            self.downs.go(0, g.at[rear], self.d1.at[rear])
            self.ups.go(1, g.at[rear], self.u1.at[rear])
            self.downs.go(1, g.at[front], self.d1.at[front])
            self.pass_on(0, g, 0)

        def step(self, r):
            ups, downs = self.ups, self.downs
            front, rear = self.part.front, self.part.rear
            far, six, rows = self.part.far, self.part.six, self.part.rows
            if r == 1:
                ups.came(0)
                ups.go(2, self.u1.at[front], self.u2.at[front])
                downs.came(0)
                downs.go(2, self.d1.at[rear], self.d2.at[rear])
                ups.came(1)
                ups.go(3, self.u1.at[rear], self.u2.at[rear])
                downs.came(1)
                downs.go(3, self.d1.at[front], self.d2.at[front])
                self.pass_on(1, self.u1, 7)
                self.pass_on(2, self.d1, 1)
            elif r == 2:
                ups.came(2, 3)
                self.pack(self.su, self.u2, 6, 1, 0)
                ups.go(4, self.su.at[0:far], self.u3.at[0:far])
                ups.go(5, self.su.at[far:six], self.u3.at[far:six])
                downs.came(2, 3)
                self.pack(self.sd, self.d2, 2, NZ - 1, 2)
                downs.go(4, self.sd.at[0:far], self.d3.at[0:far])
                downs.go(5, self.sd.at[far:six], self.d3.at[far:six])
                self.pass_on(3, self.u2, 6)
                self.pass_on(4, self.d2, 2)
            else:
                ups.came(4)
                ups.go(6, self.u3.at[0:far], self.far.at[0:far])
                downs.came(4)
                downs.go(6, self.d3.at[0:far], self.far.at[far:2 * far])
                for line, ref, n, rel in ((ups, self.u3, 5, 5), (downs, self.d3, 6, 3)):
                    line.came(5)

                    def code(yy, ref=ref):
                        return ref[pl.ds(pl.multiple_of(far + yy * rows, 16), rows), :]

                    def scales(yy, ref=ref):
                        return ref[2 * rows:far, :]

                    self.hand(n, ((z + rel) % NZ) * NY + y, code, scales)

        def last(self):
            far, rows = self.part.far, self.part.rows
            self.ups.came(6)
            self.downs.came(6)

            def code(yy):
                at = (yy // 2) * far + (yy % 2) * rows
                return self.far[pl.ds(pl.multiple_of(at, 16), rows), :]

            def scales(yy):
                return self.far[pl.ds(pl.multiple_of((yy // 2) * far + 2 * rows, 16), 16), :]

            self.hand(7, ((z + 4) % NZ) * NY + y, code, scales)

        def spread(self):
            p = self.p
            whole(ysend[p], y_sem.at[p]).wait_recv()
            for t in (4, 3, 5, 2, 6, 1, 7, 0):
                for i in range(2):
                    to = (dp + t) % ND
                    k = (to + 8 * i) % NS
                    if t == 0:
                        gx[p][i, dp] = got[p][source_of[k]]
                        continue
                    xs[p][i, t] = got[p][source_of[k]]
                    remote(xs[p].at[i, t], gx[p].at[i, dp], x_sem.at[p, 0],
                           x_sem.at[p, 1], {"dp": to}).start()

        def arrive(self):
            whole(xs[self.p].at[:, 1:ND], x_sem.at[self.p]).wait_recv()

        def open(self, i):
            part, p = self.part, self.p
            blk = block_at[(dp + 8 * i) % NS]
            for t in range(ND):
                scales = scale_of(gx[p][i, t, part.tail, :])
                for kk, n in enumerate(part.chunks):
                    v = (widen(gx[p][i, t, kk * SR:kk * SR + SR, :])
                         * scale_row(scales, blk * part.w + kk))
                    hi, lo = split(v)
                    ghi[i, t * SR:t * SR + SR, n * CH:n * CH + CH] = hi
                    glo[i, t * SR:t * SR + SR, n * CH:n * CH + CH] = lo

        def project(self, i):
            cols = self.part.cols

            def part(m, _):
                rows = rows_of(m, 256)
                p = dot(lf[i, rows, :], ghi[i, :, cols]) + dot(lf[i, rows, :], glo[i, :, cols])
                hi, lo = split(p)
                phi[i, rows, cols] = hi
                plo[i, rows, cols] = lo
                return 0

            lax.fori_loop(0, 2, part, 0, unroll=True)

    class Train:
        def __init__(self, part, way, towards, refs, ascending):
            self.part, self.p, self.ascending = part, part.p, ascending
            self.near, self.far, self.later, self.one, self.zero, self.out2, self.out1 = refs
            self.line = Line(part.p, way, towards)

        def place(self, r):
            return r if self.ascending else NZ - r

        def four(self):
            some = slice(0, 2) if self.ascending else slice(2, 4)
            self.line.go(0, ybuf[self.p][4].at[some], self.far)

        def three(self):
            self.line.go(1, ybuf[self.p][self.place(3)], self.near)

        def three_far(self):
            self.line.came(0)
            self.line.go(2, self.far, self.later)

        def code(self, r, j, part_rows, old):
            src = ((z + self.place(r)) % NZ) * NY + y
            o = plan[src * NB + j]
            oz, oy = lax.shift_right_logical(o, 2), lax.bitwise_and(o, NY - 1)
            new = ybuf[self.p][self.place(r)][oy][part_rows, :].astype(i32)
            if r == 2:
                before = (z + (NZ - 1 if self.ascending else 1)) % NZ
                near = self.near[oy][part_rows, :].astype(i32)
                far = self.later[lax.bitwise_and(o, 1)][part_rows, :].astype(i32)
                at = jnp.full(near.shape, (oz == before).astype(i32), i32)
                old = jnp.where(at > 0, near, far)
            at = jnp.full(new.shape, (oz == z).astype(i32), i32)
            return jnp.where(at > 0, new, old)

        def blocks(self, r, first, last, out, came):
            part = self.part
            for j in range(first, last):
                rows = slice(j * part.rows, (j + 1) * part.rows)
                old = None if r == 2 else came[rows, :].astype(i32)
                out[rows, :] = self.code(r, j, part.data, old).astype(i16)

        def scales(self, r, out, came):
            part = self.part
            tile = jnp.zeros((16, CH), i32) if r == 2 else came[part.scales, :].astype(i32)
            for j in range(NB):
                new = self.code(r, j, part.tail, tile)
                tile = jnp.where(row_id // part.w == j, new, tile)
            out[part.scales, :] = tile.astype(i16)

        def two(self):
            part = self.part
            self.line.came(1, 2)
            self.blocks(2, 0, 4, self.out2, None)
            self.line.go(3, self.out2.at[part.front], self.one.at[part.front])
            self.blocks(2, 4, NB, self.out2, None)
            self.scales(2, self.out2, None)
            self.line.go(4, self.out2.at[part.rear], self.one.at[part.rear])

        def last(self):
            part = self.part
            self.line.came(3)
            self.blocks(1, 0, 4, self.out1, self.one)
            self.line.go(5, self.out1.at[part.front], self.zero.at[part.front])
            self.line.came(4)
            self.blocks(1, 4, NB, self.out1, self.one)
            self.scales(1, self.out1, self.one)
            self.line.go(6, self.out1.at[part.rear], self.zero.at[part.rear])

        def arrived(self):
            self.line.came(5, 6)

    class Inward:
        def __init__(self, part):
            self.part, self.p = part, part.p
            self.ups = Train(part, 2, up, ur[part.p], True)
            self.downs = Train(part, 3, down, dr[part.p], False)

        def multiply(self, i):
            part, p = self.part, self.p

            def pairs(m, _):
                b = (x + 2 + m) % 4
                rows = rows_of(b, 128)
                r = dot(jnp.concatenate((phi[i, rows, :], plo[i, rows, :]), axis=0),
                        rf[i, :, part.cols])
                u = r[:128] + r[128:]
                for cc in range(2):
                    sc = jnp.zeros((16, CH), f32)
                    for kk in range(part.w):
                        q, e = encode(u[cc * SR:cc * SR + SR, kk * CH:kk * CH + CH])
                        xu[p][i, b * 2 + cc, kk * SR:kk * SR + SR, :] = q
                        sc = jnp.where(row_id % part.w == kk, e, sc)
                    xu[p][i, b * 2 + cc, part.tail, :] = sc.astype(i32).astype(i16)
                return 0

            lax.fori_loop(0, 4, pairs, 0, unroll=True)

        def hand_out(self, i):
            p = self.p
            ux[p][dp + 8 * i] = xu[p][i, dp]
            for t in (4, 3, 5, 2, 6, 1, 7):
                to = (dp + t) % ND
                remote(xu[p].at[i, to], ux[p].at[dp + 8 * i], x_sem.at[NP + p, 0],
                       x_sem.at[NP + p, 1], {"dp": to}).start()

        def arrive(self):
            whole(xu[self.p].at[:, 1:ND], x_sem.at[NP + self.p]).wait_recv()

        def across(self, n):
            p = self.p
            d = (z + n) % NZ
            for t in range(1, NY):
                yy = (y + t) % NY
                yback[p][n, t - 1] = ux[p][slot_of[d * NY + yy]]
                remote(yback[p].at[n, t - 1], ybuf[p][n].at[y], back_sem.at[p, n, 0],
                       back_sem.at[p, n, 1], {"owner": z * NY + yy}).start()
            ybuf[p][n][y] = ux[p][slot_of[d * NY + y]]

        def crossed(self, n):
            whole(yback[self.p].at[n], back_sem.at[self.p, n]).wait_recv()

        def begin(self):
            self.across(4)
            self.across(3)
            self.across(5)

        def one(self):
            self.crossed(4)
            self.ups.four()
            self.downs.four()
            self.crossed(3)
            self.ups.three()
            self.crossed(5)
            self.downs.three()
            self.across(2)
            self.across(6)

        def two(self):
            self.ups.three_far()
            self.downs.three_far()
            self.across(1)
            self.across(7)

        def three(self):
            self.crossed(2)
            self.ups.two()
            self.crossed(6)
            self.downs.two()
            self.across(0)

        def four(self):
            self.crossed(1)
            self.ups.last()
            self.crossed(7)
            self.downs.last()

        def finish(self):
            part, p = self.part, self.p
            self.crossed(0)
            self.ups.arrived()
            self.downs.arrived()
            for j in range(NB):
                o = plan[me * NB + j]
                near = ybuf[p][0][lax.bitwise_and(o, NY - 1)].astype(i32)
                off = lax.bitwise_and(lax.shift_right_logical(o, 2) + NZ - z, NZ - 1)
                above = jnp.where(off < 4, 1, jnp.where(
                    off == 4, lax.shift_right_logical(lax.bitwise_and(o, NY - 1), 1), 0))
                local = (off == 0).astype(i32)
                rows = slice(j * part.rows, (j + 1) * part.rows)
                full = jnp.zeros((part.rows, CH), i32)
                code = jnp.where(full + above > 0, dr[p][4][rows, :].astype(i32),
                                 ur[p][4][rows, :].astype(i32))
                code = jnp.where(full + local > 0, near[part.data, :], code)
                tile = jnp.where(row_id * 0 + above > 0, dr[p][4][part.scales, :].astype(i32),
                                 ur[p][4][part.scales, :].astype(i32))
                tile = jnp.where(row_id * 0 + local > 0, near[part.tail, :], tile)
                tile = scale_of(tile)
                for kk, n in enumerate(part.chunks):
                    r = j * part.w + kk
                    update[j, :, n * CH:n * CH + CH] = (
                        code[kk * SR:kk * SR + SR].astype(f32) * tile[r:r + 1, :])

    def stat(which, i):
        def block(m, _):
            b = (x + 1 + m) % 4
            if which == 0:
                ohi, olo = ghi[i, rows_of(b, 128), :], glo[i, rows_of(b, 128), :]
                f = dot(jnp.concatenate((ohi, olo), axis=0), ghi[i], ((1,), (1,)))
                f = f[:128] + f[128:] + dot(ohi, glo[i], ((1,), (1,)))
            else:
                chi, clo = ghi[i, :, rows_of(b, 128)], glo[i, :, rows_of(b, 128)]
                f = (dot(chi, ghi[i], ((0,), (0,))) + dot(clo, ghi[i], ((0,), (0,)))
                     + dot(chi, glo[i], ((0,), (0,))))
            for cc in range(2):
                sc = jnp.zeros((16, CH), f32)
                for n in range(4):
                    q, e = encode(f[cc * SR:cc * SR + SR, n * CH:n * CH + CH])
                    sx[which][i, b * 2 + cc, n * SR:n * SR + SR, :] = q
                    sc = jnp.where(row_id == n, e, sc)
                sx[which][i, b * 2 + cc, 256:SLOT, :] = sc.astype(i32).astype(i16)
            return 0

        lax.fori_loop(0, 4, block, 0, unroll=2)

    def give(which, i):
        sr[which][dp + 8 * i] = sx[which][i, dp]
        for t in (4, 3, 5, 2, 6, 1, 7):
            to = (dp + t) % ND
            remote(sx[which].at[i, to], sr[which].at[dp + 8 * i], x_sem.at[2 * NP + which, 0],
                   x_sem.at[2 * NP + which, 1], {"dp": to}).start()

    def renew(which, held, out):
        whole(sx[which].at[:, 1:ND], x_sem.at[2 * NP + which]).wait_recv()

        def slot(k, _):
            w = weight[k]
            scales = scale_of(sr[which][k, 256:SLOT, :])
            for n in range(4):
                cols = slice(n * CH, n * CH + CH)
                term = widen(sr[which][k, n * SR:n * SR + SR, :]) * scales[n:n + 1, :]
                held[k, :, cols] = stat_decay * held[k, :, cols] + w * term
            pltpu.make_async_copy(held.at[k], out.at[k], out_sem.at[which]).start()
            return 0

        lax.fori_loop(0, NS, slot, 0)

    out0, out1 = (Outward(part) for part in PARTS)
    in0, in1 = (Inward(part) for part in PARTS)
    right_far, left_far, right_straight, left_straight, right_both, left_both = {}, {}, {}, {}, {}, {}

    def far(k):
        fill(snd.at[k], 1, lambda j, kk: pair_sum(0, j, k))
        if k % 2 == 0:
            right_far[k] = ship(k, right)
        else:
            left_far[k] = ship(k, left)

    def straight(k):
        if k % 2 == 1:
            fill(snd.at[4 + k], 1, lambda j, kk: pair_sum(1, j, k))
            right_straight[k] = ship(4 + k, right)
        else:
            fill(snd.at[4 + k], 1, lambda j, kk: pair_sum(2, j, k))
            left_straight[k] = ship(4 + k, left)

    def both(k):
        if k % 2 == 0:
            right_far[k].wait_recv()
            fill(snd.at[8 + k], 1, lambda j, kk: pair_sum(1, j, k) + received(k, j))
            right_both[k] = ship(8 + k, right)
        else:
            left_far[k].wait_recv()
            fill(snd.at[8 + k], 1, lambda j, kk: pair_sum(2, j, k) + received(k, j))
            left_both[k] = ship(8 + k, left)

    def total(part):
        for k in part.chunks:
            for cps in (right_straight, left_straight, right_both, left_both):
                if k in cps:
                    cps[k].wait_recv()
        fill(unit[part.p], part.w, lambda j, kk: (
            pair_sum(3, j, part.chunks[kk]) + received(4 + part.chunks[kk], j)
            + received(8 + part.chunks[kk], j)))

    ready(0)
    pair[2].start()
    pair[1].start()
    pair[3].start()
    for cp in root_in + stat_in:
        cp.start()
    far(0)
    far(1)
    ready(2)
    straight(0)
    ready(1)
    straight(1)
    both(0)
    both(1)
    far(2)
    far(3)
    straight(2)
    straight(3)
    ready(3)
    total(PARTS[0])
    out0.start()
    both(2)
    both(3)
    out0.step(1)
    total(PARTS[1])
    for which, (src, dst) in enumerate(((left_root, lf), (right_root, rf))):
        for i in range(2):
            for t in range(1, ND):
                to = (dp + t) % ND
                remote(src.at[(to + 8 * i) % NS], dst.at[i, rows_of(dp)],
                       x_sem.at[2 * NP + 2 + which, 0],
                       x_sem.at[2 * NP + 2 + which, 1], {"dp": to}).start()
    place_slots()
    out0.step(2)
    out0.step(3)
    out1.start()
    out0.last()
    out1.step(1)
    out0.spread()
    out1.step(2)
    out0.arrive()
    out0.open(0)
    out0.open(1)
    out1.step(3)
    out1.last()
    out1.spread()
    for cp in root_in:
        cp.wait()
    whole(lf.at[:, 0:7 * SR], x_sem.at[2 * NP + 2]).wait_recv()
    whole(rf.at[:, 0:7 * SR], x_sem.at[2 * NP + 3]).wait_recv()
    out0.project(0)
    out0.project(1)
    out1.arrive()
    out1.open(0)
    out1.project(0)
    in0.multiply(0)
    in0.hand_out(0)
    out1.open(1)
    out1.project(1)
    in0.multiply(1)
    in0.hand_out(1)
    in1.multiply(0)
    in1.multiply(1)
    stat(0, 0)
    in0.arrive()
    in0.begin()
    in0.one()
    in1.hand_out(0)
    in1.hand_out(1)
    give(0, 0)
    in0.two()
    stat(1, 0)
    give(1, 0)
    in0.three()
    in1.arrive()
    in1.begin()
    in0.four()
    in1.one()
    stat(0, 1)
    give(0, 1)
    in0.finish()
    stat(1, 1)
    give(1, 1)
    in1.two()
    in1.three()
    for cp in stat_in:
        cp.wait()
    renew(0, ls, left_new)
    in1.four()
    renew(1, rs, right_new)
    in1.finish()

    pltpu.make_async_copy(ls, left_new, out_sem.at[0]).wait()
    pltpu.make_async_copy(rs, right_new, out_sem.at[1]).wait()
    for cp in sent + group:
        cp.wait_send()


def shampoo(plan, grads, left_stat, right_stat, left_root, right_root):
    hbm = pl.BlockSpec(memory_space=pl.ANY)
    vmem = pltpu.VMEM

    def each(lead, rows, times=1):
        return [vmem((*lead, rows(part), CH), i16) for part in PARTS for _ in range(times)]

    def unit(part):
        return part.unit

    def message(part):
        return part.message

    train = [vmem(shape, i16) for part in PARTS for shape in (
        (NY, part.message, CH), (2, part.message, CH), (2, part.message, CH),
        *[(part.unit, CH)] * 4)]

    return pl.pallas_call(
        shampoo_kernel,
        out_shape=(
            jax.ShapeDtypeStruct((NS, SR, BO), f32),
            jax.ShapeDtypeStruct((NS, SR, BO), f32),
            jax.ShapeDtypeStruct((NB, SR, BO), f32),
        ),
        in_specs=[pl.BlockSpec(memory_space=pltpu.SMEM), hbm, hbm, hbm, hbm, hbm],
        out_specs=(hbm, hbm, pl.BlockSpec(memory_space=vmem)),
        scratch_shapes=[
            pltpu.SMEM((NO,), i32),
            pltpu.SMEM((NS + NO,), i32),
            pltpu.SMEM((NS + NO,), i32),
            pltpu.SMEM((NS,), f32),
            vmem((4, NB, SR, BO), bf16),
            vmem((4, NB, SR, BO), bf16),
            vmem((12, UNIT, CH), i16),
            vmem((12, UNIT, CH), i16),
            *each((), unit),
            *[vmem((rows, CH), i16) for part in PARTS for rows in (
                *[part.unit] * 4, part.six, part.six, 2 * part.far, part.six, part.six)],
            *each((NZ, NY - 1), message),
            *each((NO,), message),
            *each((2, ND), message),
            *each((2, ND), message),
            *[vmem((2, BO, BO), bf16)] * 6,
            *each((2, ND), message),
            *each((2 * ND,), message),
            *each((NY,), message, NZ),
            *each((NZ, NY - 1), message),
            *train,
            *train,
            *[vmem((2, ND, SLOT, CH), i16)] * 2,
            *[vmem((2 * ND, SLOT, CH), i16)] * 2,
            vmem((NS, SR, BO), f32),
            vmem((NS, SR, BO), f32),
            *[vmem((NB, part.rows, CH), i16) for part in PARTS],
            pltpu.SemaphoreType.DMA((2, 4)),
            pltpu.SemaphoreType.DMA((10,)),
            pltpu.SemaphoreType.DMA((2, 12)),
            pltpu.SemaphoreType.DMA((NP, 4, 2, 7)),
            pltpu.SemaphoreType.DMA((NP, 2)),
            pltpu.SemaphoreType.DMA((NP, NZ, 2)),
            pltpu.SemaphoreType.DMA((2 * NP + 4, 2)),
            pltpu.SemaphoreType.DMA((2,)),
        ],
        compiler_params=pltpu.CompilerParams(
            collective_id=0, has_side_effects=True, vmem_limit_bytes=LIMIT),
        name="shampoo",
    )(plan, grads, left_stat, right_stat, left_root, right_root)


def local(grads, plan, left_stat, right_stat, left_root, right_root):
    left_new, right_new, update = shampoo(
        plan, grads[0], left_stat[0], right_stat[0], left_root[0], right_root[0])
    return left_new[None], right_new[None], update


def solution(mesh):
    return jax.shard_map(
        local,
        mesh=mesh,
        in_specs=(
            P("dp", "owner", None, None),
            P(),
            P("owner", None, "dp", None),
            P("owner", None, "dp", None),
            P("owner", None, "dp", None),
            P("owner", None, "dp", None),
        ),
        out_specs=(
            P("owner", None, "dp", None),
            P("owner", None, "dp", None),
            P("owner", "dp", None),
        ),
        check_vma=False,
    )
```
